128 devices in a mesh: row: 16 (over z, x), col: 8 (over y, core).
Axes of the slice: x: 4, y: 4, z: 4, core: 2. Of those that a mesh axis runs over, the one named last changes fastest.
Arguments:
- object_init: float32 [2, 8192, 4096], P(None, 'row', 'col'), may hold values from -6 to 6
- probe_init: float32 [2, 256, 256], replicated, may hold values from -6 to 6
- amplitudes: bfloat16 [16, 8, 8, 256, 256], P('row', 'col'), may hold values from 0 to 3
- scan_offsets: int32 [16, 8, 8, 2], P('row', 'col'), may hold values from 0 to 7936, as said below
- live_count: int32 [16, 8], P('row', 'col'), may hold values from 1 to 8, as said below
- smooth_class: int32 [8192, 4096], P('row', 'col'), may hold values from 0 to 3
- class_weight: float32 [4], replicated, may hold values from 0.03 to 0.24
Outputs:
- object_final: float32 [2, 8192, 4096], P(None, 'row', 'col')
- probe_final: float32 [2, 256, 256], replicated
The draws below stay inside these ranges and needn't reach their ends.
Inputs may be any that keep to these rules, and one draw needn't show every extreme that they name: `scan_offsets`: multiples of 128. Each slot's pattern starts inside the tile of the device that holds the slot and lies wholly inside the window; unused slots hold offsets of the same kind. `live_count`: some devices use all 8 slots in every draw, one uses a single slot; the others between.
All inputs are finite; a program needn't handle non-finite values.
Results may differ from the reference program's by a relative error of at most 0.0025.
The reference program's roundings to bfloat16 on the way count: a program that leaves them out, or rounds other values in their place, can miss the bound.
Values sent between devices are 32-bit elements; how exact they have to be, the bound alone decides.
A program may use at most 192 MiB of HBM per device.

```python
import math
import jax
import jax.numpy as jnp
from jax import lax

P_SIZE = 256
TILE = 512
POS_CAP = 8
ITERS = 2
NCLASS = 4
NR = 8192
NC = 4096
N_ROW = 16
N_COL = 8


def draw_scan_offsets(key, part):
    key = jax.random.fold_in(key, 11)
    key_rows, key_cols = jax.random.split(key)
    step_len = P_SIZE // 2
    per_tile = TILE // step_len
    edge_count = (TILE - P_SIZE) // step_len + 1
    row_id = jnp.arange(N_ROW, dtype=jnp.int32)[:, None, None]
    col_id = jnp.arange(N_COL, dtype=jnp.int32)[None, :, None]
    rows_limit = jnp.where(row_id == N_ROW - 1, edge_count, per_tile)
    cols_limit = jnp.where(col_id == N_COL - 1, edge_count, per_tile)
    raw_rows = jax.random.randint(key_rows, (N_ROW, N_COL, POS_CAP), 0, 1048576)
    raw_cols = jax.random.randint(key_cols, (N_ROW, N_COL, POS_CAP), 0, 1048576)
    offset_rows = row_id * TILE + step_len * (raw_rows % rows_limit)
    offset_cols = col_id * TILE + step_len * (raw_cols % cols_limit)
    stacked = jnp.stack([offset_rows, offset_cols], -1).astype(jnp.int32)
    stacked = stacked.at[0, 0, 0].set(jnp.array([0, 0], jnp.int32))
    far_corner = jnp.array([N_ROW * TILE - P_SIZE, N_COL * TILE - P_SIZE], jnp.int32)
    stacked = stacked.at[N_ROW - 1, N_COL - 1, 0].set(far_corner)
    return stacked


def draw_live_count(key, part):
    key = jax.random.fold_in(key, 23)
    key_base, key_busy = jax.random.split(key)
    base_count = jax.random.randint(key_base, (N_ROW, N_COL), POS_CAP // 4, POS_CAP // 2 + 1)
    ranking = jax.random.permutation(key_busy, N_ROW * N_COL).reshape(N_ROW, N_COL)
    busy = ranking < max(1, N_ROW * N_COL // 8)
    counts = jnp.where(busy, POS_CAP, base_count)
    counts = jnp.where(ranking == N_ROW * N_COL - 1, 1, counts)
    return counts.astype(jnp.int32)


def touch_ends(values, rng, least, high):
    index_at = [jax.random.randint(jax.random.fold_in(rng, axis), (), 0, length) for axis, length in enumerate(values.shape)]
    longest = values.shape.index(max(values.shape))
    next_to = index_at[:longest] + [(index_at[longest] + 1) % values.shape[longest]] + index_at[longest + 1:]
    return values.at[tuple(index_at)].set(least).at[tuple(next_to)].set(high)


def shard_levels(stream_key, extent, cuts, least, largest):
    factor_of, own = 1.0, jax.random.fold_in(stream_key, 6)
    for position, blocks in cuts:
        steps = jnp.exp(jax.random.uniform(jax.random.fold_in(own, position), (blocks,), jnp.float32, least / len(cuts), largest / len(cuts)))
        factor_of = factor_of * jnp.repeat(steps, extent[position] // blocks).reshape([-1 if axis == position else 1 for axis in range(len(extent))])
    return factor_of


def normal_values(own_key, shape, spread, limit, cuts=(), kind=jnp.bfloat16):
    loudness = shard_levels(own_key, shape, cuts, -0.22, 0.18) if cuts else 1.0
    values = jax.random.normal(own_key, shape, jnp.float32) * spread * loudness
    return jnp.minimum(jnp.maximum(values, -limit), limit).astype(kind)


def setup_inputs(seed: int = 0) -> dict:
    keys = jax.random.split(jax.random.key(seed), 8)
    object_init = normal_values(keys[0], (2, NR, NC), 1.0, 6.0, ((1, 16), (2, 8)), jnp.float32)
    probe_init = normal_values(keys[1], (2, P_SIZE, P_SIZE), 1.0, 6.0, (), jnp.float32)
    amplitudes = jnp.clip(3.0 * jax.random.uniform(keys[2], (N_ROW, N_COL, POS_CAP, P_SIZE, P_SIZE), jnp.float32) ** shard_levels(keys[2], (N_ROW, N_COL, POS_CAP, P_SIZE, P_SIZE), ((0, 16), (1, 8)), -0.2, 0.2), 0.0, 3.0).astype(jnp.bfloat16)
    scan_offsets = draw_scan_offsets(jax.random.fold_in(keys[7], 71), 0)
    live_count = draw_live_count(jax.random.fold_in(keys[7], 71), 0)
    smooth_class = touch_ends(jax.random.randint(keys[5], (NR, NC), 0, NCLASS), jax.random.fold_in(keys[5], 1), 0, NCLASS - 1).astype(jnp.int32)
    class_weight = jnp.clip(jnp.exp(jax.random.uniform(keys[6], (NCLASS,), jnp.float32, math.log(0.03), math.log(0.24))), 0.03, 0.24)
    return {"object_init": object_init, "probe_init": probe_init, "amplitudes": amplitudes, "scan_offsets": scan_offsets, "live_count": live_count, "smooth_class": smooth_class, "class_weight": class_weight}


def dft_tables(length):
    index = jnp.arange(length, dtype=jnp.int32)
    index_product = index[:, None] * index[None, :] % length
    phases = 2.0 * math.pi / length * index_product.astype(jnp.float32)
    dft_scale = 1.0 / math.sqrt(length)
    return ((jnp.cos(phases) * dft_scale).astype(jnp.bfloat16), (-jnp.sin(phases) * dft_scale).astype(jnp.bfloat16))

def right_times(left_re, left_im, table_re, table_im, conj_sign):
    batch_rows = left_re.shape[0]
    length = table_re.shape[0]
    stacked = jnp.concatenate([left_re, left_im], 0).astype(jnp.float32)
    dft_table = jnp.concatenate([table_re, table_im], 1).astype(jnp.float32)
    result = jnp.einsum('spq,qn->spn', stacked, dft_table, precision=lax.Precision.HIGHEST)
    real_real = result[:batch_rows, :, :length]
    real_imag = result[:batch_rows, :, length:]
    imag_real = result[batch_rows:, :, :length]
    imag_imag = result[batch_rows:, :, length:]
    return (real_real - conj_sign * imag_imag, conj_sign * real_imag + imag_real)

def left_times(table_re, table_im, right_re, right_im, conj_sign):
    batch_rows = right_re.shape[0]
    length = table_re.shape[0]
    dft_table = jnp.concatenate([table_re, table_im], 0).astype(jnp.float32)
    stacked = jnp.concatenate([right_re, right_im], 0).astype(jnp.float32)
    result = jnp.einsum('mp,spn->smn', dft_table, stacked, precision=lax.Precision.HIGHEST)
    cos_real = result[:batch_rows, :length]
    sin_real = result[:batch_rows, length:]
    cos_imag = result[batch_rows:, :length]
    sin_imag = result[batch_rows:, length:]
    return (cos_real - conj_sign * sin_imag, cos_imag + conj_sign * sin_real)

def project_patches(patches, probe_now, measured, live_mask, table_re, table_im):
    probe_re = probe_now[0]
    probe_im = probe_now[1]
    patch_re = patches[:, 0]
    patch_im = patches[:, 1]
    exit_re = (probe_re * patch_re - probe_im * patch_im).astype(jnp.bfloat16)
    exit_im = (probe_re * patch_im + probe_im * patch_re).astype(jnp.bfloat16)
    half_re, half_im = right_times(exit_re, exit_im, table_re, table_im, 1.0)
    far_re, far_im = left_times(table_re, table_im, half_re.astype(jnp.bfloat16), half_im.astype(jnp.bfloat16), 1.0)
    modulus = jnp.sqrt(far_re * far_re + far_im * far_im)
    factor = measured.astype(jnp.float32) / jnp.maximum(modulus, 1.0) - 1.0
    corr_re = (far_re * factor).astype(jnp.bfloat16)
    corr_im = (far_im * factor).astype(jnp.bfloat16)
    back_re, back_im = right_times(corr_re, corr_im, table_re, table_im, -1.0)
    diff_re, diff_im = left_times(table_re, table_im, back_re.astype(jnp.bfloat16), back_im.astype(jnp.bfloat16), -1.0)
    slot_mask = live_mask[:, None, None]
    diff_re = diff_re * slot_mask
    diff_im = diff_im * slot_mask
    slot_terms = jnp.stack([probe_re * diff_re + probe_im * diff_im, probe_re * diff_im - probe_im * diff_re, (probe_re * probe_re + probe_im * probe_im) * slot_mask], 1)
    probe_grad = jnp.stack([lax.optimization_barrier(jnp.sum(patch_re * diff_re + patch_im * diff_im, 0)), lax.optimization_barrier(jnp.sum(patch_re * diff_im - patch_im * diff_re, 0))], 0)
    probe_weight = lax.optimization_barrier(jnp.sum((patch_re * patch_re + patch_im * patch_im) * slot_mask, 0))
    return (slot_terms, probe_grad, probe_weight)

def reference(object_init, probe_init, amplitudes, scan_offsets, live_count, smooth_class, class_weight):
    table_re, table_im = dft_tables(P_SIZE)
    offsets = scan_offsets.reshape(-1, 2)
    measured = amplitudes.reshape(-1, P_SIZE, P_SIZE)
    slot_index = jnp.arange(POS_CAP, dtype=jnp.int32)
    live_mask = (slot_index[None, None, :] < live_count[:, :, None]).astype(jnp.float32).reshape(-1)
    smooth_rate = class_weight[smooth_class]
    object_now = object_init
    probe_now = probe_init
    for sweep in range(ITERS):

        def visit_slot(carry, item):
            deposits, grad_sum, weight_sum = carry
            offset, measured_one, live_one = item
            corner_start = (jnp.int32(0), offset[0], offset[1])
            patch = lax.dynamic_slice(object_now, corner_start, (2, P_SIZE, P_SIZE))
            slot_terms, probe_grad, probe_weight = project_patches(patch[None], probe_now, measured_one[None], live_one[None], table_re, table_im)
            region = lax.dynamic_slice(deposits, corner_start, (3, P_SIZE, P_SIZE))
            deposits = lax.dynamic_update_slice(deposits, region + slot_terms[0], corner_start)
            return ((deposits, grad_sum + probe_grad, weight_sum + probe_weight), None)
        start_carry = (jnp.zeros((3, NR, NC), jnp.float32), jnp.zeros((2, P_SIZE, P_SIZE), jnp.float32), jnp.zeros((P_SIZE, P_SIZE), jnp.float32))
        (deposits, grad_sum, weight_sum), unused = lax.scan(visit_slot, start_carry, (offsets, measured, live_mask))
        updated = object_now + deposits[:2] / (deposits[2] + 1.0)
        padded = jnp.pad(updated, ((0, 0), (1, 1), (1, 1)))
        center = padded[:, 1:-1, 1:-1]
        neighbours = padded[:, 2:, 1:-1] + padded[:, :-2, 1:-1] + padded[:, 1:-1, 2:] + padded[:, 1:-1, :-2]
        object_now = updated + smooth_rate * (neighbours - 4.0 * center)
        probe_now = probe_now + grad_sum / (weight_sum + 1.0)
    return (object_now, probe_now)
```

```python
import functools
import math

import jax
import jax.numpy as jnp
import ml_dtypes
import numpy as np
from jax import lax
from jax.experimental import pallas as pl
from jax.experimental.pallas import tpu as pltpu
from jax.sharding import PartitionSpec as P

F32 = jnp.float32
BF16 = jnp.bfloat16
T = 512
S = 256
H = 128
X = T + H
RING = 8
STRIP = H + RING
MESH = pl.DeviceIdType.MESH
ANY = pl.BlockSpec(memory_space=pl.ANY)
VMEM = pl.BlockSpec(memory_space=pltpu.VMEM)
SMEM = pl.BlockSpec(memory_space=pltpu.SMEM)
VMEM_BYTES = 50 * 1024 * 1024


def dft_blocks():
    index = np.arange(S)
    phases = 2.0 * math.pi / S * (index[:, None] * index[None, :] % S)
    re = (np.cos(phases) / math.sqrt(S)).astype(ml_dtypes.bfloat16)
    im = (-np.sin(phases) / math.sqrt(S)).astype(ml_dtypes.bfloat16)
    right = np.block([[re, im], [-im, re]])
    left = np.block([[re, -im], [im, re]])
    return right, left


class Copies:
    def __init__(self, send_sems, recv_sems):
        self.send_sems, self.recv_sems, self.count = send_sems, recv_sems, 0
        self.started = []

    def make(self, src, dst, device):
        k = self.count
        self.count += 1
        return pltpu.make_async_remote_copy(
            src_ref=src,
            dst_ref=dst,
            send_sem=self.send_sems.at[k],
            recv_sem=self.recv_sems.at[k],
            device_id=device,
            device_id_type=MESH,
        )

    def start(self, src, dst, device):
        copy = self.make(src, dst, device)
        copy.start()
        self.started.append(copy)
        return copy

    def finish(self):
        for copy in self.started:
            copy.wait_send()


def around():
    row, col = lax.axis_index("row"), lax.axis_index("col")
    up = (lax.rem(row + 15, 16), col)
    down = (lax.rem(row + 1, 16), col)
    left = (row, lax.rem(col + 7, 8))
    right = (row, lax.rem(col + 1, 8))
    return up, down, left, right


def greet(devices):
    barrier = pltpu.get_barrier_semaphore()
    for device in devices:
        pl.semaphore_signal(barrier, inc=1, device_id=device, device_id_type=MESH)
    pl.semaphore_wait(barrier, len(devices))


def strips_kernel(obj, from_below, from_right, send_sems, recv_sems):
    up, down, left, right = around()
    greet([up, down, left, right])
    copies = Copies(send_sems, recv_sems)
    side = copies.start(obj.at[:, :, pl.ds(0, H)], from_right, left)
    rows = copies.start(
        obj.at[:, pl.ds(0, STRIP), :], from_below.at[:, :, pl.ds(0, T)], up
    )
    side.wait_recv()
    corner = copies.start(
        from_right.at[:, pl.ds(0, STRIP), :], from_below.at[:, :, pl.ds(T, H)], up
    )
    rows.wait_recv()
    corner.wait_recv()
    copies.finish()


def exchange_strips(obj):
    return pl.pallas_call(
        strips_kernel,
        name="object_strips",
        out_shape=[
            jax.ShapeDtypeStruct((2, STRIP, X), F32),
            jax.ShapeDtypeStruct((2, T, H), F32),
        ],
        in_specs=[ANY],
        out_specs=[ANY, ANY],
        scratch_shapes=[pltpu.SemaphoreType.DMA((3,)), pltpu.SemaphoreType.DMA((3,))],
        compiler_params=pltpu.CompilerParams(
            collective_id=0, has_side_effects=True, vmem_limit_bytes=VMEM_BYTES
        ),
    )(obj)


def project(patch_re, patch_im, probe_re, probe_im, measured, right, left):
    exit_re = (probe_re * patch_re - probe_im * patch_im).astype(BF16)
    exit_im = (probe_re * patch_im + probe_im * patch_re).astype(BF16)
    half = jnp.dot(
        jnp.concatenate([exit_re, exit_im], 1), right, preferred_element_type=F32
    ).astype(BF16)
    far = jnp.dot(
        left, jnp.concatenate([half[:, :S], half[:, S:]], 0), preferred_element_type=F32
    )
    far_re, far_im = far[:S], far[S:]
    square = far_re * far_re + far_im * far_im
    factor = measured.astype(F32) * lax.rsqrt(jnp.maximum(square, 1.0)) - 1.0
    corr = jnp.concatenate([(far_re * factor).astype(BF16), (far_im * factor).astype(BF16)], 1)
    back = jnp.dot(corr, left, preferred_element_type=F32).astype(BF16)
    diff = jnp.dot(
        right, jnp.concatenate([back[:, :S], back[:, S:]], 0), preferred_element_type=F32
    )
    return diff[:S], diff[S:]


def visit_slots(obj, probe, amps, offsets, live, right, left, deposits, sums):
    row0 = lax.axis_index("row") * T
    col0 = lax.axis_index("col") * T
    deposits[...] = jnp.zeros_like(deposits)
    sums[...] = jnp.zeros_like(sums)
    total = live[0, 0]

    def place(slot):
        y = pl.multiple_of(offsets[slot, 0] - row0, H)
        x = pl.multiple_of(offsets[slot, 1] - col0, H)
        return pl.ds(y, S), pl.ds(x, S)

    def pair(step, carry):
        found = []
        for slot in (2 * step, 2 * step + 1):
            rows, cols = place(slot)
            probe_re, probe_im = probe[0], probe[1]
            patch_re, patch_im = obj[0, rows, cols], obj[1, rows, cols]
            found.append(
                project(
                    patch_re, patch_im, probe_re, probe_im, amps[slot], right[...], left[...]
                )
            )
        grads = [0.0, 0.0, 0.0]
        for slot, (diff_re, diff_im) in zip((2 * step, 2 * step + 1), found):
            rows, cols = place(slot)
            mask = (slot < total).astype(F32)
            probe_re, probe_im = probe[0], probe[1]
            patch_re, patch_im = obj[0, rows, cols], obj[1, rows, cols]
            diff_re, diff_im = diff_re * mask, diff_im * mask
            deposits[0, rows, cols] += probe_re * diff_re + probe_im * diff_im
            deposits[1, rows, cols] += probe_re * diff_im - probe_im * diff_re
            grads[0] += patch_re * diff_re + patch_im * diff_im
            grads[1] += patch_re * diff_im - patch_im * diff_re
            grads[2] += (patch_re * patch_re + patch_im * patch_im) * mask
        for c in range(3):
            for ct in range(2):
                sums[ct, :, c] += grads[c][:, ct * H : (ct + 1) * H].reshape(32, 8, H)
        return carry

    lax.fori_loop(0, (total + 1) // 2, pair, 0)


def columns_as_rows(columns, out):
    lane = lax.broadcasted_iota(jnp.int32, (X, H), 1)
    gathered = jnp.zeros((X, H), F32)
    for k, column in enumerate(columns):
        gathered = jnp.where(lane == k, column, gathered)
    out[...] = gathered.T[:8]


def first_kernel(
    obj, below, beside, probe, amps, offsets, live, right, left,
    deposits, sums, lines, starts, canvas, sems,
):
    copies = [
        pltpu.make_async_copy(obj, canvas.at[:, pl.ds(0, T), pl.ds(0, T)], sems.at[0]),
        pltpu.make_async_copy(
            below.at[:, pl.ds(0, H), :], canvas.at[:, pl.ds(T, H), :], sems.at[1]
        ),
        pltpu.make_async_copy(beside, canvas.at[:, pl.ds(0, T), pl.ds(T, H)], sems.at[2]),
    ]
    for copy in copies:
        copy.start()
    lane = lax.broadcasted_iota(jnp.int32, (8, H), 1)
    row0 = lax.axis_index("row") * T
    col0 = lax.axis_index("col") * T
    found = jnp.zeros((8, H), F32)
    for slot in range(8):
        at = (offsets[slot, 0] - row0) // H * 4 + (offsets[slot, 1] - col0) // H
        used = (slot < live[0, 0]).astype(F32)
        found += jnp.where(lane == at, used, 0.0)
    starts[...] = found
    for copy in copies:
        copy.wait()
    visit_slots(canvas, probe, amps, offsets, live, right, left, deposits, sums)
    columns_as_rows(
        [deposits[c, :, T - 1 : T] for c in range(2)]
        + [deposits[c, :, H : H + 1] for c in range(2)]
        + [canvas[c, :, T - 1 : T] for c in range(2)]
        + [canvas[c, :, H : H + 1] for c in range(2)],
        lines,
    )


def first_pass(obj, below, beside, probe, amps, offsets, live, right, left):
    return pl.pallas_call(
        first_kernel,
        name="first_slots",
        out_shape=[
            jax.ShapeDtypeStruct((2, X, X), F32),
            jax.ShapeDtypeStruct((2, 32, 3, 8, H), F32),
            jax.ShapeDtypeStruct((8, X), F32),
            jax.ShapeDtypeStruct((8, H), F32),
        ],
        in_specs=[ANY, ANY, ANY, VMEM, VMEM, SMEM, SMEM, VMEM, VMEM],
        out_specs=[VMEM] * 4,
        scratch_shapes=[pltpu.VMEM((2, X, X), F32), pltpu.SemaphoreType.DMA((3,))],
        compiler_params=pltpu.CompilerParams(vmem_limit_bytes=VMEM_BYTES),
    )(obj, below, beside, probe, amps, offsets, live, right, left)


class ProbeSum:
    def __init__(self, copies, sums, probe, out, pair_in, part, z_in, z_part, plane_in):
        row, col = lax.axis_index("row"), lax.axis_index("col")
        self.z, x = row // 4, lax.rem(row, 4)
        y, self.core = col // 2, lax.rem(col, 2)
        self.p = x * 4 + y
        self.tile = lax.rem(self.p, 8)
        self.copies, self.sums, self.probe, self.out = copies, sums, probe, out
        self.pair_in, self.part, self.z_in, self.z_part = pair_in, part, z_in, z_part
        self.plane_in = plane_in
        self.other = (row, y * 2 + 1 - self.core)
        self.z_peers = [(lax.rem(self.z + k, 4) * 4 + x, col) for k in range(1, 4)]
        self.plane_peers = [self.in_plane(lax.rem(self.p + k, 16)) for k in range(1, 16)]

    def in_plane(self, p):
        return (self.z * 4 + p // 4, lax.rem(p, 4) * 2 + self.core)

    def peers(self):
        return self.z_peers + self.plane_peers

    def start_pair(self):
        self.pair = self.copies.start(self.sums.at[1 - self.core], self.pair_in, self.other)

    def start_z(self):
        self.pair.wait_recv()
        self.part[...] = self.sums[self.core] + self.pair_in[...]
        self.z_sent = []
        for k in range(1, 4):
            at = lax.rem(self.z + k, 4) * 8
            self.z_sent.append(
                self.copies.start(
                    self.part.at[pl.ds(at, 8)], self.z_in.at[k - 1], self.z_peers[k - 1]
                )
            )

    def start_plane(self):
        for copy in self.z_sent:
            copy.wait_recv()
        self.z_part[...] = (
            self.part[pl.ds(self.z * 8, 8)] + self.z_in[0] + self.z_in[1] + self.z_in[2]
        )
        self.plane_in[self.p] = self.z_part[self.tile]
        for k in range(1, 16):
            tile = lax.rem(self.p + k, 8)
            self.copies.start(
                self.z_part.at[tile], self.plane_in.at[self.p], self.plane_peers[k - 1]
            )
        self.first = self.copies.count - 15

    def landed(self, ref, number):
        pltpu.make_async_remote_copy(
            src_ref=ref,
            dst_ref=ref,
            send_sem=self.copies.send_sems.at[number],
            recv_sem=self.copies.recv_sems.at[number],
            device_id=self.other,
            device_id_type=MESH,
        ).wait_recv()

    def start_back(self):
        for k in range(1, 16):
            self.landed(self.plane_in.at[lax.rem(self.p + 16 - k, 16)], self.first + k - 1)
        total = self.plane_in[0]
        for k in range(1, 16):
            total = total + self.plane_in[k]
        rt = self.z * 8 + self.tile
        rows, cols = pl.ds(pl.multiple_of(rt * 8, 8), 8), pl.ds(pl.multiple_of(self.core * H, H), H)
        inverse = 1.0 / (total[2] + 1.0)
        for c in range(2):
            self.out[self.core, rt, c] = self.probe[c, rows, cols] + total[c] * inverse
        mine = self.out.at[self.core, rt]
        group = self.p // 8 * 8
        self.first = self.copies.count
        for k in range(1, 8):
            self.copies.start(mine, mine, self.in_plane(group + lax.rem(self.tile + k, 8)))

    def start_back_z(self):
        for k in range(1, 8):
            tile = lax.rem(self.tile + 8 - k, 8)
            self.landed(self.out.at[self.core, self.z * 8 + tile], self.first + k - 1)
        mine = self.out.at[self.core, pl.ds(self.z * 8, 8)]
        self.first = self.copies.count
        for k in range(1, 4):
            self.copies.start(mine, mine, self.z_peers[k - 1])

    def start_back_pair(self):
        for k in range(1, 4):
            at = lax.rem(self.z + 4 - k, 4) * 8
            self.landed(self.out.at[self.core, pl.ds(at, 8)], self.first + k - 1)
        mine = self.out.at[self.core]
        self.first = self.copies.count
        self.copies.start(mine, mine, self.other)

    def end(self):
        self.landed(self.out.at[1 - self.core], self.first)


PROBE_SCRATCH = [
    pltpu.VMEM((32, 3, 8, H), F32),
    pltpu.VMEM((32, 3, 8, H), F32),
    pltpu.VMEM((3, 8, 3, 8, H), F32),
    pltpu.VMEM((8, 3, 8, H), F32),
    pltpu.VMEM((16, 3, 8, H), F32),
]
PROBE_COPIES = 1 + 3 + 15 + 7 + 3 + 1


def middle_kernel(
    deposits, sums, lines, starts, obj, beside, classes, probe,
    from_left, from_right, from_up, from_down, lines_lr, lines_up, lines_down,
    starts_lr, starts_up, starts_down, obj_up, class_down, class_right, probe_out,
    corners, pair_in, part, z_in, z_part, plane_in, own_sems, send_sems, recv_sems,
):
    up, down, left, right = around()
    copies = Copies(send_sems, recv_sems)
    probe_sum = ProbeSum(
        copies, sums, probe, probe_out, pair_in, part, z_in, z_part, plane_in
    )
    own = [
        pltpu.make_async_copy(
            deposits.at[:, pl.ds(r, STRIP), pl.ds(c, H)], corners.at[k], own_sems.at[k]
        )
        for k, (r, c) in enumerate(((0, 0), (0, T), (X - STRIP, 0), (X - STRIP, T)))
    ]
    for copy in own:
        copy.start()
    greet([up, down, left, right] + probe_sum.peers())
    probe_sum.start_pair()
    first = [
        copies.start(deposits.at[:, :, pl.ds(T, H)], from_left, right),
        copies.start(deposits.at[:, :, pl.ds(0, H)], from_right, left),
        copies.start(lines, lines_lr.at[0], right),
        copies.start(lines, lines_lr.at[1], left),
        copies.start(starts, starts_lr.at[0], right),
        copies.start(starts, starts_lr.at[1], left),
    ]
    middle = pl.ds(H, T - H)
    later = [
        copies.start(
            deposits.at[:, pl.ds(X - STRIP, STRIP), middle], from_up.at[:, :, middle], down
        ),
        copies.start(deposits.at[:, pl.ds(0, STRIP), middle], from_down.at[:, :, middle], up),
        copies.start(
            obj.at[:, pl.ds(T - RING, RING), :], obj_up.at[:, :, pl.ds(0, T)], down
        ),
        copies.start(
            beside.at[:, pl.ds(T - RING, RING), :], obj_up.at[:, :, pl.ds(T, H)], down
        ),
        copies.start(lines, lines_up.at[2], down),
        copies.start(lines, lines_down.at[2], up),
        copies.start(starts, starts_up.at[2], down),
        copies.start(starts, starts_down.at[2], up),
    ]
    class_side = copies.start(classes.at[:, pl.ds(0, H)], class_right, left)
    probe_sum.start_z()
    for copy in first:
        copy.wait_recv()
    for copy in own:
        copy.wait()
    corners[0] = corners[0] + from_left[:, pl.ds(0, STRIP), :]
    corners[1] = corners[1] + from_right[:, pl.ds(0, STRIP), :]
    corners[2] = corners[2] + from_left[:, pl.ds(X - STRIP, STRIP), :]
    corners[3] = corners[3] + from_right[:, pl.ds(X - STRIP, STRIP), :]
    later += [
        copies.start(corners.at[0], from_down.at[:, :, pl.ds(0, H)], up),
        copies.start(corners.at[1], from_down.at[:, :, pl.ds(T, H)], up),
        copies.start(corners.at[2], from_up.at[:, :, pl.ds(0, H)], down),
        copies.start(corners.at[3], from_up.at[:, :, pl.ds(T, H)], down),
        copies.start(lines_lr, lines_up.at[pl.ds(0, 2)], down),
        copies.start(lines_lr, lines_down.at[pl.ds(0, 2)], up),
        copies.start(starts_lr, starts_up.at[pl.ds(0, 2)], down),
        copies.start(starts_lr, starts_down.at[pl.ds(0, 2)], up),
    ]
    probe_sum.start_plane()
    later.append(
        copies.start(classes.at[pl.ds(0, H), :], class_down.at[:, pl.ds(0, T)], up)
    )
    class_side.wait_recv()
    later.append(
        copies.start(class_right.at[pl.ds(0, H), :], class_down.at[:, pl.ds(T, H)], up)
    )
    probe_sum.start_back()
    probe_sum.start_back_z()
    probe_sum.start_back_pair()
    for copy in later:
        copy.wait_recv()
    probe_sum.end()
    copies.finish()


def exchange_middle(deposits, sums, lines, starts, obj, beside, classes, probe):
    count = PROBE_COPIES + 25
    return pl.pallas_call(
        middle_kernel,
        name="exchange_middle",
        out_shape=[
            jax.ShapeDtypeStruct((2, X, H), F32),
            jax.ShapeDtypeStruct((2, X, H), F32),
            jax.ShapeDtypeStruct((2, STRIP, X), F32),
            jax.ShapeDtypeStruct((2, STRIP, X), F32),
            jax.ShapeDtypeStruct((2, 8, X), F32),
            jax.ShapeDtypeStruct((3, 8, X), F32),
            jax.ShapeDtypeStruct((3, 8, X), F32),
            jax.ShapeDtypeStruct((2, 8, H), F32),
            jax.ShapeDtypeStruct((3, 8, H), F32),
            jax.ShapeDtypeStruct((3, 8, H), F32),
            jax.ShapeDtypeStruct((2, RING, X), F32),
            jax.ShapeDtypeStruct((H, X), jnp.int32),
            jax.ShapeDtypeStruct((T, H), jnp.int32),
            jax.ShapeDtypeStruct((2, 32, 2, 8, H), F32),
        ],
        in_specs=[ANY, VMEM, ANY, ANY, ANY, ANY, ANY, VMEM],
        out_specs=[VMEM, VMEM] + [ANY] * 11 + [VMEM],
        scratch_shapes=[pltpu.VMEM((4, 2, STRIP, H), F32)]
        + PROBE_SCRATCH
        + [
            pltpu.SemaphoreType.DMA((4,)),
            pltpu.SemaphoreType.DMA((count,)),
            pltpu.SemaphoreType.DMA((count,)),
        ],
        compiler_params=pltpu.CompilerParams(
            collective_id=1, has_side_effects=True, vmem_limit_bytes=VMEM_BYTES
        ),
    )(deposits, sums, lines, starts, obj, beside, classes, probe)


def last_kernel(
    deposits, sums, lines, obj, probe,
    from_left, from_up, from_down, lines_lr, lines_up, obj_up, probe_out,
    corner_down, corner_up, pair_in, part, z_in, z_part, plane_in,
    own_sems, send_sems, recv_sems,
):
    up, down, left, right = around()
    copies = Copies(send_sems, recv_sems)
    probe_sum = ProbeSum(
        copies, sums, probe, probe_out, pair_in, part, z_in, z_part, plane_in
    )
    own = [
        pltpu.make_async_copy(
            deposits.at[:, pl.ds(X - STRIP, STRIP), pl.ds(0, H)], corner_down, own_sems.at[0]
        ),
        pltpu.make_async_copy(
            deposits.at[:, pl.ds(0, RING), pl.ds(0, H)], corner_up, own_sems.at[1]
        ),
    ]
    for copy in own:
        copy.start()
    greet([up, down, left, right] + probe_sum.peers())
    probe_sum.start_pair()
    middle = pl.ds(H, T - H)
    side = copies.start(deposits.at[:, :, pl.ds(T, H)], from_left, right)
    line_copies = [
        copies.start(lines, lines_lr.at[0], right),
        copies.start(lines, lines_lr.at[1], left),
    ]
    later = [
        copies.start(
            deposits.at[:, pl.ds(X - STRIP, STRIP), middle], from_up.at[:, :, middle], down
        ),
        copies.start(deposits.at[:, pl.ds(0, RING), middle], from_down.at[:, :, middle], up),
        copies.start(obj.at[:, pl.ds(T - RING, RING), pl.ds(0, T)], obj_up, down),
        copies.start(lines, lines_up.at[2], down),
    ]
    probe_sum.start_z()
    for copy in line_copies:
        copy.wait_recv()
    side.wait_recv()
    for copy in own:
        copy.wait()
    corner_down[...] = corner_down[...] + from_left[:, pl.ds(X - STRIP, STRIP), :]
    corner_up[...] = corner_up[...] + from_left[:, pl.ds(0, RING), :]
    later += [
        copies.start(corner_down, from_up.at[:, :, pl.ds(0, H)], down),
        copies.start(corner_up, from_down.at[:, :, pl.ds(0, H)], up),
        copies.start(lines_lr, lines_up.at[pl.ds(0, 2)], down),
    ]
    probe_sum.start_plane()
    probe_sum.start_back()
    probe_sum.start_back_z()
    probe_sum.start_back_pair()
    for copy in later:
        copy.wait_recv()
    probe_sum.end()
    copies.finish()


def exchange_last(deposits, sums, lines, obj, probe):
    count = PROBE_COPIES + 10
    return pl.pallas_call(
        last_kernel,
        name="exchange_last",
        out_shape=[
            jax.ShapeDtypeStruct((2, X, H), F32),
            jax.ShapeDtypeStruct((2, STRIP, T), F32),
            jax.ShapeDtypeStruct((2, RING, T), F32),
            jax.ShapeDtypeStruct((2, 8, X), F32),
            jax.ShapeDtypeStruct((3, 8, X), F32),
            jax.ShapeDtypeStruct((2, RING, T), F32),
            jax.ShapeDtypeStruct((2, 32, 2, 8, H), F32),
        ],
        in_specs=[ANY, VMEM, ANY, ANY, VMEM],
        out_specs=[VMEM] + [ANY] * 5 + [VMEM],
        scratch_shapes=[pltpu.VMEM((2, STRIP, H), F32), pltpu.VMEM((2, RING, H), F32)]
        + PROBE_SCRATCH
        + [
            pltpu.SemaphoreType.DMA((2,)),
            pltpu.SemaphoreType.DMA((count,)),
            pltpu.SemaphoreType.DMA((count,)),
        ],
        compiler_params=pltpu.CompilerParams(
            collective_id=2, has_side_effects=True, vmem_limit_bytes=VMEM_BYTES
        ),
    )(deposits, sums, lines, obj, probe)


def start_table(starts, starts_lr, starts_up, starts_down):
    def count(by, bx):
        dr, dc = by // 4, bx // 4
        at = by % 4 * 4 + bx % 4
        if dr == 0:
            ref = starts if dc == 0 else starts_lr
            return starts[0, at] if dc == 0 else ref[0 if dc < 0 else 1, 0, at]
        ref = starts_up if dr < 0 else starts_down
        return ref[{-1: 0, 1: 1, 0: 2}[dc], 0, at]

    return count


def block_weight(count, square, by, bx, rows):
    first, size = rows
    total = 1.0
    for qy in range(2):
        for qx in range(2):
            total = total + count(by - qy, bx - qx) * square[
                pl.ds(qy * H + first, size), pl.ds(qx * H, H)
            ]
    return total


def spread_lines(rows):
    packed = jnp.concatenate(rows + [jnp.zeros((H - len(rows), X), F32)], 0)
    return packed.T


def with_far(line, far_up, far_down):
    parts = [line[:, :H], line[:, H:T], line[:, T:]]
    if far_up is not None:
        parts[0] = parts[0] + far_up
    if far_down is not None:
        parts[2] = parts[2] + far_down
    return jnp.concatenate(parts, 1)


def shifted_sum(canvas, c, first, rows, cols):
    whole = canvas[c, pl.ds(first, rows), :]
    width = cols + 2 * H
    left = pltpu.roll(whole, 1, 1)[:, H : H + cols]
    right = pltpu.roll(whole, width - 1, 1)[:, H : H + cols]
    above = canvas[c, pl.ds(first - 1, rows), pl.ds(H, cols)]
    below = canvas[c, pl.ds(first + 1, rows), pl.ds(H, cols)]
    return below + above + right + left, whole[:, H : H + cols]


def rates(classes, weights):
    value = jnp.full(classes.shape, weights[0], F32)
    for k in range(1, 4):
        value = jnp.where(classes == k, weights[k], value)
    return value


def second_kernel(
    obj, below, beside, obj_up, deposits_in, from_left, from_right, from_up, from_down,
    lines_lr, lines_up, lines_down, starts, starts_lr, starts_up, starts_down,
    classes, class_down, class_right, weights, probe_old, probe_tiles,
    amps, offsets, live, right, left,
    obj_out, probe_out, deposits, sums, lines, canvas, square, sems,
):
    copies = [
        pltpu.make_async_copy(obj, canvas.at[:, pl.ds(RING, T), pl.ds(H, T)], sems.at[0]),
        pltpu.make_async_copy(
            below, canvas.at[:, pl.ds(RING + T, STRIP), pl.ds(H, X)], sems.at[1]
        ),
        pltpu.make_async_copy(
            beside, canvas.at[:, pl.ds(RING, T), pl.ds(H + T, H)], sems.at[2]
        ),
        pltpu.make_async_copy(obj_up, canvas.at[:, pl.ds(0, RING), pl.ds(H, X)], sems.at[3]),
    ]
    for copy in copies:
        copy.start()
    square[...] = probe_old[0] * probe_old[0] + probe_old[1] * probe_old[1]
    for c in range(2):
        for ct in range(2):
            probe_out[c, :, ct * H : (ct + 1) * H] = probe_tiles[ct, :, c].reshape(S, H)
    count = start_table(starts, starts_lr, starts_up, starts_down)
    rows = []
    for side, base in ((0, 0), (1, 2)):
        for c in range(2):
            k = base + c
            rows.append(
                with_far(
                    lines_lr[side, k : k + 1],
                    lines_up[side, k : k + 1, T:],
                    lines_down[side, k : k + 1, :H],
                )
            )
    for side, base in ((0, 4), (1, 6)):
        for c in range(2):
            k = base + c
            rows.append(
                jnp.concatenate(
                    [lines_lr[side, k : k + 1, :T], lines_down[side, k : k + 1, :H]], 1
                )
            )
    ring = spread_lines(rows)
    for copy in copies:
        copy.wait()
    for by in range(-1, 6):
        if by == -1:
            at, size, first = 0, RING, H - RING
        elif by == 5:
            at, size, first = RING + X, RING, 0
        else:
            at, size, first = RING + by * H, H, 0
        for bx in range(-1, 6):
            edge = bx in (-1, 5)
            if edge and by in (-1, 5):
                continue
            inverse = 1.0 / block_weight(count, square, by, bx, (first, size))
            cols = pl.ds(H + bx * H, H)
            for c in range(2):
                if edge:
                    k = 0 if bx == -1 else 2
                    piece = ring[by * H : (by + 1) * H]
                    grad = jnp.broadcast_to(piece[:, k + c : k + c + 1], (H, H))
                    base = jnp.broadcast_to(piece[:, k + 4 + c : k + 5 + c], (H, H))
                else:
                    base = canvas[c, pl.ds(at, size), cols]
                    block = pl.ds(bx * H, H)
                    if by == -1:
                        grad = from_up[c, 0:RING, block]
                    elif by == 5:
                        grad = from_down[c, H:STRIP, block]
                    else:
                        grad = deposits_in[c, pl.ds(by * H, H), block]
                        if by == 0:
                            grad = grad + from_up[c, RING:STRIP, block]
                        if by == 4:
                            grad = grad + from_down[c, 0:H, block]
                        if bx == 0:
                            grad = grad + from_left[c, pl.ds(by * H, H), :]
                        if bx == 4:
                            grad = grad + from_right[c, pl.ds(by * H, H), :]
                canvas[c, pl.ds(at, size), cols] = base + grad * inverse
    blank_outside(canvas, RING + T, H + T)
    for by in range(5):
        if by < 4:
            levels = jnp.concatenate(
                [classes[pl.ds(by * H, H), :], class_right[pl.ds(by * H, H), :]], 1
            )
        else:
            levels = class_down[...]
        rate = rates(levels, weights)
        for c in range(2):
            around_sum, center = shifted_sum(canvas, c, RING + by * H, H, X)
            obj_out[c, pl.ds(by * H, H), :] = center + rate * (around_sum - 4.0 * center)
    visit_slots(obj_out, probe_out, amps, offsets, live, right, left, deposits, sums)
    columns_as_rows(
        [deposits[c, :, T - 1 : T] for c in range(2)]
        + [deposits[c, :, 0:1] for c in range(2)]
        + [deposits[c, :, T : T + 1] for c in range(2)]
        + [obj_out[c, :, T - 1 : T] for c in range(2)],
        lines,
    )


def blank_outside(canvas, rows_end, cols_end):
    row, col = lax.axis_index("row"), lax.axis_index("col")
    _, height, width = canvas.shape

    @pl.when(row == 0)
    def _():
        canvas[:, 0:RING, :] = jnp.zeros((2, RING, width), F32)

    @pl.when(row == 15)
    def _():
        canvas[:, rows_end:, :] = jnp.zeros((2, height - rows_end, width), F32)

    @pl.when(col == 0)
    def _():
        canvas[:, :, 0:H] = jnp.zeros((2, height, H), F32)

    @pl.when(col == 7)
    def _():
        canvas[:, :, cols_end:] = jnp.zeros((2, height, width - cols_end), F32)


def second_pass(*operands):
    specs = [ANY] * 4 + [VMEM] * 8 + [SMEM] * 4 + [VMEM] * 3 + [SMEM] + [VMEM] * 2
    specs += [VMEM, SMEM, SMEM, VMEM, VMEM]
    return pl.pallas_call(
        second_kernel,
        name="second_slots",
        out_shape=[
            jax.ShapeDtypeStruct((2, X, X), F32),
            jax.ShapeDtypeStruct((2, S, S), F32),
            jax.ShapeDtypeStruct((2, X, X), F32),
            jax.ShapeDtypeStruct((2, 32, 3, 8, H), F32),
            jax.ShapeDtypeStruct((8, X), F32),
        ],
        in_specs=specs,
        out_specs=[VMEM] * 5,
        scratch_shapes=[
            pltpu.VMEM((2, X + 2 * RING, X + 2 * H), F32),
            pltpu.VMEM((S, S), F32),
            pltpu.SemaphoreType.DMA((4,)),
        ],
        compiler_params=pltpu.CompilerParams(vmem_limit_bytes=VMEM_BYTES),
    )(*operands)


def final_kernel(
    obj, obj_up, deposits, from_left, from_up, from_down, lines_lr, lines_up,
    starts, starts_lr, starts_up, starts_down, classes, weights, probe_old, probe_tiles,
    obj_out, probe_out, canvas, square, sems,
):
    copies = [
        pltpu.make_async_copy(
            obj.at[:, pl.ds(0, T + RING), :],
            canvas.at[:, pl.ds(RING, T + RING), pl.ds(H, X)],
            sems.at[0],
        ),
        pltpu.make_async_copy(obj_up, canvas.at[:, pl.ds(0, RING), pl.ds(H, T)], sems.at[1]),
    ]
    for copy in copies:
        copy.start()
    square[...] = probe_old[0] * probe_old[0] + probe_old[1] * probe_old[1]
    for c in range(2):
        for ct in range(2):
            probe_out[c, :, ct * H : (ct + 1) * H] = probe_tiles[ct, :, c].reshape(S, H)
    count = start_table(starts, starts_lr, starts_up, starts_down)
    rows = []
    for c in range(2):
        rows.append(with_far(lines_lr[0, c : c + 1], lines_up[0, c : c + 1, T:], None))
    for c in range(2):
        far = lines_up[1, 2 + c : 3 + c, T:] + lines_up[2, 4 + c : 5 + c, T:]
        rows.append(with_far(lines_lr[1, 2 + c : 3 + c], far, None))
    for c in range(2):
        rows.append(lines_lr[0, 6 + c : 7 + c])
    ring = spread_lines(rows)
    for copy in copies:
        copy.wait()
    for by in range(-1, 5):
        if by == -1:
            at, size, first = 0, RING, H - RING
        elif by == 4:
            at, size, first = RING + T, RING, 0
        else:
            at, size, first = RING + by * H, H, 0
        for bx in range(-1, 5):
            edge = bx in (-1, 4)
            if edge and by in (-1, 4):
                continue
            inverse = 1.0 / block_weight(count, square, by, bx, (first, size))
            cols = pl.ds(H + bx * H, H)
            for c in range(2):
                block = pl.ds(max(bx, 0) * H, H)
                base = canvas[c, pl.ds(at, size), cols]
                if edge:
                    piece = ring[by * H : (by + 1) * H]
                    k = c if bx == -1 else 2 + c
                    grad = jnp.broadcast_to(piece[:, k : k + 1], (H, H))
                    if bx == -1:
                        base = jnp.broadcast_to(piece[:, 4 + c : 5 + c], (H, H))
                    else:
                        grad = grad + deposits[c, pl.ds(by * H, H), block]
                elif by == -1:
                    grad = from_up[c, 0:RING, block]
                else:
                    grad = deposits[c, pl.ds(by * H, size), block]
                    if by == 0:
                        grad = grad + from_up[c, RING:STRIP, block]
                    if by == 4:
                        grad = grad + from_down[c, :, block]
                    if bx == 0:
                        grad = grad + from_left[c, pl.ds(by * H, size), :]
                canvas[c, pl.ds(at, size), cols] = base + grad * inverse
    blank_outside(canvas, RING + T, H + T)
    for by in range(4):
        rate = rates(classes[pl.ds(by * H, H), :], weights)
        for c in range(2):
            around_sum, center = shifted_sum(canvas, c, RING + by * H, H, T)
            obj_out[c, pl.ds(by * H, H), :] = center + rate * (around_sum - 4.0 * center)


def final_pass(*operands):
    specs = [ANY] * 2 + [VMEM] * 6 + [SMEM] * 4 + [VMEM, SMEM, VMEM, VMEM]
    return pl.pallas_call(
        final_kernel,
        name="final_update",
        out_shape=[
            jax.ShapeDtypeStruct((2, T, T), F32),
            jax.ShapeDtypeStruct((2, S, S), F32),
        ],
        in_specs=specs,
        out_specs=[VMEM] * 2,
        scratch_shapes=[
            pltpu.VMEM((2, T + 2 * RING, T + 2 * H), F32),
            pltpu.VMEM((S, S), F32),
            pltpu.SemaphoreType.DMA((2,)),
        ],
        compiler_params=pltpu.CompilerParams(vmem_limit_bytes=VMEM_BYTES),
    )(*operands)


def per_device(
    object_init, probe_init, amplitudes, scan_offsets, live_count, smooth_class, class_weight
):
    right, left = (jnp.asarray(table) for table in dft_blocks())
    amps = amplitudes.reshape(8, S, S)
    offsets = scan_offsets.reshape(8, 2)
    below, beside = exchange_strips(object_init)
    deposits, sums, lines, starts = first_pass(
        object_init, below, beside, probe_init, amps, offsets, live_count, right, left
    )
    (
        from_left, from_right, from_up, from_down, lines_lr, lines_up, lines_down,
        starts_lr, starts_up, starts_down, obj_up, class_down, class_right, probe_tiles,
    ) = exchange_middle(
        deposits, sums, lines, starts, object_init, beside, smooth_class, probe_init
    )
    object_next, probe_next, deposits, sums, lines = second_pass(
        object_init, below, beside, obj_up, deposits, from_left, from_right, from_up, from_down,
        lines_lr, lines_up, lines_down, starts, starts_lr, starts_up, starts_down,
        smooth_class, class_down, class_right, class_weight, probe_init, probe_tiles,
        amps, offsets, live_count, right, left,
    )
    from_left, from_up, from_down, lines_lr, lines_up, obj_up, probe_tiles = exchange_last(
        deposits, sums, lines, object_next, probe_next
    )
    return tuple(
        final_pass(
            object_next, obj_up, deposits, from_left, from_up, from_down, lines_lr, lines_up,
            starts, starts_lr, starts_up, starts_down, smooth_class, class_weight,
            probe_next, probe_tiles,
        )
    )


def solution(mesh):
    in_specs = (
        P(None, "row", "col"),
        P(),
        P("row", "col", None, None, None),
        P("row", "col", None, None),
        P("row", "col"),
        P("row", "col"),
        P(),
    )
    out_specs = (P(None, "row", "col"), P())
    return jax.shard_map(
        per_device, mesh=mesh, in_specs=in_specs, out_specs=out_specs, check_vma=False
    )
```

```python
import functools
import math

import jax
import jax.numpy as jnp
import ml_dtypes
import numpy as np
from jax import lax
from jax.experimental import pallas as pl
from jax.experimental.pallas import tpu as pltpu
from jax.sharding import PartitionSpec as P

F32 = jnp.float32
BF16 = jnp.bfloat16
T = 512
S = 256
H = 128
X = T + H
RING = 8
STRIP = H + RING
MESH = pl.DeviceIdType.MESH
ANY = pl.BlockSpec(memory_space=pl.ANY)
VMEM = pl.BlockSpec(memory_space=pltpu.VMEM)
SMEM = pl.BlockSpec(memory_space=pltpu.SMEM)
VMEM_BYTES = 64 * 1024 * 1024


def dft_blocks():
    index = np.arange(S)
    phases = 2.0 * math.pi / S * (index[:, None] * index[None, :] % S)
    re = (np.cos(phases) / math.sqrt(S)).astype(ml_dtypes.bfloat16)
    im = (-np.sin(phases) / math.sqrt(S)).astype(ml_dtypes.bfloat16)
    right = np.block([[re, im], [-im, re]])
    left = np.block([[re, -im], [im, re]])
    return right, left


class Copies:
    def __init__(self, send_sems, recv_sems):
        self.send_sems, self.recv_sems, self.count = send_sems, recv_sems, 0
        self.started = []

    def make(self, src, dst, device):
        k = self.count
        self.count += 1
        return pltpu.make_async_remote_copy(
            src_ref=src,
            dst_ref=dst,
            send_sem=self.send_sems.at[k],
            recv_sem=self.recv_sems.at[k],
            device_id=device,
            device_id_type=MESH,
        )

    def start(self, src, dst, device):
        copy = self.make(src, dst, device)
        copy.start()
        self.started.append(copy)
        return copy

    def finish(self):
        assert self.count == self.send_sems.shape[0]
        for copy in self.started:
            copy.wait_send()


def around():
    row, col = lax.axis_index("row"), lax.axis_index("col")
    up = (lax.rem(row + 15, 16), col)
    down = (lax.rem(row + 1, 16), col)
    left = (row, lax.rem(col + 7, 8))
    right = (row, lax.rem(col + 1, 8))
    return up, down, left, right


def greet(devices):
    barrier = pltpu.get_barrier_semaphore()
    for device in devices:
        pl.semaphore_signal(barrier, inc=1, device_id=device, device_id_type=MESH)
    pl.semaphore_wait(barrier, len(devices))


def count_starts(offsets, live, out):
    lane = lax.broadcasted_iota(jnp.int32, (8, H), 1)
    row0 = lax.axis_index("row") * T
    col0 = lax.axis_index("col") * T
    found = jnp.zeros((8, H), F32)
    for slot in range(8):
        at = lax.div(offsets[0, slot] - row0, H) * 4 + lax.div(offsets[1, slot] - col0, H)
        found += jnp.where((lane == at) & (live[0, 0] > slot), 1.0, 0.0)
    out[...] = found


def strips_kernel(
    obj, offsets, live, from_below, from_right, starts, counted, own_sem, send_sems, recv_sems
):
    up, down, left, right = around()
    row, col = lax.axis_index("row"), lax.axis_index("col")
    near = {
        (dr, dc): (lax.rem(row + dr + 16, 16), lax.rem(col + dc + 8, 8))
        for dr in (-1, 0, 1)
        for dc in (-1, 0, 1)
        if (dr, dc) != (0, 0)
    }
    count_starts(offsets, live, counted)
    greet(list(near.values()))
    copies = Copies(send_sems, recv_sems)
    rows = copies.start(
        obj.at[:, pl.ds(0, STRIP), :], from_below.at[:, :, pl.ds(0, T)], up
    )
    side = copies.start(obj.at[:, :, pl.ds(0, H)], from_right, left)
    small = [
        copies.start(counted, starts.at[1 - dr, 1 - dc], device)
        for (dr, dc), device in near.items()
    ]
    own = pltpu.make_async_copy(counted, starts.at[1, 1], own_sem)
    own.start()
    side.wait_recv()
    corner = copies.start(
        from_right.at[:, pl.ds(0, STRIP), :], from_below.at[:, :, pl.ds(T, H)], up
    )
    for copy in small:
        copy.wait_recv()
    own.wait()
    rows.wait_recv()
    corner.wait_recv()
    copies.finish()


def exchange_strips(obj, offsets, live):
    return pl.pallas_call(
        strips_kernel,
        name="object_strips",
        out_shape=[
            jax.ShapeDtypeStruct((2, STRIP, X), F32),
            jax.ShapeDtypeStruct((2, T, H), F32),
            jax.ShapeDtypeStruct((3, 3, 8, H), F32),
        ],
        in_specs=[ANY, SMEM, SMEM],
        out_specs=[ANY, ANY, ANY],
        scratch_shapes=[
            pltpu.VMEM((8, H), F32),
            pltpu.SemaphoreType.DMA,
            pltpu.SemaphoreType.DMA((11,)),
            pltpu.SemaphoreType.DMA((11,)),
        ],
        compiler_params=pltpu.CompilerParams(
            collective_id=0, has_side_effects=True, vmem_limit_bytes=VMEM_BYTES
        ),
    )(obj, offsets, live)


def project(patch_re, patch_im, probe_re, probe_im, measured, right, left):
    exit_re = (probe_re * patch_re - probe_im * patch_im).astype(BF16)
    exit_im = (probe_re * patch_im + probe_im * patch_re).astype(BF16)
    half = jnp.dot(
        jnp.concatenate([exit_re, exit_im], 1), right, preferred_element_type=F32
    ).astype(BF16)
    far = jnp.dot(
        left, jnp.concatenate([half[:, :S], half[:, S:]], 0), preferred_element_type=F32
    )
    far_re, far_im = far[:S], far[S:]
    square = far_re * far_re + far_im * far_im
    factor = measured.astype(F32) * lax.rsqrt(jnp.maximum(square, 1.0)) - 1.0
    corr = jnp.concatenate([(far_re * factor).astype(BF16), (far_im * factor).astype(BF16)], 1)
    back = jnp.dot(corr, left, preferred_element_type=F32).astype(BF16)
    diff = jnp.dot(
        right, jnp.concatenate([back[:, :S], back[:, S:]], 0), preferred_element_type=F32
    )
    return diff[:S], diff[S:]


def visit_slots(obj, probe, amps, offsets, live, right, left, deposits, sums):
    row0 = lax.axis_index("row") * T
    col0 = lax.axis_index("col") * T
    total = live[0, 0]

    def place(slot):
        y = pl.multiple_of(offsets[0, slot] - row0, H)
        x = pl.multiple_of(offsets[1, slot] - col0, H)
        return pl.ds(y, S), pl.ds(x, S)

    def pair(step, carry):
        found = []
        for slot in (2 * step, 2 * step + 1):
            rows, cols = place(slot)
            probe_re, probe_im = probe[0], probe[1]
            patch_re, patch_im = obj[0, rows, cols], obj[1, rows, cols]
            found.append(
                project(
                    patch_re, patch_im, probe_re, probe_im, amps[slot], right[...], left[...]
                )
            )
        grads = [0.0, 0.0, 0.0]
        for slot, (diff_re, diff_im) in zip((2 * step, 2 * step + 1), found):
            rows, cols = place(slot)
            mask = (slot < total).astype(F32)
            probe_re, probe_im = probe[0], probe[1]
            patch_re, patch_im = obj[0, rows, cols], obj[1, rows, cols]
            diff_re, diff_im = diff_re * mask, diff_im * mask
            deposits[0, rows, cols] += probe_re * diff_re + probe_im * diff_im
            deposits[1, rows, cols] += probe_re * diff_im - probe_im * diff_re
            grads[0] += patch_re * diff_re + patch_im * diff_im
            grads[1] += patch_re * diff_im - patch_im * diff_re
            grads[2] += (patch_re * patch_re + patch_im * patch_im) * mask
        for c in range(3):
            for ct in range(2):
                sums[ct, :, c] += grads[c][:, ct * H : (ct + 1) * H].reshape(32, 8, H)
        return carry

    lax.fori_loop(0, (total + 1) // 2, pair, 0)


def columns_as_rows(columns, out):
    lane = lax.broadcasted_iota(jnp.int32, (X, H), 1)
    gathered = jnp.zeros((X, H), F32)
    for k, column in enumerate(columns):
        gathered = jnp.where(lane == k, column, gathered)
    out[...] = gathered.T[:8]


def slots_kernel(first, *refs):
    obj_refs, refs = (refs[:3], refs[3:]) if first else (refs[:1], refs[1:])
    (
        probe_in, amps_in, offsets, live, right, left,
        deposits, sums, lines, canvas, probe, amps, sems,
    ) = refs
    pairs = [(probe_in, probe), (amps_in, amps)]
    if first:
        obj, below, beside = obj_refs
        pairs += [
            (obj, canvas.at[:, pl.ds(0, T), pl.ds(0, T)]),
            (below.at[:, pl.ds(0, H), :], canvas.at[:, pl.ds(T, H), :]),
            (beside, canvas.at[:, pl.ds(0, T), pl.ds(T, H)]),
        ]
    else:
        pairs += [(obj_refs[0], canvas)]
    copies = [
        pltpu.make_async_copy(src, dst, sems.at[k]) for k, (src, dst) in enumerate(pairs)
    ]
    for copy in copies:
        copy.start()
    deposits[...] = jnp.zeros_like(deposits)
    sums[...] = jnp.zeros_like(sums)
    for copy in copies:
        copy.wait()
    visit_slots(canvas, probe, amps, offsets, live, right, left, deposits, sums)
    columns = [deposits[c, :, T - 1 : T] for c in range(2)]
    if first:
        columns += [deposits[c, :, H : H + 1] for c in range(2)]
        columns += [canvas[c, :, T - 1 : T] for c in range(2)]
        columns += [canvas[c, :, H : H + 1] for c in range(2)]
    else:
        columns += [deposits[c, :, 0:1] for c in range(2)]
        columns += [deposits[c, :, T : T + 1] for c in range(2)]
        columns += [canvas[c, :, T - 1 : T] for c in range(2)]
    columns_as_rows(columns, lines)


def slots_pass(obj_parts, probe, amps, offsets, live, right, left):
    count = len(obj_parts)
    return pl.pallas_call(
        functools.partial(slots_kernel, count == 3),
        name="first_slots" if count == 3 else "second_slots",
        out_shape=[
            jax.ShapeDtypeStruct((2, X, X), F32),
            jax.ShapeDtypeStruct((2, 32, 3, 8, H), F32),
            jax.ShapeDtypeStruct((8, X), F32),
        ],
        in_specs=[ANY] * count + [ANY, ANY, SMEM, SMEM, VMEM, VMEM],
        out_specs=[VMEM] * 3,
        scratch_shapes=[
            pltpu.VMEM((2, X, X), F32),
            pltpu.VMEM((2, S, S), F32),
            pltpu.VMEM((8, S, S), BF16),
            pltpu.SemaphoreType.DMA((5,)),
        ],
        compiler_params=pltpu.CompilerParams(vmem_limit_bytes=VMEM_BYTES),
    )(*obj_parts, probe, amps, offsets, live, right, left)


class ProbeSum:
    def __init__(self, copies, sums_in, sums, probe, out, pair_in, part, y_in, y_part, rows_in):
        self.row, col = lax.axis_index("row"), lax.axis_index("col")
        self.y, self.core = col // 2, lax.rem(col, 2)
        self.tile = lax.rem(self.row, 8)
        self.copies, self.sums, self.probe, self.out = copies, sums, probe, out
        self.sums_in = sums_in
        self.pair_in, self.part, self.y_in, self.y_part = pair_in, part, y_in, y_part
        self.rows_in = rows_in
        self.col = col
        self.other = (self.row, self.y * 2 + 1 - self.core)
        self.y_peers = [
            (self.row, lax.rem(self.y + k, 4) * 2 + self.core) for k in range(1, 4)
        ]
        self.row_peers = [(lax.rem(self.row + k, 16), col) for k in range(1, 16)]

    def peers(self):
        return self.y_peers + self.row_peers

    def start_pair(self):
        self.pair = self.copies.start(self.sums_in.at[1 - self.core], self.pair_in, self.other)

    def start_y(self):
        self.pair.wait_recv()
        self.part[...] = self.sums[self.core] + self.pair_in[...]
        self.y_sent = []
        for k in range(1, 4):
            at = lax.rem(self.y + k, 4) * 8
            self.y_sent.append(
                self.copies.start(
                    self.part.at[pl.ds(at, 8)], self.y_in.at[k - 1], self.y_peers[k - 1]
                )
            )

    def start_rows(self):
        for copy in self.y_sent:
            copy.wait_recv()
        self.y_part[...] = (
            self.part[pl.ds(self.y * 8, 8)] + self.y_in[0] + self.y_in[1] + self.y_in[2]
        )
        self.rows_in[self.row] = self.y_part[self.tile]
        for k in range(1, 16):
            tile = lax.rem(self.row + k, 8)
            self.copies.start(
                self.y_part.at[tile], self.rows_in.at[self.row], self.row_peers[k - 1]
            )
        self.first = self.copies.count - 15

    def landed(self, ref, number):
        pltpu.make_async_remote_copy(
            src_ref=ref,
            dst_ref=ref,
            send_sem=self.copies.send_sems.at[number],
            recv_sem=self.copies.recv_sems.at[number],
            device_id=self.other,
            device_id_type=MESH,
        ).wait_recv()

    def start_back(self):
        for k in range(1, 16):
            self.landed(self.rows_in.at[lax.rem(self.row + 16 - k, 16)], self.first + k - 1)
        total = self.rows_in[0]
        for k in range(1, 16):
            total = total + self.rows_in[k]
        rt = self.y * 8 + self.tile
        rows, cols = pl.ds(pl.multiple_of(rt * 8, 8), 8), pl.ds(pl.multiple_of(self.core * H, H), H)
        inverse = 1.0 / (total[2] + 1.0)
        for c in range(2):
            self.out[self.core, rt, c] = self.probe[c, rows, cols] + total[c] * inverse
        mine = self.out.at[self.core, rt]
        group = self.row // 8 * 8
        self.first = self.copies.count
        for k in range(1, 8):
            self.copies.start(mine, mine, (group + lax.rem(self.tile + k, 8), self.col))

    def start_back_y(self):
        for k in range(1, 8):
            tile = lax.rem(self.tile + 8 - k, 8)
            self.landed(self.out.at[self.core, self.y * 8 + tile], self.first + k - 1)
        mine = self.out.at[self.core, pl.ds(self.y * 8, 8)]
        self.first = self.copies.count
        for k in range(1, 4):
            self.copies.start(mine, mine, self.y_peers[k - 1])

    def start_back_pair(self):
        for k in range(1, 4):
            at = lax.rem(self.y + 4 - k, 4) * 8
            self.landed(self.out.at[self.core, pl.ds(at, 8)], self.first + k - 1)
        mine = self.out.at[self.core]
        self.first = self.copies.count
        self.copies.start(mine, mine, self.other)

    def end(self):
        self.landed(self.out.at[1 - self.core], self.first)


PROBE_SCRATCH = [
    pltpu.VMEM((32, 3, 8, H), F32),
    pltpu.VMEM((32, 3, 8, H), F32),
    pltpu.VMEM((3, 8, 3, 8, H), F32),
    pltpu.VMEM((8, 3, 8, H), F32),
    pltpu.VMEM((16, 3, 8, H), F32),
]
PROBE_COPIES = 1 + 3 + 15 + 7 + 3 + 1


def start_table(starts):
    def count(by, bx):
        return starts[by // 4 + 1, bx // 4 + 1, 0, by % 4 * 4 + bx % 4]

    return count


def block_weight(count, square, by, bx, rows):
    first, size = rows
    total = 1.0
    for qy in range(2):
        for qx in range(2):
            total = total + count(by - qy, bx - qx) * square[
                pl.ds(qy * H + first, size), pl.ds(qx * H, H)
            ]
    return total


def spread_lines(rows):
    length = rows[0].shape[1]
    packed = jnp.concatenate(rows + [jnp.zeros((H - len(rows), length), F32)], 0)
    return packed.T


def shifted_sum(canvas, c, first, rows, cols):
    whole = canvas[c, pl.ds(first, rows), :]
    width = cols + 2 * H
    left = pltpu.roll(whole, 1, 1)[:, H : H + cols]
    right = pltpu.roll(whole, width - 1, 1)[:, H : H + cols]
    above = canvas[c, pl.ds(first - 1, rows), pl.ds(H, cols)]
    below = canvas[c, pl.ds(first + 1, rows), pl.ds(H, cols)]
    return below + above + right + left, whole[:, H : H + cols]


def rates(classes, weights):
    value = jnp.full(classes.shape, weights[0], F32)
    for k in range(1, 4):
        value = jnp.where(classes == k, weights[k], value)
    return value


def blank_sides(canvas, cols_end, first, size):
    col = lax.axis_index("col")
    width = canvas.shape[2]

    @pl.when(col == 0)
    def _():
        canvas[:, pl.ds(first, size), 0:H] = jnp.zeros((2, size, H), F32)

    @pl.when(col == 7)
    def _():
        canvas[:, pl.ds(first, size), cols_end:] = jnp.zeros((2, size, width - cols_end), F32)


def blank_outside(canvas, rows_end, cols_end):
    row = lax.axis_index("row")
    _, height, width = canvas.shape

    @pl.when(row == 0)
    def _():
        canvas[:, 0:RING, :] = jnp.zeros((2, RING, width), F32)

    @pl.when(row == 15)
    def _():
        canvas[:, rows_end:, :] = jnp.zeros((2, height - rows_end, width), F32)

    blank_sides(canvas, cols_end, 0, height)


MIDDLE = pl.ds(H, T - H)
LINES = [(0, 0), (0, 1), (1, 2), (1, 3), (0, 4), (0, 5), (1, 6), (1, 7)]
PIECES = [(c, first, size) for c in range(2) for first, size in ((0, 72), (72, 64))]


def unpack_probe(tiles, out):
    for c in range(2):
        for ct in range(2):
            out[c, :, ct * H : (ct + 1) * H] = tiles[ct, :, c].reshape(S, H)


def middle_kernel(
    deposits, sums_in, lines, obj, below, beside, classes_in, probe_in, starts, weights,
    obj_out, probe_out,
    canvas, grads, classes, probe, sums, square, corners, tiles,
    from_left, from_right, from_up, from_down, lines_lr, lines_up, lines_down,
    class_down, class_right,
    pair_in, part, y_in, y_part, rows_in, own_sems, send_sems, recv_sems,
):
    up, down, left, right = around()
    copies = Copies(send_sems, recv_sems)
    probe_sum = ProbeSum(copies, sums_in, sums, probe, tiles, pair_in, part, y_in, y_part, rows_in)
    pairs = [
        (sums_in, sums),
        (probe_in, probe),
        (deposits, grads),
        (obj, canvas.at[:, pl.ds(RING, T), pl.ds(H, T)]),
        (below, canvas.at[:, pl.ds(RING + T, STRIP), pl.ds(H, X)]),
        (beside, canvas.at[:, pl.ds(RING, T), pl.ds(H + T, H)]),
        (classes_in, classes),
    ]
    own = [pltpu.make_async_copy(src, dst, own_sems.at[k]) for k, (src, dst) in enumerate(pairs)]
    for copy in own:
        copy.start()
    greet([left, right] + probe_sum.peers())
    probe_sum.start_pair()
    later = [
        copies.start(lines, lines_up.at[2], down),
        copies.start(lines, lines_down.at[2], up),
        copies.start(
            obj.at[:, pl.ds(T - RING, RING), :], canvas.at[:, pl.ds(0, RING), pl.ds(H, T)], down
        ),
        copies.start(
            beside.at[:, pl.ds(T - RING, RING), :],
            canvas.at[:, pl.ds(0, RING), pl.ds(H + T, H)],
            down,
        ),
    ]

    def send_piece(k):
        c, first, size = PIECES[k]
        later.append(
            copies.start(
                deposits.at[c, pl.ds(X - STRIP + first, size), MIDDLE],
                from_up.at[c, pl.ds(first, size), MIDDLE],
                down,
            )
        )
        later.append(
            copies.start(
                deposits.at[c, pl.ds(first, size), MIDDLE],
                from_down.at[c, pl.ds(first, size), MIDDLE],
                up,
            )
        )

    for k in range(4):
        send_piece(k)
    own[0].wait()
    probe_sum.start_y()
    side = [
        copies.start(lines, lines_lr.at[0], right),
        copies.start(lines, lines_lr.at[1], left),
        copies.start(deposits.at[:, :, pl.ds(T, H)], from_left, right),
        copies.start(deposits.at[:, :, pl.ds(0, H)], from_right, left),
        copies.start(classes_in.at[:, pl.ds(0, H)], class_right, left),
    ]
    count = start_table(starts)
    for copy in own[1:]:
        copy.wait()
    square[...] = probe[0] * probe[0] + probe[1] * probe[1]

    def update(by, bx, ring=None):
        if by in (-1, 5):
            at, size, first = (0, RING, H - RING) if by == -1 else (RING + X, RING, 0)
        else:
            at, size, first = RING + by * H, H, 0
        edge = bx in (-1, 5)
        inverse = 1.0 / block_weight(count, square, by, bx, (first, size))
        cols = pl.ds(H + bx * H, H)
        for c in range(2):
            if edge:
                k = 0 if bx == -1 else 2
                grad = jnp.broadcast_to(ring[:, k + c : k + c + 1], (H, H))
                base = jnp.broadcast_to(ring[:, k + 4 + c : k + 5 + c], (H, H))
            else:
                base = canvas[c, pl.ds(at, size), cols]
                block = pl.ds(bx * H, H)
                if by == -1:
                    grad = from_up[c, 0:RING, block]
                elif by == 5:
                    grad = from_down[c, H:STRIP, block]
                else:
                    grad = grads[c, pl.ds(by * H, H), block]
                    if by == 0:
                        grad = grad + from_up[c, RING:STRIP, block]
                    if by == 4:
                        grad = grad + from_down[c, 0:H, block]
                    if bx == 0:
                        grad = grad + from_left[c, pl.ds(by * H, H), :]
                    if bx == 4:
                        grad = grad + from_right[c, pl.ds(by * H, H), :]
            canvas[c, pl.ds(at, size), cols] = base + grad * inverse

    def smooth(by):
        if by < 4:
            levels = jnp.concatenate(
                [classes[pl.ds(by * H, H), :], class_right[pl.ds(by * H, H), :]], 1
            )
        else:
            levels = class_down[...]
        rate = rates(levels, weights)
        for c in range(2):
            around_sum, center = shifted_sum(canvas, c, RING + by * H, H, X)
            obj_out[c, pl.ds(by * H, H), :] = center + rate * (around_sum - 4.0 * center)

    for by in (1, 2, 3):
        for bx in (1, 2, 3):
            update(by, bx)
    probe_sum.start_rows()
    for copy in side:
        copy.wait_recv()
    for k, (first, source) in enumerate(
        ((0, from_left), (0, from_right), (X - STRIP, from_left), (X - STRIP, from_right))
    ):
        column = 0 if k % 2 == 0 else T
        corners[k] = (
            grads[:, pl.ds(first, STRIP), pl.ds(column, H)]
            + source[:, pl.ds(first, STRIP), :]
        )
    probe_sum.start_back()
    later += [
        copies.start(lines_lr, lines_up.at[pl.ds(0, 2)], down),
        copies.start(lines_lr, lines_down.at[pl.ds(0, 2)], up),
        copies.start(corners.at[0], from_down.at[:, :, pl.ds(0, H)], up),
        copies.start(corners.at[2], from_up.at[:, :, pl.ds(0, H)], down),
        copies.start(corners.at[1], from_down.at[:, :, pl.ds(T, H)], up),
        copies.start(corners.at[3], from_up.at[:, :, pl.ds(T, H)], down),
    ]
    class_later = [
        copies.start(classes_in.at[pl.ds(0, H), :], class_down.at[:, pl.ds(0, T)], up),
        copies.start(class_right.at[pl.ds(0, H), :], class_down.at[:, pl.ds(T, H)], up),
    ]
    for by in (1, 2, 3):
        update(by, 0)
        update(by, 4)
    probe_sum.start_back_y()
    rows = [lines_lr[side_at, k : k + 1] for side_at, k in LINES]
    ring = spread_lines(rows)
    for by in (1, 2, 3):
        for bx in (-1, 5):
            update(by, bx, ring[by * H : (by + 1) * H])
    blank_sides(canvas, H + T, RING + H, 3 * H)
    smooth(2)
    probe_sum.start_back_pair()
    for copy in later:
        copy.wait_recv()
    far = []
    for n, (side_at, k) in enumerate(LINES):
        above = lines_up[side_at, k : k + 1, T:]
        below_it = lines_down[side_at, k : k + 1, :H]
        if n < 4:
            pieces = [rows[n][:, :H] + above, rows[n][:, T:] + below_it]
        else:
            pieces = [rows[n][:, :H], below_it]
        far.append(jnp.concatenate(pieces, 1))
    ring = spread_lines(far)
    for by in (0, 4):
        for bx in range(5):
            update(by, bx)
        for bx in (-1, 5):
            update(by, bx, ring[:H] if by == 0 else ring[H:])
    for by in (-1, 5):
        for bx in range(5):
            update(by, bx)
    blank_outside(canvas, RING + T, H + T)
    for by in (0, 1, 3):
        smooth(by)
    for copy in class_later:
        copy.wait_recv()
    smooth(4)
    probe_sum.end()
    unpack_probe(tiles, probe_out)
    copies.finish()


def exchange_middle(deposits, sums, lines, obj, below, beside, classes, probe, starts, weights):
    count = PROBE_COPIES + 25
    return pl.pallas_call(
        middle_kernel,
        name="exchange_middle",
        out_shape=[
            jax.ShapeDtypeStruct((2, X, X), F32),
            jax.ShapeDtypeStruct((2, S, S), F32),
        ],
        in_specs=[ANY] * 8 + [SMEM, SMEM],
        out_specs=[VMEM, VMEM],
        scratch_shapes=[
            pltpu.VMEM((2, X + 2 * RING, X + 2 * H), F32),
            pltpu.VMEM((2, X, X), F32),
            pltpu.VMEM((T, T), jnp.int32),
            pltpu.VMEM((2, S, S), F32),
            pltpu.VMEM((2, 32, 3, 8, H), F32),
            pltpu.VMEM((S, S), F32),
            pltpu.VMEM((4, 2, STRIP, H), F32),
            pltpu.VMEM((2, 32, 2, 8, H), F32),
            pltpu.VMEM((2, X, H), F32),
            pltpu.VMEM((2, X, H), F32),
            pltpu.VMEM((2, STRIP, X), F32),
            pltpu.VMEM((2, STRIP, X), F32),
            pltpu.VMEM((2, 8, X), F32),
            pltpu.VMEM((3, 8, X), F32),
            pltpu.VMEM((3, 8, X), F32),
            pltpu.VMEM((H, X), jnp.int32),
            pltpu.VMEM((T, H), jnp.int32),
        ]
        + PROBE_SCRATCH
        + [
            pltpu.SemaphoreType.DMA((7,)),
            pltpu.SemaphoreType.DMA((count,)),
            pltpu.SemaphoreType.DMA((count,)),
        ],
        compiler_params=pltpu.CompilerParams(
            collective_id=1, has_side_effects=True, vmem_limit_bytes=VMEM_BYTES
        ),
    )(deposits, sums, lines, obj, below, beside, classes, probe, starts, weights)


def last_kernel(
    deposits, sums_in, lines, obj, classes_in, probe_in, starts, weights,
    obj_out, probe_out,
    canvas, grads, classes, probe, sums, square, corner_down, corner_up, tiles,
    from_left, from_up, from_down, lines_lr, lines_up,
    pair_in, part, y_in, y_part, rows_in, own_sems, send_sems, recv_sems,
):
    up, down, left, right = around()
    copies = Copies(send_sems, recv_sems)
    probe_sum = ProbeSum(copies, sums_in, sums, probe, tiles, pair_in, part, y_in, y_part, rows_in)
    pairs = [
        (sums_in, sums),
        (probe_in, probe),
        (deposits, grads),
        (
            obj.at[:, pl.ds(0, T + RING), :],
            canvas.at[:, pl.ds(RING, T + RING), pl.ds(H, X)],
        ),
        (classes_in, classes),
    ]
    own = [pltpu.make_async_copy(src, dst, own_sems.at[k]) for k, (src, dst) in enumerate(pairs)]
    for copy in own:
        copy.start()
    greet([left, right] + probe_sum.peers())
    probe_sum.start_pair()
    later = [
        copies.start(lines, lines_up.at[2], down),
        copies.start(
            obj.at[:, pl.ds(T - RING, RING), pl.ds(0, T)],
            canvas.at[:, pl.ds(0, RING), pl.ds(H, T)],
            down,
        ),
        copies.start(deposits.at[:, pl.ds(0, RING), MIDDLE], from_down.at[:, :, MIDDLE], up),
    ]

    def send_piece(k):
        c, first, size = PIECES[k]
        later.append(
            copies.start(
                deposits.at[c, pl.ds(X - STRIP + first, size), MIDDLE],
                from_up.at[c, pl.ds(first, size), MIDDLE],
                down,
            )
        )

    for k in range(4):
        send_piece(k)
    own[0].wait()
    probe_sum.start_y()
    line_copies = [
        copies.start(lines, lines_lr.at[0], right),
        copies.start(lines, lines_lr.at[1], left),
    ]
    side = copies.start(deposits.at[:, :, pl.ds(T, H)], from_left, right)
    count = start_table(starts)
    for copy in own[1:]:
        copy.wait()
    square[...] = probe[0] * probe[0] + probe[1] * probe[1]

    def update(by, bx, ring=None):
        if by in (-1, 4):
            at, size, first = (0, RING, H - RING) if by == -1 else (RING + T, RING, 0)
        else:
            at, size, first = RING + by * H, H, 0
        inverse = 1.0 / block_weight(count, square, by, bx, (first, size))
        cols = pl.ds(H + bx * H, H)
        block = pl.ds(max(bx, 0) * H, H)
        for c in range(2):
            base = canvas[c, pl.ds(at, size), cols]
            if bx == -1:
                grad = jnp.broadcast_to(ring[:, c : c + 1], (H, H))
                base = jnp.broadcast_to(ring[:, 4 + c : 5 + c], (H, H))
            elif bx == 4:
                grad = jnp.broadcast_to(ring[:, 2 + c : 3 + c], (H, H))
                grad = grad + grads[c, pl.ds(by * H, H), block]
            elif by == -1:
                grad = from_up[c, 0:RING, block]
            else:
                grad = grads[c, pl.ds(by * H, size), block]
                if by == 0:
                    grad = grad + from_up[c, RING:STRIP, block]
                if by == 4:
                    grad = grad + from_down[c, :, block]
                if bx == 0:
                    grad = grad + from_left[c, pl.ds(by * H, size), :]
            canvas[c, pl.ds(at, size), cols] = base + grad * inverse

    def smooth(by):
        rate = rates(classes[pl.ds(by * H, H), :], weights)
        for c in range(2):
            around_sum, center = shifted_sum(canvas, c, RING + by * H, H, T)
            obj_out[c, pl.ds(by * H, H), :] = center + rate * (around_sum - 4.0 * center)

    for by in (1, 2, 3):
        for bx in (1, 2, 3):
            update(by, bx)
    probe_sum.start_rows()
    side.wait_recv()
    for copy in line_copies:
        copy.wait_recv()
    corner_down[...] = (
        grads[:, pl.ds(X - STRIP, STRIP), pl.ds(0, H)] + from_left[:, pl.ds(X - STRIP, STRIP), :]
    )
    corner_up[...] = grads[:, pl.ds(0, RING), pl.ds(0, H)] + from_left[:, pl.ds(0, RING), :]
    probe_sum.start_back()
    later += [
        copies.start(lines_lr, lines_up.at[pl.ds(0, 2)], down),
        copies.start(corner_down, from_up.at[:, :, pl.ds(0, H)], down),
        copies.start(corner_up, from_down.at[:, :, pl.ds(0, H)], up),
    ]
    for by in (1, 2, 3):
        update(by, 0)
    probe_sum.start_back_y()
    rows = [lines_lr[0, c : c + 1] for c in range(2)]
    rows += [lines_lr[1, 2 + c : 3 + c] for c in range(2)]
    rows += [lines_lr[0, 6 + c : 7 + c] for c in range(2)]
    ring = spread_lines(rows)
    for by in (1, 2, 3):
        for bx in (-1, 4):
            update(by, bx, ring[by * H : (by + 1) * H])
    blank_sides(canvas, H + T, RING + H, 3 * H)
    smooth(2)
    probe_sum.start_back_pair()
    for copy in later:
        copy.wait_recv()
    far = [rows[c][:, :H] + lines_up[0, c : c + 1, T:] for c in range(2)]
    far += [
        rows[2 + c][:, :H] + lines_up[1, 2 + c : 3 + c, T:] + lines_up[2, 4 + c : 5 + c, T:]
        for c in range(2)
    ]
    far += [rows[4 + c][:, :H] for c in range(2)]
    ring = spread_lines(far)
    for bx in range(4):
        update(0, bx)
    for bx in (-1, 4):
        update(0, bx, ring)
    for by in (-1, 4):
        for bx in range(4):
            update(by, bx)
    blank_outside(canvas, RING + T, H + T)
    for by in (0, 1, 3):
        smooth(by)
    probe_sum.end()
    unpack_probe(tiles, probe_out)
    copies.finish()


def exchange_last(deposits, sums, lines, obj, classes, probe, starts, weights):
    count = PROBE_COPIES + 13
    return pl.pallas_call(
        last_kernel,
        name="exchange_last",
        out_shape=[
            jax.ShapeDtypeStruct((2, T, T), F32),
            jax.ShapeDtypeStruct((2, S, S), F32),
        ],
        in_specs=[ANY] * 6 + [SMEM, SMEM],
        out_specs=[VMEM, VMEM],
        scratch_shapes=[
            pltpu.VMEM((2, T + 2 * RING, T + 2 * H), F32),
            pltpu.VMEM((2, X, X), F32),
            pltpu.VMEM((T, T), jnp.int32),
            pltpu.VMEM((2, S, S), F32),
            pltpu.VMEM((2, 32, 3, 8, H), F32),
            pltpu.VMEM((S, S), F32),
            pltpu.VMEM((2, STRIP, H), F32),
            pltpu.VMEM((2, RING, H), F32),
            pltpu.VMEM((2, 32, 2, 8, H), F32),
            pltpu.VMEM((2, X, H), F32),
            pltpu.VMEM((2, STRIP, T), F32),
            pltpu.VMEM((2, RING, T), F32),
            pltpu.VMEM((2, 8, X), F32),
            pltpu.VMEM((3, 8, X), F32),
        ]
        + PROBE_SCRATCH
        + [
            pltpu.SemaphoreType.DMA((5,)),
            pltpu.SemaphoreType.DMA((count,)),
            pltpu.SemaphoreType.DMA((count,)),
        ],
        compiler_params=pltpu.CompilerParams(
            collective_id=2, has_side_effects=True, vmem_limit_bytes=VMEM_BYTES
        ),
    )(deposits, sums, lines, obj, classes, probe, starts, weights)


def hand_over_kernel(obj, probe, obj_out, probe_out):
    obj_out[...] = obj[...]
    probe_out[...] = probe[...]


def hand_over(obj, probe):
    specs = [
        pl.BlockSpec((2, T // 4, T), lambda i: (0, i, 0)),
        pl.BlockSpec((2, S // 4, S), lambda i: (0, i, 0)),
    ]
    return pl.pallas_call(
        hand_over_kernel,
        name="hand_over",
        grid=(4,),
        out_shape=[
            jax.ShapeDtypeStruct((2, T, T), F32),
            jax.ShapeDtypeStruct((2, S, S), F32),
        ],
        in_specs=specs,
        out_specs=specs,
        compiler_params=pltpu.CompilerParams(vmem_limit_bytes=VMEM_BYTES),
    )(obj, probe)


def per_device(
    object_init, probe_init, amplitudes, scan_offsets, live_count, smooth_class, class_weight
):
    right, left = (jnp.asarray(table) for table in dft_blocks())
    slots = functools.partial(
        slots_pass,
        amps=amplitudes.reshape(8, S, S),
        offsets=scan_offsets.reshape(8, 2).T,
        live=live_count,
        right=right,
        left=left,
    )
    below, beside, starts = exchange_strips(
        object_init, scan_offsets.reshape(8, 2).T, live_count
    )
    deposits, sums, lines = slots((object_init, below, beside), probe_init)
    object_next, probe_next = exchange_middle(
        deposits, sums, lines, object_init, below, beside, smooth_class, probe_init,
        starts, class_weight,
    )
    deposits, sums, lines = slots((object_next,), probe_next)
    return tuple(
        hand_over(
            *exchange_last(
                deposits, sums, lines, object_next, smooth_class, probe_next, starts, class_weight
            )
        )
    )


def solution(mesh):
    in_specs = (
        P(None, "row", "col"),
        P(),
        P("row", "col", None, None, None),
        P("row", "col", None, None),
        P("row", "col"),
        P("row", "col"),
        P(),
    )
    out_specs = (P(None, "row", "col"), P())
    return jax.shard_map(
        per_device, mesh=mesh, in_specs=in_specs, out_specs=out_specs, check_vma=False
    )
```

```python
import math

import jax
import jax.numpy as jnp
import ml_dtypes
import numpy as np
from jax import lax
from jax.experimental import pallas as pl
from jax.experimental.pallas import tpu as pltpu
from jax.sharding import PartitionSpec as P

F32 = jnp.float32
BF16 = jnp.bfloat16
T = 512
S = 256
H = 128
X = T + H
RING = 8
STRIP = H + RING
MESH = pl.DeviceIdType.MESH
ANY = pl.BlockSpec(memory_space=pl.ANY)
VMEM = pl.BlockSpec(memory_space=pltpu.VMEM)
SMEM = pl.BlockSpec(memory_space=pltpu.SMEM)
VMEM_BYTES = 64 * 1024 * 1024


def dft_blocks():
    index = np.arange(S)
    phases = 2.0 * math.pi / S * (index[:, None] * index[None, :] % S)
    re = (np.cos(phases) / math.sqrt(S)).astype(ml_dtypes.bfloat16)
    im = (-np.sin(phases) / math.sqrt(S)).astype(ml_dtypes.bfloat16)
    right = np.block([[re, im], [-im, re]])
    left = np.block([[re, -im], [im, re]])
    return right, left


class Copies:
    def __init__(self, send_sems, recv_sems):
        self.send_sems, self.recv_sems, self.count = send_sems, recv_sems, 0
        self.started = []

    def make(self, src, dst, device):
        k = self.count
        self.count += 1
        return pltpu.make_async_remote_copy(
            src_ref=src,
            dst_ref=dst,
            send_sem=self.send_sems.at[k],
            recv_sem=self.recv_sems.at[k],
            device_id=device,
            device_id_type=MESH,
        )

    def start(self, src, dst, device):
        copy = self.make(src, dst, device)
        copy.start()
        self.started.append(copy)
        return copy

    def finish(self):
        for copy in self.started:
            copy.wait_send()
        self.started = []


def around():
    row, col = lax.axis_index("row"), lax.axis_index("col")
    up = (lax.rem(row + 15, 16), col)
    down = (lax.rem(row + 1, 16), col)
    left = (row, lax.rem(col + 7, 8))
    right = (row, lax.rem(col + 1, 8))
    return up, down, left, right


def greet(devices):
    barrier = pltpu.get_barrier_semaphore()
    for device in devices:
        pl.semaphore_signal(barrier, inc=1, device_id=device, device_id_type=MESH)
    pl.semaphore_wait(barrier, len(devices))


def count_starts(offsets, live, out):
    lane = lax.broadcasted_iota(jnp.int32, (8, H), 1)
    row0 = lax.axis_index("row") * T
    col0 = lax.axis_index("col") * T
    found = jnp.zeros((8, H), F32)
    for slot in range(8):
        at = lax.div(offsets[0, slot] - row0, H) * 4 + lax.div(offsets[1, slot] - col0, H)
        found += jnp.where((lane == at) & (live[0, 0] > slot), 1.0, 0.0)
    out[...] = found


def project(patch_re, patch_im, probe_re, probe_im, measured, right, left):
    exit_re = (probe_re * patch_re - probe_im * patch_im).astype(BF16)
    exit_im = (probe_re * patch_im + probe_im * patch_re).astype(BF16)
    half = jnp.dot(
        jnp.concatenate([exit_re, exit_im], 1), right, preferred_element_type=F32
    ).astype(BF16)
    far = jnp.dot(
        left, jnp.concatenate([half[:, :S], half[:, S:]], 0), preferred_element_type=F32
    )
    far_re, far_im = far[:S], far[S:]
    square = far_re * far_re + far_im * far_im
    factor = measured.astype(F32) * lax.rsqrt(jnp.maximum(square, 1.0)) - 1.0
    corr = jnp.concatenate([(far_re * factor).astype(BF16), (far_im * factor).astype(BF16)], 1)
    back = jnp.dot(corr, left, preferred_element_type=F32).astype(BF16)
    diff = jnp.dot(
        right, jnp.concatenate([back[:, :S], back[:, S:]], 0), preferred_element_type=F32
    )
    return diff[:S], diff[S:]


def visit_slots(canvas, probe, amps, offsets, live, right, left, terms, deposits, sums):
    row0 = lax.axis_index("row") * T
    col0 = lax.axis_index("col") * T
    sums[...] = jnp.zeros_like(sums)

    def start_block(slot):
        by = jnp.clip(lax.div(offsets[0, slot] - row0, H), 0, 3)
        bx = jnp.clip(lax.div(offsets[1, slot] - col0, H), 0, 3)
        return by, bx

    def place(slot):
        by, bx = start_block(slot)
        return pl.ds(by * H + RING, S), pl.ds(bx * H + H, S)

    def pair(step, carry):
        found = []
        for slot in (2 * step, 2 * step + 1):
            rows, cols = place(slot)
            probe_re, probe_im = probe[0], probe[1]
            patch_re, patch_im = canvas[0, rows, cols], canvas[1, rows, cols]
            found.append(
                project(
                    patch_re, patch_im, probe_re, probe_im, amps[slot], right[...], left[...]
                )
            )
        inner = pl.ds(H, S)
        grads = [0.0, 0.0, 0.0]
        for slot, (diff_re, diff_im) in zip((2 * step, 2 * step + 1), found):
            rows, cols = place(slot)
            mask = jnp.where(jnp.broadcast_to(live[0, 0], (1, S)) > slot, 1.0, 0.0)
            probe_re, probe_im = probe[0], probe[1]
            patch_re, patch_im = canvas[0, rows, cols], canvas[1, rows, cols]
            diff_re, diff_im = diff_re * mask, diff_im * mask
            terms[slot, 0, inner, inner] = probe_re * diff_re + probe_im * diff_im
            terms[slot, 1, inner, inner] = probe_re * diff_im - probe_im * diff_re
            grads[0] += patch_re * diff_re + patch_im * diff_im
            grads[1] += patch_re * diff_im - patch_im * diff_re
            grads[2] += (patch_re * patch_re + patch_im * patch_im) * mask
        for c in range(3):
            for ct in range(2):
                sums[ct, :, c] += grads[c][:, ct * H : (ct + 1) * H].reshape(32, 8, H)
        return carry

    lax.fori_loop(0, 4, pair, 0)

    starts_at = [start_block(slot) for slot in range(8)]

    def gather(block, carry):
        by, bx = block // 5, lax.rem(block, 5)
        total = [None, None]
        for slot in range(8):
            y = jnp.clip(by - starts_at[slot][0], -1, 2) * H + H
            x = jnp.clip(bx - starts_at[slot][1], -1, 2) * H + H
            rows, cols = pl.ds(y, H), pl.ds(x, H)
            for c in range(2):
                part = terms[slot, c, rows, cols]
                total[c] = part if slot == 0 else total[c] + part
        for c in range(2):
            deposits[
                c, pl.ds(pl.multiple_of(by * H, H), H), pl.ds(pl.multiple_of(bx * H, H), H)
            ] = total[c]
        return carry

    lax.fori_loop(0, 25, gather, 0)


def frame_terms(terms):
    for slot in range(8):
        terms[slot, :, 0:H, :] = jnp.zeros((2, H, 2 * S), F32)
        terms[slot, :, S + H :, :] = jnp.zeros((2, H, 2 * S), F32)
        terms[slot, :, H : S + H, 0:H] = jnp.zeros((2, S, H), F32)
        terms[slot, :, H : S + H, S + H :] = jnp.zeros((2, S, H), F32)


def columns_as_rows(columns, out):
    lane = lax.broadcasted_iota(jnp.int32, (X, H), 1)
    gathered = jnp.zeros((X, H), F32)
    for k, column in enumerate(columns):
        gathered = jnp.where(lane == k, column, gathered)
    out[...] = gathered.T[:8]


class ProbeSum:
    def __init__(self, copies, sums, probe, out, pair_in, part, y_in, y_part, rows_in):
        self.row, col = lax.axis_index("row"), lax.axis_index("col")
        self.y, self.core = col // 2, lax.rem(col, 2)
        self.tile = lax.rem(self.row, 8)
        self.copies, self.sums, self.probe, self.out = copies, sums, probe, out
        self.pair_in, self.part, self.y_in, self.y_part = pair_in, part, y_in, y_part
        self.rows_in = rows_in
        self.col = col
        self.other = (self.row, self.y * 2 + 1 - self.core)
        self.y_peers = [
            (self.row, lax.rem(self.y + k, 4) * 2 + self.core) for k in range(1, 4)
        ]
        self.row_peers = [(lax.rem(self.row + k, 16), col) for k in range(1, 16)]

    def peers(self):
        return self.y_peers + self.row_peers

    def start_pair(self):
        self.pair = self.copies.start(self.sums.at[1 - self.core], self.pair_in, self.other)

    def start_y(self):
        self.pair.wait_recv()
        self.part[...] = self.sums[self.core] + self.pair_in[...]
        self.y_sent = []
        for k in range(1, 4):
            at = lax.rem(self.y + k, 4) * 8
            self.y_sent.append(
                self.copies.start(
                    self.part.at[pl.ds(at, 8)], self.y_in.at[k - 1], self.y_peers[k - 1]
                )
            )

    def start_rows(self):
        for copy in self.y_sent:
            copy.wait_recv()
        self.y_part[...] = (
            self.part[pl.ds(self.y * 8, 8)] + self.y_in[0] + self.y_in[1] + self.y_in[2]
        )
        self.rows_in[self.row] = self.y_part[self.tile]
        for k in range(1, 16):
            tile = lax.rem(self.row + k, 8)
            self.copies.start(
                self.y_part.at[tile], self.rows_in.at[self.row], self.row_peers[k - 1]
            )
        self.first = self.copies.count - 15

    def landed(self, ref, number):
        pltpu.make_async_remote_copy(
            src_ref=ref,
            dst_ref=ref,
            send_sem=self.copies.send_sems.at[number],
            recv_sem=self.copies.recv_sems.at[number],
            device_id=self.other,
            device_id_type=MESH,
        ).wait_recv()

    def start_back(self):
        for k in range(1, 16):
            self.landed(self.rows_in.at[lax.rem(self.row + 16 - k, 16)], self.first + k - 1)
        total = self.rows_in[0]
        for k in range(1, 16):
            total = total + self.rows_in[k]
        rt = self.y * 8 + self.tile
        rows, cols = pl.ds(pl.multiple_of(rt * 8, 8), 8), pl.ds(pl.multiple_of(self.core * H, H), H)
        inverse = 1.0 / (total[2] + 1.0)
        for c in range(2):
            self.out[self.core, rt, c] = self.probe[c, rows, cols] + total[c] * inverse
        mine = self.out.at[self.core, rt]
        group = self.row // 8 * 8
        self.first = self.copies.count
        for k in range(1, 8):
            self.copies.start(mine, mine, (group + lax.rem(self.tile + k, 8), self.col))

    def start_back_y(self):
        for k in range(1, 8):
            tile = lax.rem(self.tile + 8 - k, 8)
            self.landed(self.out.at[self.core, self.y * 8 + tile], self.first + k - 1)
        mine = self.out.at[self.core, pl.ds(self.y * 8, 8)]
        self.first = self.copies.count
        for k in range(1, 4):
            self.copies.start(mine, mine, self.y_peers[k - 1])

    def start_back_pair(self):
        for k in range(1, 4):
            at = lax.rem(self.y + 4 - k, 4) * 8
            self.landed(self.out.at[self.core, pl.ds(at, 8)], self.first + k - 1)
        mine = self.out.at[self.core]
        self.first = self.copies.count
        self.copies.start(mine, mine, self.other)

    def end(self):
        self.landed(self.out.at[1 - self.core], self.first)


PROBE_COPIES = 1 + 3 + 15 + 7 + 3 + 1


def start_table(starts):
    def count(by, bx):
        return starts[by // 4 + 1, bx // 4 + 1, 0, by % 4 * 4 + bx % 4]

    return count


def block_weight(count, square, by, bx, rows):
    first, size = rows
    total = 1.0
    for qy in range(2):
        for qx in range(2):
            total = total + count(by - qy, bx - qx) * square[
                pl.ds(qy * H + first, size), pl.ds(qx * H, H)
            ]
    return total


def spread_lines(rows):
    length = rows[0].shape[1]
    packed = jnp.concatenate(rows + [jnp.zeros((H - len(rows), length), F32)], 0)
    return packed.T


def shifted_sum(canvas, c, first, rows, cols):
    width = cols + 2 * H
    whole = canvas[c, pl.ds(first, rows), pl.ds(0, width)]
    left = pltpu.roll(whole, 1, 1)[:, H : H + cols]
    right = pltpu.roll(whole, width - 1, 1)[:, H : H + cols]
    above = canvas[c, pl.ds(first - 1, rows), pl.ds(H, cols)]
    below = canvas[c, pl.ds(first + 1, rows), pl.ds(H, cols)]
    return below + above + right + left, whole[:, H : H + cols]


def rates(classes, weights):
    value = jnp.full(classes.shape, weights[0], F32)
    for k in range(1, 4):
        value = jnp.where(classes == k, weights[k], value)
    return value


def blank_sides(canvas, cols_end, first, size):
    col = lax.axis_index("col")
    width = canvas.shape[2]

    @pl.when(col == 0)
    def _():
        canvas[:, pl.ds(first, size), 0:H] = jnp.zeros((2, size, H), F32)

    @pl.when(col == 7)
    def _():
        canvas[:, pl.ds(first, size), cols_end:] = jnp.zeros((2, size, width - cols_end), F32)


def blank_outside(canvas, rows_end, cols_end):
    row = lax.axis_index("row")
    _, height, width = canvas.shape

    @pl.when(row == 0)
    def _():
        canvas[:, 0:RING, :] = jnp.zeros((2, RING, width), F32)

    @pl.when(row == 15)
    def _():
        canvas[:, rows_end:, :] = jnp.zeros((2, height - rows_end, width), F32)

    blank_sides(canvas, cols_end, 0, height)


MIDDLE = pl.ds(H, T - H)
LINES = [(0, 0), (0, 1), (1, 2), (1, 3), (0, 4), (0, 5), (1, 6), (1, 7)]
PIECES = [(c, first, size) for c in range(2) for first, size in ((0, 72), (72, 64))]


def unpack_probe(tiles, out):
    for c in range(2):
        for ct in range(2):
            out[c, :, ct * H : (ct + 1) * H] = tiles[ct, :, c].reshape(S, H)


def middle_phase(
    copies, probe_sum, grads, lines, classes, class_down, class_right, probe, starts, weights,
    canvas, canvas_next, probe_next, square, corners, tiles,
    from_left, from_right, from_up, from_down, lines_lr, lines_up, lines_down,
):
    up, down, left, right = around()
    probe_sum.start_pair()
    later = [
        copies.start(lines, lines_up.at[2], down),
        copies.start(lines, lines_down.at[2], up),
    ]

    def send_piece(k):
        c, first, size = PIECES[k]
        later.append(
            copies.start(
                grads.at[c, pl.ds(X - STRIP + first, size), MIDDLE],
                from_up.at[c, pl.ds(first, size), MIDDLE],
                down,
            )
        )
        later.append(
            copies.start(
                grads.at[c, pl.ds(first, size), MIDDLE],
                from_down.at[c, pl.ds(first, size), MIDDLE],
                up,
            )
        )

    for k in range(4):
        send_piece(k)
    probe_sum.start_y()
    side = [
        copies.start(lines, lines_lr.at[0], right),
        copies.start(lines, lines_lr.at[1], left),
        copies.start(grads.at[:, :, pl.ds(T, H)], from_left, right),
        copies.start(grads.at[:, :, pl.ds(0, H)], from_right, left),
    ]
    count = start_table(starts)
    square[...] = probe[0] * probe[0] + probe[1] * probe[1]

    def update(by, bx, ring=None):
        if by in (-1, 5):
            at, size, first = (0, RING, H - RING) if by == -1 else (RING + X, RING, 0)
        else:
            at, size, first = RING + by * H, H, 0
        edge = bx in (-1, 5)
        inverse = 1.0 / block_weight(count, square, by, bx, (first, size))
        cols = pl.ds(H + bx * H, H)
        for c in range(2):
            if edge:
                k = 0 if bx == -1 else 2
                grad = jnp.broadcast_to(ring[:, k + c : k + c + 1], (H, H))
                base = jnp.broadcast_to(ring[:, k + 4 + c : k + 5 + c], (H, H))
            else:
                base = canvas[c, pl.ds(at, size), cols]
                block = pl.ds(bx * H, H)
                if by == -1:
                    grad = from_up[c, 0:RING, block]
                elif by == 5:
                    grad = from_down[c, H:STRIP, block]
                else:
                    grad = grads[c, pl.ds(by * H, H), block]
                    if by == 0:
                        grad = grad + from_up[c, RING:STRIP, block]
                    if by == 4:
                        grad = grad + from_down[c, 0:H, block]
                    if bx == 0:
                        grad = grad + from_left[c, pl.ds(by * H, H), :]
                    if bx == 4:
                        grad = grad + from_right[c, pl.ds(by * H, H), :]
            canvas[c, pl.ds(at, size), cols] = base + grad * inverse

    def smooth(by):
        if by < 4:
            levels = jnp.concatenate(
                [classes[pl.ds(by * H, H), :], class_right[pl.ds(by * H, H), :]], 1
            )
        else:
            levels = class_down[...]
        rate = rates(levels, weights)
        for c in range(2):
            around_sum, center = shifted_sum(canvas, c, RING + by * H, H, X)
            canvas_next[c, pl.ds(RING + by * H, H), pl.ds(H, X)] = center + rate * (around_sum - 4.0 * center)

    for by in (1, 2, 3):
        for bx in (1, 2, 3):
            update(by, bx)
    probe_sum.start_rows()
    for copy in side:
        copy.wait_recv()
    for k, (first, source) in enumerate(
        ((0, from_left), (0, from_right), (X - STRIP, from_left), (X - STRIP, from_right))
    ):
        column = 0 if k % 2 == 0 else T
        corners[k] = (
            grads[:, pl.ds(first, STRIP), pl.ds(column, H)]
            + source[:, pl.ds(first, STRIP), :]
        )
    probe_sum.start_back()
    later += [
        copies.start(lines_lr, lines_up.at[pl.ds(0, 2)], down),
        copies.start(lines_lr, lines_down.at[pl.ds(0, 2)], up),
        copies.start(corners.at[0], from_down.at[:, :, pl.ds(0, H)], up),
        copies.start(corners.at[2], from_up.at[:, :, pl.ds(0, H)], down),
        copies.start(corners.at[1], from_down.at[:, :, pl.ds(T, H)], up),
        copies.start(corners.at[3], from_up.at[:, :, pl.ds(T, H)], down),
    ]
    for by in (1, 2, 3):
        update(by, 0)
        update(by, 4)
    probe_sum.start_back_y()
    rows = [lines_lr[side_at, k : k + 1] for side_at, k in LINES]
    ring = spread_lines(rows)
    for by in (1, 2, 3):
        for bx in (-1, 5):
            update(by, bx, ring[by * H : (by + 1) * H])
    blank_sides(canvas, H + T, RING + H, 3 * H)
    smooth(2)
    probe_sum.start_back_pair()
    for copy in later:
        copy.wait_recv()
    far = []
    for n, (side_at, k) in enumerate(LINES):
        above = lines_up[side_at, k : k + 1, T:]
        below_it = lines_down[side_at, k : k + 1, :H]
        if n < 4:
            pieces = [rows[n][:, :H] + above, rows[n][:, T:] + below_it]
        else:
            pieces = [rows[n][:, :H], below_it]
        far.append(jnp.concatenate(pieces, 1))
    ring = spread_lines(far)
    for by in (0, 4):
        for bx in range(5):
            update(by, bx)
        for bx in (-1, 5):
            update(by, bx, ring[:H] if by == 0 else ring[H:])
    for by in (-1, 5):
        for bx in range(5):
            update(by, bx)
    blank_outside(canvas, RING + T, H + T)
    for by in (0, 1, 3, 4):
        smooth(by)
    probe_sum.end()
    unpack_probe(tiles, probe_next)
    copies.finish()


def last_phase(
    copies, probe_sum, grads, lines, classes, probe, starts, weights,
    canvas, ring_out, ring_up, obj_out, probe_out, square, corner_down, corner_up, tiles,
    from_left, from_up, from_down, lines_lr, lines_up,
):
    up, down, left, right = around()
    ring_out[...] = canvas[:, pl.ds(T, RING), pl.ds(H, T)]
    probe_sum.start_pair()
    later = [
        copies.start(lines, lines_up.at[2], down),
        copies.start(ring_out, ring_up, down),
        copies.start(grads.at[:, pl.ds(0, RING), MIDDLE], from_down.at[:, :, MIDDLE], up),
    ]

    def send_piece(k):
        c, first, size = PIECES[k]
        later.append(
            copies.start(
                grads.at[c, pl.ds(X - STRIP + first, size), MIDDLE],
                from_up.at[c, pl.ds(first, size), MIDDLE],
                down,
            )
        )

    for k in range(4):
        send_piece(k)
    probe_sum.start_y()
    line_copies = [
        copies.start(lines, lines_lr.at[0], right),
        copies.start(lines, lines_lr.at[1], left),
    ]
    side = copies.start(grads.at[:, :, pl.ds(T, H)], from_left, right)
    count = start_table(starts)
    square[...] = probe[0] * probe[0] + probe[1] * probe[1]

    def update(by, bx, ring=None):
        if by in (-1, 4):
            at, size, first = (0, RING, H - RING) if by == -1 else (RING + T, RING, 0)
        else:
            at, size, first = RING + by * H, H, 0
        inverse = 1.0 / block_weight(count, square, by, bx, (first, size))
        cols = pl.ds(H + bx * H, H)
        block = pl.ds(max(bx, 0) * H, H)
        for c in range(2):
            base = canvas[c, pl.ds(at, size), cols]
            if bx == -1:
                grad = jnp.broadcast_to(ring[:, c : c + 1], (H, H))
                base = jnp.broadcast_to(ring[:, 4 + c : 5 + c], (H, H))
            elif bx == 4:
                grad = jnp.broadcast_to(ring[:, 2 + c : 3 + c], (H, H))
                grad = grad + grads[c, pl.ds(by * H, H), block]
            elif by == -1:
                base = ring_up[c, :, block]
                grad = from_up[c, 0:RING, block]
            else:
                grad = grads[c, pl.ds(by * H, size), block]
                if by == 0:
                    grad = grad + from_up[c, RING:STRIP, block]
                if by == 4:
                    grad = grad + from_down[c, :, block]
                if bx == 0:
                    grad = grad + from_left[c, pl.ds(by * H, size), :]
            canvas[c, pl.ds(at, size), cols] = base + grad * inverse

    def smooth(by):
        rate = rates(classes[pl.ds(by * H, H), :], weights)
        for c in range(2):
            around_sum, center = shifted_sum(canvas, c, RING + by * H, H, T)
            obj_out[c, pl.ds(by * H, H), :] = center + rate * (around_sum - 4.0 * center)

    for by in (1, 2, 3):
        for bx in (1, 2, 3):
            update(by, bx)
    probe_sum.start_rows()
    side.wait_recv()
    for copy in line_copies:
        copy.wait_recv()
    corner_down[...] = (
        grads[:, pl.ds(X - STRIP, STRIP), pl.ds(0, H)] + from_left[:, pl.ds(X - STRIP, STRIP), :]
    )
    corner_up[...] = grads[:, pl.ds(0, RING), pl.ds(0, H)] + from_left[:, pl.ds(0, RING), :]
    probe_sum.start_back()
    later += [
        copies.start(lines_lr, lines_up.at[pl.ds(0, 2)], down),
        copies.start(corner_down, from_up.at[:, :, pl.ds(0, H)], down),
        copies.start(corner_up, from_down.at[:, :, pl.ds(0, H)], up),
    ]
    for by in (1, 2, 3):
        update(by, 0)
    probe_sum.start_back_y()
    rows = [lines_lr[0, c : c + 1] for c in range(2)]
    rows += [lines_lr[1, 2 + c : 3 + c] for c in range(2)]
    rows += [lines_lr[0, 6 + c : 7 + c] for c in range(2)]
    ring = spread_lines(rows)
    for by in (1, 2, 3):
        for bx in (-1, 4):
            update(by, bx, ring[by * H : (by + 1) * H])
    blank_sides(canvas, H + T, RING + H, 3 * H)
    smooth(2)
    probe_sum.start_back_pair()
    for copy in later:
        copy.wait_recv()
    far = [rows[c][:, :H] + lines_up[0, c : c + 1, T:] for c in range(2)]
    far += [
        rows[2 + c][:, :H] + lines_up[1, 2 + c : 3 + c, T:] + lines_up[2, 4 + c : 5 + c, T:]
        for c in range(2)
    ]
    far += [rows[4 + c][:, :H] for c in range(2)]
    ring = spread_lines(far)
    for bx in range(4):
        update(0, bx)
    for bx in (-1, 4):
        update(0, bx, ring)
    for by in (-1, 4):
        for bx in range(4):
            update(by, bx)
    blank_outside(canvas, RING + T, H + T)
    for by in (0, 1, 3):
        smooth(by)
    probe_sum.end()
    unpack_probe(tiles, probe_out)
    copies.finish()


def whole_kernel(
    obj, probe_in, amps_in, offsets, live, classes_in, weights, right_table, left_table,
    obj_out, probe_out,
    canvas, canvas_next, terms, grads, sums, probe, probe_next, amps, classes, class_down,
    class_right, square, counted, starts_in, starts, lines, ring_out, ring_up, corners, corner_down,
    corner_up, tiles, tiles_last, part, y_part, *refs
):
    landing, landing_last, (sems, send_sems, recv_sems) = refs[:10], refs[10:18], refs[18:]
    up, down, left, right = around()
    row, col = lax.axis_index("row"), lax.axis_index("col")
    copies = Copies(send_sems, recv_sems)
    probe_sum = ProbeSum(
        copies, sums, probe, tiles, landing[7], part, landing[8], y_part, landing[9]
    )
    probe_sum_last = ProbeSum(
        copies, sums, probe_next, tiles_last, landing_last[5], part, landing_last[6], y_part,
        landing_last[7],
    )
    near = {
        (dr, dc): (lax.rem(row + dr + 16, 16), lax.rem(col + dc + 8, 8))
        for dr in (-1, 0, 1)
        for dc in (-1, 0, 1)
        if (dr, dc) != (0, 0)
    }
    pairs = [
        (obj, canvas.at[:, pl.ds(RING, T), pl.ds(H, T)]),
        (probe_in, probe),
        (amps_in, amps),
        (classes_in, classes),
    ]
    own = [pltpu.make_async_copy(src, dst, sems.at[k]) for k, (src, dst) in enumerate(pairs)]
    for copy in own:
        copy.start()
    count_starts(offsets, live, counted)
    greet([device for (dr, dc), device in near.items() if dc != 0] + probe_sum.peers())
    rows = copies.start(
        obj.at[:, pl.ds(0, STRIP), :], canvas.at[:, pl.ds(RING + T, STRIP), pl.ds(H, T)], up
    )
    beside = copies.start(
        obj.at[:, :, pl.ds(0, H)], canvas.at[:, pl.ds(RING, T), pl.ds(H + T, H)], left
    )
    class_beside = copies.start(classes_in.at[:, pl.ds(0, H)], class_right, left)
    strips = [
        rows,
        copies.start(
            obj.at[:, pl.ds(T - RING, RING), :], canvas.at[:, pl.ds(0, RING), pl.ds(H, T)], down
        ),
    ]
    small = [
        copies.start(counted, starts_in.at[1 - dr, 1 - dc], device)
        for (dr, dc), device in near.items()
    ]
    starts_in[1, 1] = counted[...]
    frame_terms(terms)
    beside.wait_recv()
    corner = [
        copies.start(
            canvas.at[:, pl.ds(RING, STRIP), pl.ds(H + T, H)],
            canvas.at[:, pl.ds(RING + T, STRIP), pl.ds(H + T, H)],
            up,
        ),
        copies.start(
            canvas.at[:, pl.ds(T, RING), pl.ds(H + T, H)],
            canvas.at[:, pl.ds(0, RING), pl.ds(H + T, H)],
            down,
        ),
    ]
    class_beside.wait_recv()
    class_later = [
        copies.start(classes_in.at[pl.ds(0, H), :], class_down.at[:, pl.ds(0, T)], up),
        copies.start(class_right.at[pl.ds(0, H), :], class_down.at[:, pl.ds(T, H)], up),
    ]
    for copy in own:
        copy.wait()
    for copy in small:
        copy.wait_recv()
    to_scalars = pltpu.make_async_copy(starts_in, starts, sems.at[4])
    to_scalars.start()
    for copy in strips + corner:
        copy.wait_recv()
    to_scalars.wait()
    visit_slots(
        canvas, probe, amps, offsets, live, right_table, left_table, terms, grads, sums
    )
    inside = pl.ds(RING, X)
    columns_as_rows(
        [grads[c, :, T - 1 : T] for c in range(2)]
        + [grads[c, :, H : H + 1] for c in range(2)]
        + [canvas[c, inside, H + T - 1 : H + T] for c in range(2)]
        + [canvas[c, inside, H + H : H + H + 1] for c in range(2)],
        lines,
    )
    for copy in class_later:
        copy.wait_recv()
    copies.finish()
    middle_phase(
        copies, probe_sum, grads, lines, classes, class_down, class_right, probe, starts,
        weights, canvas, canvas_next, probe_next, square, corners, tiles, *landing[:7],
    )
    visit_slots(
        canvas_next, probe_next, amps, offsets, live, right_table, left_table, terms, grads, sums
    )
    columns_as_rows(
        [grads[c, :, T - 1 : T] for c in range(2)]
        + [grads[c, :, 0:1] for c in range(2)]
        + [grads[c, :, T : T + 1] for c in range(2)]
        + [canvas_next[c, inside, H + T - 1 : H + T] for c in range(2)],
        lines,
    )
    last_phase(
        copies, probe_sum_last, grads, lines, classes, probe_next, starts, weights,
        canvas_next, ring_out, ring_up, obj_out, probe_out, square, corner_down, corner_up, tiles_last,
        *landing_last[:5],
    )
    assert copies.count == send_sems.shape[0]


PROBE_LANDING = [
    pltpu.VMEM((32, 3, 8, H), F32),
    pltpu.VMEM((3, 8, 3, 8, H), F32),
    pltpu.VMEM((16, 3, 8, H), F32),
]
COPIES = 16 + 2 * PROBE_COPIES + 20 + 13


def whole(obj, probe, amps, offsets, live, classes, weights, right, left):
    wide = (2, X + 2 * RING, X + 2 * H)
    scratch = [
        pltpu.VMEM(wide, F32),
        pltpu.VMEM(wide, F32),
        pltpu.VMEM((8, 2, 2 * S, 2 * S), F32),
        pltpu.VMEM((2, X, X), F32),
        pltpu.VMEM((2, 32, 3, 8, H), F32),
        pltpu.VMEM((2, S, S), F32),
        pltpu.VMEM((2, S, S), F32),
        pltpu.VMEM((8, S, S), BF16),
        pltpu.VMEM((T, T), jnp.int32),
        pltpu.VMEM((H, X), jnp.int32),
        pltpu.VMEM((T, H), jnp.int32),
        pltpu.VMEM((S, S), F32),
        pltpu.VMEM((8, H), F32),
        pltpu.VMEM((3, 3, 8, H), F32),
        pltpu.SMEM((3, 3, 8, H), F32),
        pltpu.VMEM((8, X), F32),
        pltpu.VMEM((2, RING, T), F32),
        pltpu.VMEM((2, RING, T), F32),
        pltpu.VMEM((4, 2, STRIP, H), F32),
        pltpu.VMEM((2, STRIP, H), F32),
        pltpu.VMEM((2, RING, H), F32),
        pltpu.VMEM((2, 32, 2, 8, H), F32),
        pltpu.VMEM((2, 32, 2, 8, H), F32),
        pltpu.VMEM((32, 3, 8, H), F32),
        pltpu.VMEM((8, 3, 8, H), F32),
    ]
    landing = [
        pltpu.VMEM((2, X, H), F32),
        pltpu.VMEM((2, X, H), F32),
        pltpu.VMEM((2, STRIP, X), F32),
        pltpu.VMEM((2, STRIP, X), F32),
        pltpu.VMEM((2, 8, X), F32),
        pltpu.VMEM((3, 8, X), F32),
        pltpu.VMEM((3, 8, X), F32),
    ] + PROBE_LANDING
    landing_last = [
        pltpu.VMEM((2, X, H), F32),
        pltpu.VMEM((2, STRIP, T), F32),
        pltpu.VMEM((2, RING, T), F32),
        pltpu.VMEM((2, 8, X), F32),
        pltpu.VMEM((3, 8, X), F32),
    ] + PROBE_LANDING
    return pl.pallas_call(
        whole_kernel,
        name="reconstruct",
        out_shape=[
            jax.ShapeDtypeStruct((2, T, T), F32),
            jax.ShapeDtypeStruct((2, S, S), F32),
        ],
        in_specs=[ANY, ANY, ANY, SMEM, SMEM, ANY, SMEM, VMEM, VMEM],
        out_specs=[VMEM, VMEM],
        scratch_shapes=scratch
        + landing
        + landing_last
        + [
            pltpu.SemaphoreType.DMA((5,)),
            pltpu.SemaphoreType.DMA((COPIES,)),
            pltpu.SemaphoreType.DMA((COPIES,)),
        ],
        compiler_params=pltpu.CompilerParams(
            collective_id=0, has_side_effects=True, vmem_limit_bytes=VMEM_BYTES
        ),
    )(obj, probe, amps, offsets, live, classes, weights, right, left)


def hand_over_kernel(obj, probe, obj_out, probe_out):
    obj_out[...] = obj[...]
    probe_out[...] = probe[...]


def hand_over(obj, probe):
    specs = [
        pl.BlockSpec((2, T // 4, T), lambda i: (0, i, 0)),
        pl.BlockSpec((2, S // 4, S), lambda i: (0, i, 0)),
    ]
    return pl.pallas_call(
        hand_over_kernel,
        name="hand_over",
        grid=(4,),
        out_shape=[
            jax.ShapeDtypeStruct((2, T, T), F32),
            jax.ShapeDtypeStruct((2, S, S), F32),
        ],
        in_specs=specs,
        out_specs=specs,
        compiler_params=pltpu.CompilerParams(vmem_limit_bytes=VMEM_BYTES),
    )(obj, probe)


def per_device(
    object_init, probe_init, amplitudes, scan_offsets, live_count, smooth_class, class_weight
):
    right, left = (jnp.asarray(table) for table in dft_blocks())
    return tuple(
        hand_over(
            *whole(
                object_init,
                probe_init,
                amplitudes.reshape(8, S, S),
                scan_offsets.reshape(8, 2).T,
                live_count,
                smooth_class,
                class_weight,
                right,
                left,
            )
        )
    )


def solution(mesh):
    in_specs = (
        P(None, "row", "col"),
        P(),
        P("row", "col", None, None, None),
        P("row", "col", None, None),
        P("row", "col"),
        P("row", "col"),
        P(),
    )
    out_specs = (P(None, "row", "col"), P())
    return jax.shard_map(
        per_device, mesh=mesh, in_specs=in_specs, out_specs=out_specs, check_vma=False
    )
```

```python
import math

import jax
import jax.numpy as jnp
import ml_dtypes
import numpy as np
from jax import lax
from jax.experimental import pallas as pl
from jax.experimental.pallas import tpu as pltpu
from jax.sharding import PartitionSpec as P

F32 = jnp.float32
BF16 = jnp.bfloat16
T = 512
S = 256
H = 128
X = T + H
RING = 8
STRIP = H + RING
MESH = pl.DeviceIdType.MESH
ANY = pl.BlockSpec(memory_space=pl.ANY)
VMEM = pl.BlockSpec(memory_space=pltpu.VMEM)
SMEM = pl.BlockSpec(memory_space=pltpu.SMEM)
VMEM_BYTES = 64 * 1024 * 1024


def dft_blocks():
    index = np.arange(S)
    phases = 2.0 * math.pi / S * (index[:, None] * index[None, :] % S)
    re = (np.cos(phases) / math.sqrt(S)).astype(ml_dtypes.bfloat16)
    im = (-np.sin(phases) / math.sqrt(S)).astype(ml_dtypes.bfloat16)
    right = np.block([[re, im], [-im, re]])
    left = np.block([[re, -im], [im, re]])
    return right, left


class Copies:
    def __init__(self, send_sems, recv_sems):
        self.send_sems, self.recv_sems, self.count = send_sems, recv_sems, 0
        self.started = []

    def make(self, src, dst, device):
        k = self.count
        self.count += 1
        return pltpu.make_async_remote_copy(
            src_ref=src,
            dst_ref=dst,
            send_sem=self.send_sems.at[k],
            recv_sem=self.recv_sems.at[k],
            device_id=device,
            device_id_type=MESH,
        )

    def start(self, src, dst, device):
        copy = self.make(src, dst, device)
        copy.start()
        self.started.append(copy)
        return copy

    def finish(self):
        for copy in self.started:
            copy.wait_send()
        self.started = []


def around():
    row, col = lax.axis_index("row"), lax.axis_index("col")
    up = (lax.rem(row + 15, 16), col)
    down = (lax.rem(row + 1, 16), col)
    left = (row, lax.rem(col + 7, 8))
    right = (row, lax.rem(col + 1, 8))
    return up, down, left, right


def greet(devices):
    barrier = pltpu.get_barrier_semaphore()
    for device in devices:
        pl.semaphore_signal(barrier, inc=1, device_id=device, device_id_type=MESH)
    pl.semaphore_wait(barrier, len(devices))


def count_starts(offsets, live, out):
    lane = lax.broadcasted_iota(jnp.int32, (8, H), 1)
    row0 = lax.axis_index("row") * T
    col0 = lax.axis_index("col") * T
    found = jnp.zeros((8, H), F32)
    for slot in range(8):
        at = lax.div(offsets[0, slot] - row0, H) * 4 + lax.div(offsets[1, slot] - col0, H)
        found += jnp.where((lane == at) & (live[0, 0] > slot), 1.0, 0.0)
    out[...] = found


def dot(a, b):
    return jnp.dot(a, b, preferred_element_type=F32)


def side_by_side(re, im):
    return jnp.concatenate([re.astype(BF16), im.astype(BF16)], 1)


def stacked(both):
    both = both.astype(BF16)
    return jnp.concatenate([both[:, :S], both[:, S:]], 0)


def start_block(offsets, slot):
    by = lax.div(offsets[0, slot] - lax.axis_index("row") * T, H)
    bx = lax.div(offsets[1, slot] - lax.axis_index("col") * T, H)
    return jnp.clip(by, 0, 3), jnp.clip(bx, 0, 3)


def visit_slots(canvas, probe, amps, offsets, live, right, left, terms, sums):
    sums[...] = jnp.zeros_like(sums)

    def some(step, carry):
        slots = [4 * step + k for k in range(4)]
        places = []
        for slot in slots:
            by, bx = start_block(offsets, slot)
            places.append((pl.ds(by * H + RING, S), pl.ds(bx * H + H, S)))

        def leaving(rows, cols):
            probe_re, probe_im = probe[0], probe[1]
            patch_re, patch_im = canvas[0, rows, cols], canvas[1, rows, cols]
            return side_by_side(
                probe_re * patch_re - probe_im * patch_im,
                probe_re * patch_im + probe_im * patch_re,
            )

        def corrected(slot, far):
            far_re, far_im = far[:S], far[S:]
            square = far_re * far_re + far_im * far_im
            factor = amps[slot].astype(F32) * lax.rsqrt(jnp.maximum(square, 1.0)) - 1.0
            return side_by_side(far_re * factor, far_im * factor)

        waves = [leaving(rows, cols) for rows, cols in places]
        waves = [stacked(dot(wave, right[...])) for wave in waves]
        waves = [dot(left[...], wave) for wave in waves]
        waves = [corrected(slot, wave) for slot, wave in zip(slots, waves)]
        waves = [stacked(dot(wave, left[...])) for wave in waves]
        waves = [dot(right[...], wave) for wave in waves]
        inner = pl.ds(H, S)
        grads = [0.0, 0.0, 0.0]
        for slot, (rows, cols), diff in zip(slots, places, waves):
            mask = jnp.where(jnp.broadcast_to(live[0, 0], (1, S)) > slot, 1.0, 0.0)
            probe_re, probe_im = probe[0], probe[1]
            patch_re, patch_im = canvas[0, rows, cols], canvas[1, rows, cols]
            diff_re, diff_im = diff[:S] * mask, diff[S:] * mask
            terms[slot, 0, inner, inner] = probe_re * diff_re + probe_im * diff_im
            terms[slot, 1, inner, inner] = probe_re * diff_im - probe_im * diff_re
            grads[0] += patch_re * diff_re + patch_im * diff_im
            grads[1] += patch_re * diff_im - patch_im * diff_re
            grads[2] += (patch_re * patch_re + patch_im * patch_im) * mask
        for c in range(3):
            for ct in range(2):
                sums[ct, :, c] += grads[c][:, ct * H : (ct + 1) * H].reshape(32, 8, H)
        return carry

    lax.fori_loop(0, 2, some, 0)


def gather(offsets, terms, deposits, first, step, count):
    starts_at = [start_block(offsets, slot) for slot in range(8)]

    def one(block, carry):
        by, bx = first + lax.div(block, 5) * step, lax.rem(block, 5)
        total = [None, None]
        for slot in range(8):
            y = jnp.clip(by - starts_at[slot][0], -1, 2) * H + H
            x = jnp.clip(bx - starts_at[slot][1], -1, 2) * H + H
            for c in range(2):
                part = terms[slot, c, pl.ds(y, H), pl.ds(x, H)]
                total[c] = part if slot == 0 else total[c] + part
        for c in range(2):
            deposits[
                c, pl.ds(pl.multiple_of(by * H, H), H), pl.ds(pl.multiple_of(bx * H, H), H)
            ] = total[c]
        return carry

    lax.fori_loop(0, 5 * count, one, 0)


def frame_terms(terms):
    for slot in range(8):
        terms[slot, :, 0:H, :] = jnp.zeros((2, H, 2 * S), F32)
        terms[slot, :, S + H :, :] = jnp.zeros((2, H, 2 * S), F32)
        terms[slot, :, H : S + H, 0:H] = jnp.zeros((2, S, H), F32)
        terms[slot, :, H : S + H, S + H :] = jnp.zeros((2, S, H), F32)


def columns_as_rows(columns, out):
    lane = lax.broadcasted_iota(jnp.int32, (X, H), 1)
    gathered = jnp.zeros((X, H), F32)
    for k, column in enumerate(columns):
        gathered = jnp.where(lane == k, column, gathered)
    out[...] = gathered.T[:8]


class ProbeSum:
    def __init__(self, copies, sums, probe, out, pair_in, part, y_in, y_part, rows_in):
        self.row, col = lax.axis_index("row"), lax.axis_index("col")
        self.y, self.core = col // 2, lax.rem(col, 2)
        self.tile = lax.rem(self.row, 8)
        self.copies, self.sums, self.probe, self.out = copies, sums, probe, out
        self.pair_in, self.part, self.y_in, self.y_part = pair_in, part, y_in, y_part
        self.rows_in = rows_in
        self.col = col
        self.other = (self.row, self.y * 2 + 1 - self.core)
        self.y_peers = [
            (self.row, lax.rem(self.y + k, 4) * 2 + self.core) for k in range(1, 4)
        ]
        self.row_peers = [(lax.rem(self.row + k, 16), col) for k in range(1, 16)]

    def peers(self):
        return self.y_peers + self.row_peers

    def start_pair(self):
        self.pair = self.copies.start(self.sums.at[1 - self.core], self.pair_in, self.other)

    def start_y(self):
        self.pair.wait_recv()
        self.part[...] = self.sums[self.core] + self.pair_in[...]
        self.y_sent = []
        for k in range(1, 4):
            at = lax.rem(self.y + k, 4) * 8
            self.y_sent.append(
                self.copies.start(
                    self.part.at[pl.ds(at, 8)], self.y_in.at[k - 1], self.y_peers[k - 1]
                )
            )

    def start_rows(self):
        for copy in self.y_sent:
            copy.wait_recv()
        self.y_part[...] = (
            self.part[pl.ds(self.y * 8, 8)] + self.y_in[0] + self.y_in[1] + self.y_in[2]
        )
        self.rows_in[self.row] = self.y_part[self.tile]
        for k in range(1, 16):
            tile = lax.rem(self.row + k, 8)
            self.copies.start(
                self.y_part.at[tile], self.rows_in.at[self.row], self.row_peers[k - 1]
            )
        self.first = self.copies.count - 15

    def landed(self, ref, number):
        pltpu.make_async_remote_copy(
            src_ref=ref,
            dst_ref=ref,
            send_sem=self.copies.send_sems.at[number],
            recv_sem=self.copies.recv_sems.at[number],
            device_id=self.other,
            device_id_type=MESH,
        ).wait_recv()

    def start_back(self):
        for k in range(1, 16):
            self.landed(self.rows_in.at[lax.rem(self.row + 16 - k, 16)], self.first + k - 1)
        total = self.rows_in[0]
        for k in range(1, 16):
            total = total + self.rows_in[k]
        rt = self.y * 8 + self.tile
        rows, cols = pl.ds(pl.multiple_of(rt * 8, 8), 8), pl.ds(pl.multiple_of(self.core * H, H), H)
        inverse = 1.0 / (total[2] + 1.0)
        for c in range(2):
            self.out[self.core, rt, c] = self.probe[c, rows, cols] + total[c] * inverse
        mine = self.out.at[self.core, rt]
        group = self.row // 8 * 8
        self.first = self.copies.count
        for k in range(1, 8):
            self.copies.start(mine, mine, (group + lax.rem(self.tile + k, 8), self.col))

    def start_back_y(self):
        for k in range(1, 8):
            tile = lax.rem(self.tile + 8 - k, 8)
            self.landed(self.out.at[self.core, self.y * 8 + tile], self.first + k - 1)
        mine = self.out.at[self.core, pl.ds(self.y * 8, 8)]
        self.first = self.copies.count
        for k in range(1, 4):
            self.copies.start(mine, mine, self.y_peers[k - 1])

    def start_back_pair(self):
        for k in range(1, 4):
            at = lax.rem(self.y + 4 - k, 4) * 8
            self.landed(self.out.at[self.core, pl.ds(at, 8)], self.first + k - 1)
        mine = self.out.at[self.core]
        self.first = self.copies.count
        self.copies.start(mine, mine, self.other)

    def end(self):
        self.landed(self.out.at[1 - self.core], self.first)


PROBE_COPIES = 1 + 3 + 15 + 7 + 3 + 1


def start_table(starts):
    def count(by, bx):
        return starts[by // 4 + 1, bx // 4 + 1, 0, by % 4 * 4 + bx % 4]

    return count


def block_weight(count, square, by, bx, rows):
    first, size = rows
    total = 1.0
    for qy in range(2):
        for qx in range(2):
            total = total + count(by - qy, bx - qx) * square[
                pl.ds(qy * H + first, size), pl.ds(qx * H, H)
            ]
    return total


def spread_lines(rows):
    length = rows[0].shape[1]
    packed = jnp.concatenate(rows + [jnp.zeros((H - len(rows), length), F32)], 0)
    return packed.T


def shifted_sum(canvas, c, first, rows, cols):
    width = cols + 2 * H
    whole = canvas[c, pl.ds(first, rows), pl.ds(0, width)]
    left = pltpu.roll(whole, 1, 1)[:, H : H + cols]
    right = pltpu.roll(whole, width - 1, 1)[:, H : H + cols]
    above = canvas[c, pl.ds(first - 1, rows), pl.ds(H, cols)]
    below = canvas[c, pl.ds(first + 1, rows), pl.ds(H, cols)]
    return below + above + right + left, whole[:, H : H + cols]


def rates(classes, weights):
    value = jnp.full(classes.shape, weights[0], F32)
    for k in range(1, 4):
        value = jnp.where(classes == k, weights[k], value)
    return value


def blank_sides(canvas, cols_end, first, size):
    col = lax.axis_index("col")
    width = canvas.shape[2]

    @pl.when(col == 0)
    def _():
        canvas[:, pl.ds(first, size), 0:H] = jnp.zeros((2, size, H), F32)

    @pl.when(col == 7)
    def _():
        canvas[:, pl.ds(first, size), cols_end:] = jnp.zeros((2, size, width - cols_end), F32)


def blank_outside(canvas, rows_end, cols_end):
    row = lax.axis_index("row")
    _, height, width = canvas.shape

    @pl.when(row == 0)
    def _():
        canvas[:, 0:RING, :] = jnp.zeros((2, RING, width), F32)

    @pl.when(row == 15)
    def _():
        canvas[:, rows_end:, :] = jnp.zeros((2, height - rows_end, width), F32)

    blank_sides(canvas, cols_end, 0, height)


MIDDLE = pl.ds(H, T - H)
LINES = [(0, 0), (0, 1), (1, 2), (1, 3), (0, 4), (0, 5), (1, 6), (1, 7)]
HALF = H // 2
PIECES = [(c, first) for c in range(2) for first in (0, HALF)]


def unpack_probe(tiles, out):
    for c in range(2):
        for ct in range(2):
            out[c, :, ct * H : (ct + 1) * H] = tiles[ct, :, c].reshape(S, H)


def middle_phase(
    copies, probe_sum, offsets, terms, grads, lines, classes, class_down, class_right, probe, starts, weights,
    canvas, canvas_next, probe_next, square, corners, tiles,
    from_left, from_right, from_up, from_down, lines_lr, lines_up, lines_down,
):
    up, down, left, right = around()
    probe_sum.start_pair()
    gather(offsets, terms, grads, 0, 4, 2)
    later = []

    def send_piece(k):
        c, first = PIECES[k]
        later.append(
            copies.start(
                grads.at[c, pl.ds(T + first, HALF), MIDDLE],
                from_up.at[c, pl.ds(RING + first, HALF), MIDDLE],
                down,
            )
        )
        later.append(
            copies.start(
                grads.at[c, pl.ds(first, HALF), MIDDLE],
                from_down.at[c, pl.ds(first, HALF), MIDDLE],
                up,
            )
        )

    for k in range(4):
        send_piece(k)
    probe_sum.start_y()
    gather(offsets, terms, grads, 1, 1, 3)
    inside = pl.ds(RING, X)
    columns_as_rows(
        [grads[c, :, T - 1 : T] for c in range(2)]
        + [grads[c, :, H : H + 1] for c in range(2)]
        + [canvas[c, inside, H + T - 1 : H + T] for c in range(2)]
        + [canvas[c, inside, H + H : H + H + 1] for c in range(2)],
        lines,
    )
    later += [
        copies.start(
            grads.at[:, pl.ds(T - RING, RING), MIDDLE], from_up.at[:, pl.ds(0, RING), MIDDLE], down
        ),
        copies.start(
            grads.at[:, pl.ds(H, RING), MIDDLE], from_down.at[:, pl.ds(H, RING), MIDDLE], up
        ),
        copies.start(lines, lines_up.at[2], down),
        copies.start(lines, lines_down.at[2], up),
    ]
    side = [
        copies.start(lines, lines_lr.at[0], right),
        copies.start(lines, lines_lr.at[1], left),
        copies.start(grads.at[:, :, pl.ds(T, H)], from_left, right),
        copies.start(grads.at[:, :, pl.ds(0, H)], from_right, left),
    ]
    count = start_table(starts)
    square[...] = probe[0] * probe[0] + probe[1] * probe[1]

    def update(by, bx, ring=None):
        if by in (-1, 5):
            at, size, first = (0, RING, H - RING) if by == -1 else (RING + X, RING, 0)
        else:
            at, size, first = RING + by * H, H, 0
        edge = bx in (-1, 5)
        inverse = 1.0 / block_weight(count, square, by, bx, (first, size))
        cols = pl.ds(H + bx * H, H)
        for c in range(2):
            if edge:
                k = 0 if bx == -1 else 2
                grad = jnp.broadcast_to(ring[:, k + c : k + c + 1], (H, H))
                base = jnp.broadcast_to(ring[:, k + 4 + c : k + 5 + c], (H, H))
            else:
                base = canvas[c, pl.ds(at, size), cols]
                block = pl.ds(bx * H, H)
                if by == -1:
                    grad = from_up[c, 0:RING, block]
                elif by == 5:
                    grad = from_down[c, H:STRIP, block]
                else:
                    grad = grads[c, pl.ds(by * H, H), block]
                    if by == 0:
                        grad = grad + from_up[c, RING:STRIP, block]
                    if by == 4:
                        grad = grad + from_down[c, 0:H, block]
                    if bx == 0:
                        grad = grad + from_left[c, pl.ds(by * H, H), :]
                    if bx == 4:
                        grad = grad + from_right[c, pl.ds(by * H, H), :]
            canvas[c, pl.ds(at, size), cols] = base + grad * inverse

    def smooth(by):
        if by < 4:
            levels = jnp.concatenate(
                [classes[pl.ds(by * H, H), :], class_right[pl.ds(by * H, H), :]], 1
            )
        else:
            levels = class_down[...]
        rate = rates(levels, weights)
        for c in range(2):
            around_sum, center = shifted_sum(canvas, c, RING + by * H, H, X)
            canvas_next[c, pl.ds(RING + by * H, H), pl.ds(H, X)] = center + rate * (around_sum - 4.0 * center)

    for by in (1, 2, 3):
        for bx in (1, 2, 3):
            update(by, bx)
    probe_sum.start_rows()
    for copy in side:
        copy.wait_recv()
    for k, (first, source) in enumerate(
        ((0, from_left), (0, from_right), (X - STRIP, from_left), (X - STRIP, from_right))
    ):
        column = 0 if k % 2 == 0 else T
        corners[k] = (
            grads[:, pl.ds(first, STRIP), pl.ds(column, H)]
            + source[:, pl.ds(first, STRIP), :]
        )
    probe_sum.start_back()
    later += [
        copies.start(lines_lr, lines_up.at[pl.ds(0, 2)], down),
        copies.start(lines_lr, lines_down.at[pl.ds(0, 2)], up),
        copies.start(corners.at[0], from_down.at[:, :, pl.ds(0, H)], up),
        copies.start(corners.at[2], from_up.at[:, :, pl.ds(0, H)], down),
        copies.start(corners.at[1], from_down.at[:, :, pl.ds(T, H)], up),
        copies.start(corners.at[3], from_up.at[:, :, pl.ds(T, H)], down),
    ]
    for by in (1, 2, 3):
        update(by, 0)
        update(by, 4)
    probe_sum.start_back_y()
    rows = [lines_lr[side_at, k : k + 1] for side_at, k in LINES]
    ring = spread_lines(rows)
    for by in (1, 2, 3):
        for bx in (-1, 5):
            update(by, bx, ring[by * H : (by + 1) * H])
    blank_sides(canvas, H + T, RING + H, 3 * H)
    smooth(2)
    probe_sum.start_back_pair()
    for copy in later:
        copy.wait_recv()
    far = []
    for n, (side_at, k) in enumerate(LINES):
        above = lines_up[side_at, k : k + 1, T:]
        below_it = lines_down[side_at, k : k + 1, :H]
        if n < 4:
            pieces = [rows[n][:, :H] + above, rows[n][:, T:] + below_it]
        else:
            pieces = [rows[n][:, :H], below_it]
        far.append(jnp.concatenate(pieces, 1))
    ring = spread_lines(far)
    for by in (0, 4):
        for bx in range(5):
            update(by, bx)
        for bx in (-1, 5):
            update(by, bx, ring[:H] if by == 0 else ring[H:])
    for by in (-1, 5):
        for bx in range(5):
            update(by, bx)
    blank_outside(canvas, RING + T, H + T)
    for by in (0, 1, 3, 4):
        smooth(by)
    probe_sum.end()
    unpack_probe(tiles, probe_next)
    copies.finish()


def last_phase(
    copies, probe_sum, offsets, terms, grads, lines, classes, probe, starts, weights,
    canvas, ring_out, ring_up, obj_out, probe_out, square, corner_down, corner_up, tiles,
    from_left, from_up, from_down, lines_lr, lines_up,
):
    up, down, left, right = around()
    probe_sum.start_pair()
    ring_out[...] = canvas[:, pl.ds(T, RING), pl.ds(H, T)]
    gather(offsets, terms, grads, 0, 4, 2)
    later = [
        copies.start(ring_out, ring_up, down),
        copies.start(grads.at[:, pl.ds(0, RING), MIDDLE], from_down.at[:, :, MIDDLE], up),
    ]

    def send_piece(k):
        c, first = PIECES[k]
        later.append(
            copies.start(
                grads.at[c, pl.ds(T + first, HALF), MIDDLE],
                from_up.at[c, pl.ds(RING + first, HALF), MIDDLE],
                down,
            )
        )

    for k in range(4):
        send_piece(k)
    probe_sum.start_y()
    gather(offsets, terms, grads, 1, 1, 3)
    inside = pl.ds(RING, X)
    columns_as_rows(
        [grads[c, :, T - 1 : T] for c in range(2)]
        + [grads[c, :, 0:1] for c in range(2)]
        + [grads[c, :, T : T + 1] for c in range(2)]
        + [canvas[c, inside, H + T - 1 : H + T] for c in range(2)],
        lines,
    )
    later += [
        copies.start(
            grads.at[:, pl.ds(T - RING, RING), MIDDLE], from_up.at[:, pl.ds(0, RING), MIDDLE], down
        ),
        copies.start(lines, lines_up.at[2], down),
    ]
    line_copies = [
        copies.start(lines, lines_lr.at[0], right),
        copies.start(lines, lines_lr.at[1], left),
    ]
    side = copies.start(grads.at[:, :, pl.ds(T, H)], from_left, right)
    count = start_table(starts)
    square[...] = probe[0] * probe[0] + probe[1] * probe[1]

    def update(by, bx, ring=None):
        if by in (-1, 4):
            at, size, first = (0, RING, H - RING) if by == -1 else (RING + T, RING, 0)
        else:
            at, size, first = RING + by * H, H, 0
        inverse = 1.0 / block_weight(count, square, by, bx, (first, size))
        cols = pl.ds(H + bx * H, H)
        block = pl.ds(max(bx, 0) * H, H)
        for c in range(2):
            base = canvas[c, pl.ds(at, size), cols]
            if bx == -1:
                grad = jnp.broadcast_to(ring[:, c : c + 1], (H, H))
                base = jnp.broadcast_to(ring[:, 4 + c : 5 + c], (H, H))
            elif bx == 4:
                grad = jnp.broadcast_to(ring[:, 2 + c : 3 + c], (H, H))
                grad = grad + grads[c, pl.ds(by * H, H), block]
            elif by == -1:
                base = ring_up[c, :, block]
                grad = from_up[c, 0:RING, block]
            else:
                grad = grads[c, pl.ds(by * H, size), block]
                if by == 0:
                    grad = grad + from_up[c, RING:STRIP, block]
                if by == 4:
                    grad = grad + from_down[c, :, block]
                if bx == 0:
                    grad = grad + from_left[c, pl.ds(by * H, size), :]
            canvas[c, pl.ds(at, size), cols] = base + grad * inverse

    def smooth(by):
        rate = rates(classes[pl.ds(by * H, H), :], weights)
        for c in range(2):
            around_sum, center = shifted_sum(canvas, c, RING + by * H, H, T)
            obj_out[c, pl.ds(by * H, H), :] = center + rate * (around_sum - 4.0 * center)

    for by in (1, 2, 3):
        for bx in (1, 2, 3):
            update(by, bx)
    probe_sum.start_rows()
    side.wait_recv()
    for copy in line_copies:
        copy.wait_recv()
    corner_down[...] = (
        grads[:, pl.ds(X - STRIP, STRIP), pl.ds(0, H)] + from_left[:, pl.ds(X - STRIP, STRIP), :]
    )
    corner_up[...] = grads[:, pl.ds(0, RING), pl.ds(0, H)] + from_left[:, pl.ds(0, RING), :]
    probe_sum.start_back()
    later += [
        copies.start(lines_lr, lines_up.at[pl.ds(0, 2)], down),
        copies.start(corner_down, from_up.at[:, :, pl.ds(0, H)], down),
        copies.start(corner_up, from_down.at[:, :, pl.ds(0, H)], up),
    ]
    for by in (1, 2, 3):
        update(by, 0)
    probe_sum.start_back_y()
    rows = [lines_lr[0, c : c + 1] for c in range(2)]
    rows += [lines_lr[1, 2 + c : 3 + c] for c in range(2)]
    rows += [lines_lr[0, 6 + c : 7 + c] for c in range(2)]
    ring = spread_lines(rows)
    for by in (1, 2, 3):
        for bx in (-1, 4):
            update(by, bx, ring[by * H : (by + 1) * H])
    blank_sides(canvas, H + T, RING + H, 3 * H)
    smooth(2)
    probe_sum.start_back_pair()
    for copy in later:
        copy.wait_recv()
    far = [rows[c][:, :H] + lines_up[0, c : c + 1, T:] for c in range(2)]
    far += [
        rows[2 + c][:, :H] + lines_up[1, 2 + c : 3 + c, T:] + lines_up[2, 4 + c : 5 + c, T:]
        for c in range(2)
    ]
    far += [rows[4 + c][:, :H] for c in range(2)]
    ring = spread_lines(far)
    for bx in range(4):
        update(0, bx)
    for bx in (-1, 4):
        update(0, bx, ring)
    for by in (-1, 4):
        for bx in range(4):
            update(by, bx)
    blank_outside(canvas, RING + T, H + T)
    for by in (0, 1, 3):
        smooth(by)
    probe_sum.end()
    unpack_probe(tiles, probe_out)
    copies.finish()


def whole_kernel(
    obj, probe_in, amps_in, offsets, live, classes_in, weights, right_table, left_table,
    obj_out, probe_out,
    canvas, canvas_next, terms, grads, sums, probe, probe_next, amps, classes, class_down,
    class_right, square, counted, starts_in, starts, lines, ring_out, ring_up, corners, corner_down,
    corner_up, tiles, tiles_last, part, y_part, *refs
):
    landing, landing_last, (sems, send_sems, recv_sems) = refs[:10], refs[10:18], refs[18:]
    up, down, left, right = around()
    row, col = lax.axis_index("row"), lax.axis_index("col")
    copies = Copies(send_sems, recv_sems)
    probe_sum = ProbeSum(
        copies, sums, probe, tiles, landing[7], part, landing[8], y_part, landing[9]
    )
    probe_sum_last = ProbeSum(
        copies, sums, probe_next, tiles_last, landing_last[5], part, landing_last[6], y_part,
        landing_last[7],
    )
    near = {
        (dr, dc): (lax.rem(row + dr + 16, 16), lax.rem(col + dc + 8, 8))
        for dr in (-1, 0, 1)
        for dc in (-1, 0, 1)
        if (dr, dc) != (0, 0)
    }
    pairs = [
        (obj, canvas.at[:, pl.ds(RING, T), pl.ds(H, T)]),
        (probe_in, probe),
        (amps_in, amps),
        (classes_in, classes),
    ]
    own = [pltpu.make_async_copy(src, dst, sems.at[k]) for k, (src, dst) in enumerate(pairs)]
    for copy in own:
        copy.start()
    count_starts(offsets, live, counted)
    greet([device for (dr, dc), device in near.items() if dc != 0] + probe_sum.peers())
    rows = copies.start(
        obj.at[:, pl.ds(0, STRIP), :], canvas.at[:, pl.ds(RING + T, STRIP), pl.ds(H, T)], up
    )
    beside = copies.start(
        obj.at[:, :, pl.ds(0, H)], canvas.at[:, pl.ds(RING, T), pl.ds(H + T, H)], left
    )
    class_beside = copies.start(classes_in.at[:, pl.ds(0, H)], class_right, left)
    strips = [
        rows,
        copies.start(
            obj.at[:, pl.ds(T - RING, RING), :], canvas.at[:, pl.ds(0, RING), pl.ds(H, T)], down
        ),
    ]
    small = [
        copies.start(counted, starts_in.at[1 - dr, 1 - dc], device)
        for (dr, dc), device in near.items()
    ]
    starts_in[1, 1] = counted[...]
    frame_terms(terms)
    beside.wait_recv()
    corner = [
        copies.start(
            canvas.at[:, pl.ds(RING, STRIP), pl.ds(H + T, H)],
            canvas.at[:, pl.ds(RING + T, STRIP), pl.ds(H + T, H)],
            up,
        ),
        copies.start(
            canvas.at[:, pl.ds(T, RING), pl.ds(H + T, H)],
            canvas.at[:, pl.ds(0, RING), pl.ds(H + T, H)],
            down,
        ),
    ]
    class_beside.wait_recv()
    class_later = [
        copies.start(classes_in.at[pl.ds(0, H), :], class_down.at[:, pl.ds(0, T)], up),
        copies.start(class_right.at[pl.ds(0, H), :], class_down.at[:, pl.ds(T, H)], up),
    ]
    for copy in own:
        copy.wait()
    for copy in small:
        copy.wait_recv()
    to_scalars = pltpu.make_async_copy(starts_in, starts, sems.at[4])
    to_scalars.start()
    for copy in strips + corner:
        copy.wait_recv()
    to_scalars.wait()
    visit_slots(canvas, probe, amps, offsets, live, right_table, left_table, terms, sums)
    for copy in class_later:
        copy.wait_recv()
    copies.finish()
    middle_phase(
        copies, probe_sum, offsets, terms, grads, lines, classes, class_down, class_right, probe, starts,
        weights, canvas, canvas_next, probe_next, square, corners, tiles, *landing[:7],
    )
    visit_slots(
        canvas_next, probe_next, amps, offsets, live, right_table, left_table, terms, sums
    )
    last_phase(
        copies, probe_sum_last, offsets, terms, grads, lines, classes, probe_next, starts, weights,
        canvas_next, ring_out, ring_up, obj_out, probe_out, square, corner_down, corner_up, tiles_last,
        *landing_last[:5],
    )
    assert copies.count == send_sems.shape[0]


PROBE_LANDING = [
    pltpu.VMEM((32, 3, 8, H), F32),
    pltpu.VMEM((3, 8, 3, 8, H), F32),
    pltpu.VMEM((16, 3, 8, H), F32),
]
COPIES = 16 + 2 * PROBE_COPIES + 22 + 14


def whole(obj, probe, amps, offsets, live, classes, weights, right, left):
    wide = (2, X + 2 * RING, X + 2 * H)
    scratch = [
        pltpu.VMEM(wide, F32),
        pltpu.VMEM(wide, F32),
        pltpu.VMEM((8, 2, 2 * S, 2 * S), F32),
        pltpu.VMEM((2, X, X), F32),
        pltpu.VMEM((2, 32, 3, 8, H), F32),
        pltpu.VMEM((2, S, S), F32),
        pltpu.VMEM((2, S, S), F32),
        pltpu.VMEM((8, S, S), BF16),
        pltpu.VMEM((T, T), jnp.int32),
        pltpu.VMEM((H, X), jnp.int32),
        pltpu.VMEM((T, H), jnp.int32),
        pltpu.VMEM((S, S), F32),
        pltpu.VMEM((8, H), F32),
        pltpu.VMEM((3, 3, 8, H), F32),
        pltpu.SMEM((3, 3, 8, H), F32),
        pltpu.VMEM((8, X), F32),
        pltpu.VMEM((2, RING, T), F32),
        pltpu.VMEM((2, RING, T), F32),
        pltpu.VMEM((4, 2, STRIP, H), F32),
        pltpu.VMEM((2, STRIP, H), F32),
        pltpu.VMEM((2, RING, H), F32),
        pltpu.VMEM((2, 32, 2, 8, H), F32),
        pltpu.VMEM((2, 32, 2, 8, H), F32),
        pltpu.VMEM((32, 3, 8, H), F32),
        pltpu.VMEM((8, 3, 8, H), F32),
    ]
    landing = [
        pltpu.VMEM((2, X, H), F32),
        pltpu.VMEM((2, X, H), F32),
        pltpu.VMEM((2, STRIP, X), F32),
        pltpu.VMEM((2, STRIP, X), F32),
        pltpu.VMEM((2, 8, X), F32),
        pltpu.VMEM((3, 8, X), F32),
        pltpu.VMEM((3, 8, X), F32),
    ] + PROBE_LANDING
    landing_last = [
        pltpu.VMEM((2, X, H), F32),
        pltpu.VMEM((2, STRIP, T), F32),
        pltpu.VMEM((2, RING, T), F32),
        pltpu.VMEM((2, 8, X), F32),
        pltpu.VMEM((3, 8, X), F32),
    ] + PROBE_LANDING
    return pl.pallas_call(
        whole_kernel,
        name="reconstruct",
        out_shape=[
            jax.ShapeDtypeStruct((2, T, T), F32),
            jax.ShapeDtypeStruct((2, S, S), F32),
        ],
        in_specs=[ANY, ANY, ANY, SMEM, SMEM, ANY, SMEM, VMEM, VMEM],
        out_specs=[VMEM, VMEM],
        scratch_shapes=scratch
        + landing
        + landing_last
        + [
            pltpu.SemaphoreType.DMA((5,)),
            pltpu.SemaphoreType.DMA((COPIES,)),
            pltpu.SemaphoreType.DMA((COPIES,)),
        ],
        compiler_params=pltpu.CompilerParams(
            collective_id=0, has_side_effects=True, vmem_limit_bytes=VMEM_BYTES
        ),
    )(obj, probe, amps, offsets, live, classes, weights, right, left)


def hand_over_kernel(obj, probe, obj_out, probe_out):
    obj_out[...] = obj[...]
    probe_out[...] = probe[...]


def hand_over(obj, probe):
    specs = [
        pl.BlockSpec((2, T // 4, T), lambda i: (0, i, 0)),
        pl.BlockSpec((2, S // 4, S), lambda i: (0, i, 0)),
    ]
    return pl.pallas_call(
        hand_over_kernel,
        name="hand_over",
        grid=(4,),
        out_shape=[
            jax.ShapeDtypeStruct((2, T, T), F32),
            jax.ShapeDtypeStruct((2, S, S), F32),
        ],
        in_specs=specs,
        out_specs=specs,
        compiler_params=pltpu.CompilerParams(vmem_limit_bytes=VMEM_BYTES),
    )(obj, probe)


def per_device(
    object_init, probe_init, amplitudes, scan_offsets, live_count, smooth_class, class_weight
):
    right, left = (jnp.asarray(table) for table in dft_blocks())
    return tuple(
        hand_over(
            *whole(
                object_init,
                probe_init,
                amplitudes.reshape(8, S, S),
                scan_offsets.reshape(8, 2).T,
                live_count,
                smooth_class,
                class_weight,
                right,
                left,
            )
        )
    )


def solution(mesh):
    in_specs = (
        P(None, "row", "col"),
        P(),
        P("row", "col", None, None, None),
        P("row", "col", None, None),
        P("row", "col"),
        P("row", "col"),
        P(),
    )
    out_specs = (P(None, "row", "col"), P())
    return jax.shard_map(
        per_device, mesh=mesh, in_specs=in_specs, out_specs=out_specs, check_vma=False
    )
```

```python
import math

import jax
import jax.numpy as jnp
import ml_dtypes
import numpy as np
from jax import lax
from jax.experimental import pallas as pl
from jax.experimental.pallas import tpu as pltpu
from jax.sharding import PartitionSpec as P

F32 = jnp.float32
BF16 = jnp.bfloat16
T = 512
S = 256
H = 128
X = T + H
RING = 8
STRIP = H + RING
MESH = pl.DeviceIdType.MESH
ANY = pl.BlockSpec(memory_space=pl.ANY)
VMEM = pl.BlockSpec(memory_space=pltpu.VMEM)
SMEM = pl.BlockSpec(memory_space=pltpu.SMEM)
VMEM_BYTES = 64 * 1024 * 1024


def dft_blocks():
    index = np.arange(S)
    phases = 2.0 * math.pi / S * (index[:, None] * index[None, :] % S)
    re = (np.cos(phases) / math.sqrt(S)).astype(ml_dtypes.bfloat16)
    im = (-np.sin(phases) / math.sqrt(S)).astype(ml_dtypes.bfloat16)
    right = np.block([[re, im], [-im, re]])
    left = np.block([[re, -im], [im, re]])
    return right, left


class Copies:
    def __init__(self, send_sems, recv_sems):
        self.send_sems, self.recv_sems, self.count = send_sems, recv_sems, 0
        self.started = []

    def make(self, src, dst, device):
        k = self.count
        self.count += 1
        return pltpu.make_async_remote_copy(
            src_ref=src,
            dst_ref=dst,
            send_sem=self.send_sems.at[k],
            recv_sem=self.recv_sems.at[k],
            device_id=device,
            device_id_type=MESH,
        )

    def start(self, src, dst, device):
        copy = self.make(src, dst, device)
        copy.start()
        self.started.append(copy)
        return copy

    def finish(self):
        for copy in self.started:
            copy.wait_send()
        self.started = []


def around():
    row, col = lax.axis_index("row"), lax.axis_index("col")
    up = (lax.rem(row + 15, 16), col)
    down = (lax.rem(row + 1, 16), col)
    left = (row, lax.rem(col + 7, 8))
    right = (row, lax.rem(col + 1, 8))
    return up, down, left, right


def greet(devices):
    barrier = pltpu.get_barrier_semaphore()
    for device in devices:
        pl.semaphore_signal(barrier, inc=1, device_id=device, device_id_type=MESH)
    pl.semaphore_wait(barrier, len(devices))


def count_starts(offsets, live, out):
    lane = lax.broadcasted_iota(jnp.int32, (8, H), 1)
    row0 = lax.axis_index("row") * T
    col0 = lax.axis_index("col") * T
    found = jnp.zeros((8, H), F32)
    for slot in range(8):
        at = lax.div(offsets[0, slot] - row0, H) * 4 + lax.div(offsets[1, slot] - col0, H)
        found += jnp.where((lane == at) & (live[0, 0] > slot), 1.0, 0.0)
    out[...] = found


def dot(a, b):
    return jnp.dot(a, b, preferred_element_type=F32)


def side_by_side(re, im):
    return jnp.concatenate([re.astype(BF16), im.astype(BF16)], 1)


def stacked(both):
    both = both.astype(BF16)
    return jnp.concatenate([both[:, :S], both[:, S:]], 0)


def start_block(offsets, slot):
    by = lax.div(offsets[0, slot] - lax.axis_index("row") * T, H)
    bx = lax.div(offsets[1, slot] - lax.axis_index("col") * T, H)
    return jnp.clip(by, 0, 3), jnp.clip(bx, 0, 3)


def visit_slots(canvas, probe, amps, offsets, live, right, left, terms, sums):
    sums[...] = jnp.zeros_like(sums)

    def some(step, carry):
        slots = [4 * step + k for k in range(4)]
        places = []
        for slot in slots:
            by, bx = start_block(offsets, slot)
            places.append((pl.ds(by * H + RING, S), pl.ds(bx * H + H, S)))

        def leaving(rows, cols):
            probe_re, probe_im = probe[0], probe[1]
            patch_re, patch_im = canvas[0, rows, cols], canvas[1, rows, cols]
            return side_by_side(
                probe_re * patch_re - probe_im * patch_im,
                probe_re * patch_im + probe_im * patch_re,
            )

        def corrected(slot, far):
            far_re, far_im = far[:S], far[S:]
            square = far_re * far_re + far_im * far_im
            factor = amps[slot].astype(F32) * lax.rsqrt(jnp.maximum(square, 1.0)) - 1.0
            return side_by_side(far_re * factor, far_im * factor)

        waves = [leaving(rows, cols) for rows, cols in places]
        waves = [stacked(dot(wave, right[...])) for wave in waves]
        waves = [dot(left[...], wave) for wave in waves]
        waves = [corrected(slot, wave) for slot, wave in zip(slots, waves)]
        waves = [stacked(dot(wave, left[...])) for wave in waves]
        waves = [dot(right[...], wave) for wave in waves]
        inner = pl.ds(H, S)
        grads = [0.0, 0.0, 0.0]
        for slot, (rows, cols), diff in zip(slots, places, waves):
            mask = jnp.where(jnp.broadcast_to(live[0, 0], (1, S)) > slot, 1.0, 0.0)
            probe_re, probe_im = probe[0], probe[1]
            patch_re, patch_im = canvas[0, rows, cols], canvas[1, rows, cols]
            diff_re, diff_im = diff[:S] * mask, diff[S:] * mask
            terms[slot, 0, inner, inner] = probe_re * diff_re + probe_im * diff_im
            terms[slot, 1, inner, inner] = probe_re * diff_im - probe_im * diff_re
            grads[0] += patch_re * diff_re + patch_im * diff_im
            grads[1] += patch_re * diff_im - patch_im * diff_re
            grads[2] += (patch_re * patch_re + patch_im * patch_im) * mask
        for c in range(3):
            for ct in range(2):
                sums[ct, :, c] += grads[c][:, ct * H : (ct + 1) * H].reshape(32, 8, H)
        return carry

    lax.fori_loop(0, 2, some, 0)


def gather(offsets, terms, deposits, first, step, count):
    starts_at = [start_block(offsets, slot) for slot in range(8)]

    def one(block, carry):
        by, bx = first + lax.div(block, 5) * step, lax.rem(block, 5)
        total = [None, None]
        for slot in range(8):
            y = jnp.clip(by - starts_at[slot][0], -1, 2) * H + H
            x = jnp.clip(bx - starts_at[slot][1], -1, 2) * H + H
            for c in range(2):
                part = terms[slot, c, pl.ds(y, H), pl.ds(x, H)]
                total[c] = part if slot == 0 else total[c] + part
        for c in range(2):
            deposits[
                c, pl.ds(pl.multiple_of(by * H, H), H), pl.ds(pl.multiple_of(bx * H, H), H)
            ] = total[c]
        return carry

    lax.fori_loop(0, 5 * count, one, 0)


def frame_terms(terms):
    for slot in range(8):
        terms[slot, :, 0:H, :] = jnp.zeros((2, H, 2 * S), F32)
        terms[slot, :, S + H :, :] = jnp.zeros((2, H, 2 * S), F32)
        terms[slot, :, H : S + H, 0:H] = jnp.zeros((2, S, H), F32)
        terms[slot, :, H : S + H, S + H :] = jnp.zeros((2, S, H), F32)


def columns_as_rows(columns, out):
    lane = lax.broadcasted_iota(jnp.int32, (X, H), 1)
    gathered = jnp.zeros((X, H), F32)
    for k, column in enumerate(columns):
        gathered = jnp.where(lane == k, column, gathered)
    out[...] = gathered.T[:8]


class ProbeSum:
    def __init__(self, copies, sums, probe, out, pair_in, part, y_in, y_part, rows_in):
        self.row, col = lax.axis_index("row"), lax.axis_index("col")
        self.y, self.core = col // 2, lax.rem(col, 2)
        self.tile = lax.rem(self.row, 8)
        self.copies, self.sums, self.probe, self.out = copies, sums, probe, out
        self.pair_in, self.part, self.y_in, self.y_part = pair_in, part, y_in, y_part
        self.rows_in = rows_in
        self.col = col
        self.other = (self.row, self.y * 2 + 1 - self.core)
        self.y_peers = [
            (self.row, lax.rem(self.y + k, 4) * 2 + self.core) for k in range(1, 4)
        ]
        self.row_peers = [(lax.rem(self.row + k, 16), col) for k in range(1, 16)]

    def peers(self):
        return self.y_peers + self.row_peers

    def start_pair(self):
        self.pair = self.copies.start(self.sums.at[1 - self.core], self.pair_in, self.other)

    def start_y(self):
        self.pair.wait_recv()
        self.part[...] = self.sums[self.core] + self.pair_in[...]
        self.y_sent = []
        for k in range(1, 4):
            at = lax.rem(self.y + k, 4) * 8
            self.y_sent.append(
                self.copies.start(
                    self.part.at[pl.ds(at, 8)], self.y_in.at[k - 1], self.y_peers[k - 1]
                )
            )

    def start_rows(self):
        for copy in self.y_sent:
            copy.wait_recv()
        self.y_part[...] = (
            self.part[pl.ds(self.y * 8, 8)] + self.y_in[0] + self.y_in[1] + self.y_in[2]
        )
        self.rows_in[self.row] = self.y_part[self.tile]
        for k in range(1, 16):
            tile = lax.rem(self.row + k, 8)
            self.copies.start(
                self.y_part.at[tile], self.rows_in.at[self.row], self.row_peers[k - 1]
            )
        self.first = self.copies.count - 15

    def landed(self, ref, number):
        pltpu.make_async_remote_copy(
            src_ref=ref,
            dst_ref=ref,
            send_sem=self.copies.send_sems.at[number],
            recv_sem=self.copies.recv_sems.at[number],
            device_id=self.other,
            device_id_type=MESH,
        ).wait_recv()

    def start_back(self):
        for k in range(1, 16):
            self.landed(self.rows_in.at[lax.rem(self.row + 16 - k, 16)], self.first + k - 1)
        total = self.rows_in[0]
        for k in range(1, 16):
            total = total + self.rows_in[k]
        rt = self.y * 8 + self.tile
        rows, cols = pl.ds(pl.multiple_of(rt * 8, 8), 8), pl.ds(pl.multiple_of(self.core * H, H), H)
        inverse = 1.0 / (total[2] + 1.0)
        for c in range(2):
            self.out[self.core, rt, c] = self.probe[c, rows, cols] + total[c] * inverse
        mine = self.out.at[self.core, rt]
        group = self.row // 8 * 8
        self.first = self.copies.count
        for k in range(1, 8):
            self.copies.start(mine, mine, (group + lax.rem(self.tile + k, 8), self.col))

    def start_back_y(self):
        for k in range(1, 8):
            tile = lax.rem(self.tile + 8 - k, 8)
            self.landed(self.out.at[self.core, self.y * 8 + tile], self.first + k - 1)
        mine = self.out.at[self.core, pl.ds(self.y * 8, 8)]
        self.first = self.copies.count
        for k in range(1, 4):
            self.copies.start(mine, mine, self.y_peers[k - 1])

    def start_back_pair(self):
        for k in range(1, 4):
            at = lax.rem(self.y + 4 - k, 4) * 8
            self.landed(self.out.at[self.core, pl.ds(at, 8)], self.first + k - 1)
        mine = self.out.at[self.core]
        self.first = self.copies.count
        self.copies.start(mine, mine, self.other)

    def end(self):
        self.landed(self.out.at[1 - self.core], self.first)


PROBE_COPIES = 1 + 3 + 15 + 7 + 3 + 1


def start_table(starts):
    def count(by, bx):
        return starts[by // 4 + 1, bx // 4 + 1, 0, by % 4 * 4 + bx % 4]

    return count


def block_weight(count, square, by, bx, rows):
    first, size = rows
    total = 1.0
    for qy in range(2):
        for qx in range(2):
            total = total + count(by - qy, bx - qx) * square[
                pl.ds(qy * H + first, size), pl.ds(qx * H, H)
            ]
    return total


def spread_lines(rows):
    length = rows[0].shape[1]
    packed = jnp.concatenate(rows + [jnp.zeros((H - len(rows), length), F32)], 0)
    return packed.T


def shifted_sum(canvas, c, first, rows, cols):
    width = cols + 2 * H
    whole = canvas[c, pl.ds(first, rows), pl.ds(0, width)]
    left = pltpu.roll(whole, 1, 1)[:, H : H + cols]
    right = pltpu.roll(whole, width - 1, 1)[:, H : H + cols]
    above = canvas[c, pl.ds(first - 1, rows), pl.ds(H, cols)]
    below = canvas[c, pl.ds(first + 1, rows), pl.ds(H, cols)]
    return below + above + right + left, whole[:, H : H + cols]


def rates(classes, weights):
    value = jnp.full(classes.shape, weights[0], F32)
    for k in range(1, 4):
        value = jnp.where(classes == k, weights[k], value)
    return value


def blank_sides(canvas, cols_end, first, size):
    col = lax.axis_index("col")
    width = canvas.shape[2]

    @pl.when(col == 0)
    def _():
        canvas[:, pl.ds(first, size), 0:H] = jnp.zeros((2, size, H), F32)

    @pl.when(col == 7)
    def _():
        canvas[:, pl.ds(first, size), cols_end:] = jnp.zeros((2, size, width - cols_end), F32)


def blank_outside(canvas, rows_end, cols_end):
    row = lax.axis_index("row")
    _, height, width = canvas.shape

    @pl.when(row == 0)
    def _():
        canvas[:, 0:RING, :] = jnp.zeros((2, RING, width), F32)

    @pl.when(row == 15)
    def _():
        canvas[:, rows_end:, :] = jnp.zeros((2, height - rows_end, width), F32)

    blank_sides(canvas, cols_end, 0, height)


MIDDLE = pl.ds(H, T - H)
LINES = [(0, 0), (0, 1), (1, 2), (1, 3), (0, 4), (0, 5), (1, 6), (1, 7)]
HALF = H // 2
PIECES = [(c, first) for c in range(2) for first in (0, HALF)]


def unpack_probe(tiles, out):
    for c in range(2):
        for ct in range(2):
            out[c, :, ct * H : (ct + 1) * H] = tiles[ct, :, c].reshape(S, H)


def middle_phase(
    copies, probe_sum, offsets, terms, grads, lines, rate, inverse, probe, starts,
    canvas, canvas_next, probe_next, square, corners, tiles,
    from_left, from_right, from_up, from_down, lines_lr, lines_up, lines_down,
):
    up, down, left, right = around()
    probe_sum.start_pair()
    gather(offsets, terms, grads, 0, 4, 2)
    later = []
    center = []

    def send_piece(k):
        c, first = PIECES[k]
        center.append(
            copies.start(
                grads.at[c, pl.ds(T + first, HALF), MIDDLE],
                from_up.at[c, pl.ds(RING + first, HALF), MIDDLE],
                down,
            )
        )
        center.append(
            copies.start(
                grads.at[c, pl.ds(first, HALF), MIDDLE],
                from_down.at[c, pl.ds(first, HALF), MIDDLE],
                up,
            )
        )

    probe_sum.start_y()
    for k in range(4):
        send_piece(k)
    gather(offsets, terms, grads, 1, 1, 3)
    inside = pl.ds(RING, X)
    columns_as_rows(
        [grads[c, :, T - 1 : T] for c in range(2)]
        + [grads[c, :, H : H + 1] for c in range(2)]
        + [canvas[c, inside, H + T - 1 : H + T] for c in range(2)]
        + [canvas[c, inside, H + H : H + H + 1] for c in range(2)],
        lines,
    )
    center += [
        copies.start(
            grads.at[:, pl.ds(T - RING, RING), MIDDLE], from_up.at[:, pl.ds(0, RING), MIDDLE], down
        ),
        copies.start(
            grads.at[:, pl.ds(H, RING), MIDDLE], from_down.at[:, pl.ds(H, RING), MIDDLE], up
        ),
    ]
    later += [
        copies.start(lines, lines_up.at[2], down),
        copies.start(lines, lines_down.at[2], up),
    ]
    side = [
        copies.start(lines, lines_lr.at[0], right),
        copies.start(lines, lines_lr.at[1], left),
        copies.start(grads.at[:, :, pl.ds(T, H)], from_left, right),
        copies.start(grads.at[:, :, pl.ds(0, H)], from_right, left),
    ]
    probe_sum.start_rows()
    count = start_table(starts)
    square[...] = probe[0] * probe[0] + probe[1] * probe[1]

    def rows_of(by):
        if by in (-1, 5):
            return (0, RING, H - RING) if by == -1 else (RING + X, RING, 0)
        return RING + by * H, H, 0

    def prepare(by, bx):
        at, size, first = rows_of(by)
        inverse[pl.ds(at, size), pl.ds(H + bx * H, H)] = 1.0 / block_weight(
            count, square, by, bx, (first, size)
        )

    def update(by, bx, ring=None):
        at, size, _ = rows_of(by)
        edge = bx in (-1, 5)
        cols = pl.ds(H + bx * H, H)
        scale = inverse[pl.ds(at, size), cols]
        for c in range(2):
            if edge:
                k = 0 if bx == -1 else 2
                grad = jnp.broadcast_to(ring[:, k + c : k + c + 1], (H, H))
                base = jnp.broadcast_to(ring[:, k + 4 + c : k + 5 + c], (H, H))
            else:
                base = canvas[c, pl.ds(at, size), cols]
                block = pl.ds(bx * H, H)
                if by == -1:
                    grad = from_up[c, 0:RING, block]
                elif by == 5:
                    grad = from_down[c, H:STRIP, block]
                else:
                    grad = grads[c, pl.ds(by * H, H), block]
                    if by == 0:
                        grad = grad + from_up[c, RING:STRIP, block]
                    if by == 4:
                        grad = grad + from_down[c, 0:H, block]
                    if bx == 0:
                        grad = grad + from_left[c, pl.ds(by * H, H), :]
                    if bx == 4:
                        grad = grad + from_right[c, pl.ds(by * H, H), :]
            canvas[c, pl.ds(at, size), cols] = base + grad * scale

    def smooth(by):
        for c in range(2):
            around_sum, center_now = shifted_sum(canvas, c, RING + by * H, H, X)
            canvas_next[c, pl.ds(RING + by * H, H), pl.ds(H, X)] = center_now + rate[
                pl.ds(by * H, H), :
            ] * (around_sum - 4.0 * center_now)

    for by in (1, 2, 3):
        for bx in (1, 2, 3):
            prepare(by, bx)
            update(by, bx)
    for by in range(-1, 6):
        for bx in range(-1, 6):
            if not (by in (1, 2, 3) and bx in (1, 2, 3) or by in (-1, 5) and bx in (-1, 5)):
                prepare(by, bx)
    probe_sum.start_back()
    for copy in side:
        copy.wait_recv()
    for k, (first, source) in enumerate(
        ((0, from_left), (0, from_right), (X - STRIP, from_left), (X - STRIP, from_right))
    ):
        column = 0 if k % 2 == 0 else T
        corners[k] = (
            grads[:, pl.ds(first, STRIP), pl.ds(column, H)]
            + source[:, pl.ds(first, STRIP), :]
        )
    later += [
        copies.start(lines_lr, lines_up.at[pl.ds(0, 2)], down),
        copies.start(lines_lr, lines_down.at[pl.ds(0, 2)], up),
        copies.start(corners.at[0], from_down.at[:, :, pl.ds(0, H)], up),
        copies.start(corners.at[2], from_up.at[:, :, pl.ds(0, H)], down),
        copies.start(corners.at[1], from_down.at[:, :, pl.ds(T, H)], up),
        copies.start(corners.at[3], from_up.at[:, :, pl.ds(T, H)], down),
    ]
    for by in (1, 2, 3):
        update(by, 0)
        update(by, 4)
    probe_sum.start_back_y()
    for copy in center:
        copy.wait_recv()
    for by in (-1, 0, 4, 5):
        for bx in (1, 2, 3):
            update(by, bx)
    rows = [lines_lr[side_at, k : k + 1] for side_at, k in LINES]
    ring = spread_lines(rows)
    for by in (1, 2, 3):
        for bx in (-1, 5):
            update(by, bx, ring[by * H : (by + 1) * H])
    blank_sides(canvas, H + T, RING + H, 3 * H)
    smooth(2)
    probe_sum.start_back_pair()
    for copy in later:
        copy.wait_recv()
    far = []
    for n, (side_at, k) in enumerate(LINES):
        above = lines_up[side_at, k : k + 1, T:]
        below_it = lines_down[side_at, k : k + 1, :H]
        if n < 4:
            pieces = [rows[n][:, :H] + above, rows[n][:, T:] + below_it]
        else:
            pieces = [rows[n][:, :H], below_it]
        far.append(jnp.concatenate(pieces, 1))
    ring = spread_lines(far)
    for by in (0, 4):
        for bx in (0, 4):
            update(by, bx)
        for bx in (-1, 5):
            update(by, bx, ring[:H] if by == 0 else ring[H:])
    for by in (-1, 5):
        for bx in (0, 4):
            update(by, bx)
    blank_outside(canvas, RING + T, H + T)
    for by in (0, 1, 3, 4):
        smooth(by)
    probe_sum.end()
    unpack_probe(tiles, probe_next)
    copies.finish()


def last_phase(
    copies, probe_sum, offsets, terms, grads, lines, rate, inverse, probe, starts,
    canvas, ring_out, ring_up, obj_now, obj_out, out_sems, probe_out, square, corner_down, corner_up, tiles,
    from_left, from_up, from_down, lines_lr, lines_up,
):
    up, down, left, right = around()
    probe_sum.start_pair()
    ring_out[...] = canvas[:, pl.ds(T, RING), pl.ds(H, T)]
    gather(offsets, terms, grads, 0, 4, 2)
    later = []
    center = [
        copies.start(ring_out, ring_up, down),
        copies.start(grads.at[:, pl.ds(0, RING), MIDDLE], from_down.at[:, :, MIDDLE], up),
    ]

    def send_piece(k):
        c, first = PIECES[k]
        center.append(
            copies.start(
                grads.at[c, pl.ds(T + first, HALF), MIDDLE],
                from_up.at[c, pl.ds(RING + first, HALF), MIDDLE],
                down,
            )
        )

    probe_sum.start_y()
    for k in range(4):
        send_piece(k)
    gather(offsets, terms, grads, 1, 1, 3)
    inside = pl.ds(RING, X)
    columns_as_rows(
        [grads[c, :, T - 1 : T] for c in range(2)]
        + [grads[c, :, 0:1] for c in range(2)]
        + [grads[c, :, T : T + 1] for c in range(2)]
        + [canvas[c, inside, H + T - 1 : H + T] for c in range(2)],
        lines,
    )
    center.append(
        copies.start(
            grads.at[:, pl.ds(T - RING, RING), MIDDLE], from_up.at[:, pl.ds(0, RING), MIDDLE], down
        )
    )
    later.append(copies.start(lines, lines_up.at[2], down))
    line_copies = [
        copies.start(lines, lines_lr.at[0], right),
        copies.start(lines, lines_lr.at[1], left),
    ]
    side = copies.start(grads.at[:, :, pl.ds(T, H)], from_left, right)
    probe_sum.start_rows()
    count = start_table(starts)
    square[...] = probe[0] * probe[0] + probe[1] * probe[1]

    def rows_of(by):
        if by in (-1, 4):
            return (0, RING, H - RING) if by == -1 else (RING + T, RING, 0)
        return RING + by * H, H, 0

    def prepare(by, bx):
        at, size, first = rows_of(by)
        inverse[pl.ds(at, size), pl.ds(H + bx * H, H)] = 1.0 / block_weight(
            count, square, by, bx, (first, size)
        )

    def update(by, bx, ring=None):
        at, size, _ = rows_of(by)
        cols = pl.ds(H + bx * H, H)
        scale = inverse[pl.ds(at, size), cols]
        block = pl.ds(max(bx, 0) * H, H)
        for c in range(2):
            base = canvas[c, pl.ds(at, size), cols]
            if bx == -1:
                grad = jnp.broadcast_to(ring[:, c : c + 1], (H, H))
                base = jnp.broadcast_to(ring[:, 4 + c : 5 + c], (H, H))
            elif bx == 4:
                grad = jnp.broadcast_to(ring[:, 2 + c : 3 + c], (H, H))
                grad = grad + grads[c, pl.ds(by * H, H), block]
            elif by == -1:
                base = ring_up[c, :, block]
                grad = from_up[c, 0:RING, block]
            else:
                grad = grads[c, pl.ds(by * H, size), block]
                if by == 0:
                    grad = grad + from_up[c, RING:STRIP, block]
                if by == 4:
                    grad = grad + from_down[c, :, block]
                if bx == 0:
                    grad = grad + from_left[c, pl.ds(by * H, size), :]
            canvas[c, pl.ds(at, size), cols] = base + grad * scale

    leaving = []

    def smooth(by):
        rows = pl.ds(by * H, H)
        for c in range(2):
            around_sum, center_now = shifted_sum(canvas, c, RING + by * H, H, T)
            obj_now[c, rows, :] = center_now + rate[rows, 0:T] * (around_sum - 4.0 * center_now)
        copy = pltpu.make_async_copy(
            obj_now.at[:, rows, :], obj_out.at[:, rows, :], out_sems.at[by]
        )
        copy.start()
        leaving.append(copy)

    for by in (1, 2, 3):
        for bx in (1, 2, 3):
            prepare(by, bx)
            update(by, bx)
    for by in range(-1, 5):
        for bx in range(-1, 5):
            if not (by in (1, 2, 3) and bx in (1, 2, 3) or by in (-1, 4) and bx in (-1, 4)):
                prepare(by, bx)
    probe_sum.start_back()
    side.wait_recv()
    for copy in line_copies:
        copy.wait_recv()
    corner_down[...] = (
        grads[:, pl.ds(X - STRIP, STRIP), pl.ds(0, H)] + from_left[:, pl.ds(X - STRIP, STRIP), :]
    )
    corner_up[...] = grads[:, pl.ds(0, RING), pl.ds(0, H)] + from_left[:, pl.ds(0, RING), :]
    later += [
        copies.start(lines_lr, lines_up.at[pl.ds(0, 2)], down),
        copies.start(corner_down, from_up.at[:, :, pl.ds(0, H)], down),
        copies.start(corner_up, from_down.at[:, :, pl.ds(0, H)], up),
    ]
    for by in (1, 2, 3):
        update(by, 0)
    probe_sum.start_back_y()
    for copy in center:
        copy.wait_recv()
    for by in (-1, 0, 4):
        for bx in (1, 2, 3):
            update(by, bx)
    rows = [lines_lr[0, c : c + 1] for c in range(2)]
    rows += [lines_lr[1, 2 + c : 3 + c] for c in range(2)]
    rows += [lines_lr[0, 6 + c : 7 + c] for c in range(2)]
    ring = spread_lines(rows)
    for by in (1, 2, 3):
        for bx in (-1, 4):
            update(by, bx, ring[by * H : (by + 1) * H])
    blank_sides(canvas, H + T, RING + H, 3 * H)
    smooth(2)
    probe_sum.start_back_pair()
    for copy in later:
        copy.wait_recv()
    far = [rows[c][:, :H] + lines_up[0, c : c + 1, T:] for c in range(2)]
    far += [
        rows[2 + c][:, :H] + lines_up[1, 2 + c : 3 + c, T:] + lines_up[2, 4 + c : 5 + c, T:]
        for c in range(2)
    ]
    far += [rows[4 + c][:, :H] for c in range(2)]
    ring = spread_lines(far)
    update(0, 0)
    for bx in (-1, 4):
        update(0, bx, ring)
    for by in (-1, 4):
        update(by, 0)
    blank_outside(canvas, RING + T, H + T)
    for by in (0, 1, 3):
        smooth(by)
    probe_sum.end()
    unpack_probe(tiles, probe_out)
    for copy in leaving:
        copy.wait()
    copies.finish()


def whole_kernel(
    obj, probe_in, amps_in, offsets, live, classes_in, weights, right_table, left_table,
    obj_out, probe_out,
    canvas, canvas_next, terms, grads, sums, probe, probe_next, amps, classes, class_down,
    class_right, rate, inverse, obj_now, square, counted, starts_in, starts, lines, ring_out, ring_up, corners, corner_down,
    corner_up, tiles, tiles_last, part, y_part, *refs
):
    landing, landing_last, (sems, out_sems, send_sems, recv_sems) = refs[:10], refs[10:18], refs[18:]
    up, down, left, right = around()
    row, col = lax.axis_index("row"), lax.axis_index("col")
    copies = Copies(send_sems, recv_sems)
    probe_sum = ProbeSum(
        copies, sums, probe, tiles, landing[7], part, landing[8], y_part, landing[9]
    )
    probe_sum_last = ProbeSum(
        copies, sums, probe_next, tiles_last, landing_last[5], part, landing_last[6], y_part,
        landing_last[7],
    )
    near = {
        (dr, dc): (lax.rem(row + dr + 16, 16), lax.rem(col + dc + 8, 8))
        for dr in (-1, 0, 1)
        for dc in (-1, 0, 1)
        if (dr, dc) != (0, 0)
    }
    pairs = [
        (obj, canvas.at[:, pl.ds(RING, T), pl.ds(H, T)]),
        (probe_in, probe),
        (amps_in, amps),
        (classes_in, classes),
    ]
    own = [pltpu.make_async_copy(src, dst, sems.at[k]) for k, (src, dst) in enumerate(pairs)]
    for copy in own:
        copy.start()
    count_starts(offsets, live, counted)
    greet([device for (dr, dc), device in near.items() if dc != 0] + probe_sum.peers())
    rows = copies.start(
        obj.at[:, pl.ds(0, STRIP), :], canvas.at[:, pl.ds(RING + T, STRIP), pl.ds(H, T)], up
    )
    beside = copies.start(
        obj.at[:, :, pl.ds(0, H)], canvas.at[:, pl.ds(RING, T), pl.ds(H + T, H)], left
    )
    class_beside = copies.start(classes_in.at[:, pl.ds(0, H)], class_right, left)
    strips = [
        rows,
        copies.start(
            obj.at[:, pl.ds(T - RING, RING), :], canvas.at[:, pl.ds(0, RING), pl.ds(H, T)], down
        ),
    ]
    small = [
        copies.start(counted, starts_in.at[1 - dr, 1 - dc], device)
        for (dr, dc), device in near.items()
    ]
    starts_in[1, 1] = counted[...]
    frame_terms(terms)
    own[3].wait()
    rate[0:T, 0:T] = rates(classes[...], weights)
    beside.wait_recv()
    corner = [
        copies.start(
            canvas.at[:, pl.ds(RING, STRIP), pl.ds(H + T, H)],
            canvas.at[:, pl.ds(RING + T, STRIP), pl.ds(H + T, H)],
            up,
        ),
        copies.start(
            canvas.at[:, pl.ds(T, RING), pl.ds(H + T, H)],
            canvas.at[:, pl.ds(0, RING), pl.ds(H + T, H)],
            down,
        ),
    ]
    class_beside.wait_recv()
    class_later = [
        copies.start(classes_in.at[pl.ds(0, H), :], class_down.at[:, pl.ds(0, T)], up),
        copies.start(class_right.at[pl.ds(0, H), :], class_down.at[:, pl.ds(T, H)], up),
    ]
    for copy in own[:3]:
        copy.wait()
    for copy in small:
        copy.wait_recv()
    to_scalars = pltpu.make_async_copy(starts_in, starts, sems.at[4])
    to_scalars.start()
    for copy in strips + corner:
        copy.wait_recv()
    to_scalars.wait()
    visit_slots(canvas, probe, amps, offsets, live, right_table, left_table, terms, sums)
    for copy in class_later:
        copy.wait_recv()
    rate[0:T, T:X] = rates(class_right[...], weights)
    rate[T:X, :] = rates(class_down[...], weights)
    copies.finish()
    middle_phase(
        copies, probe_sum, offsets, terms, grads, lines, rate, inverse, probe, starts, canvas, canvas_next, probe_next, square, corners, tiles, *landing[:7],
    )
    visit_slots(
        canvas_next, probe_next, amps, offsets, live, right_table, left_table, terms, sums
    )
    last_phase(
        copies, probe_sum_last, offsets, terms, grads, lines, rate, inverse, probe_next, starts,
        canvas_next, ring_out, ring_up, obj_now, obj_out, out_sems, probe_out, square, corner_down, corner_up, tiles_last,
        *landing_last[:5],
    )
    assert copies.count == send_sems.shape[0]


PROBE_LANDING = [
    pltpu.VMEM((32, 3, 8, H), F32),
    pltpu.VMEM((3, 8, 3, 8, H), F32),
    pltpu.VMEM((16, 3, 8, H), F32),
]
COPIES = 16 + 2 * PROBE_COPIES + 22 + 14


def whole(obj, probe, amps, offsets, live, classes, weights, right, left):
    wide = (2, X + 2 * RING, X + 2 * H)
    scratch = [
        pltpu.VMEM(wide, F32),
        pltpu.VMEM(wide, F32),
        pltpu.VMEM((8, 2, 2 * S, 2 * S), F32),
        pltpu.VMEM((2, X, X), F32),
        pltpu.VMEM((2, 32, 3, 8, H), F32),
        pltpu.VMEM((2, S, S), F32),
        pltpu.VMEM((2, S, S), F32),
        pltpu.VMEM((8, S, S), BF16),
        pltpu.VMEM((T, T), jnp.int32),
        pltpu.VMEM((H, X), jnp.int32),
        pltpu.VMEM((T, H), jnp.int32),
        pltpu.VMEM((X, X), F32),
        pltpu.VMEM(wide[1:], F32),
        pltpu.VMEM((2, T, T), F32),
        pltpu.VMEM((S, S), F32),
        pltpu.VMEM((8, H), F32),
        pltpu.VMEM((3, 3, 8, H), F32),
        pltpu.SMEM((3, 3, 8, H), F32),
        pltpu.VMEM((8, X), F32),
        pltpu.VMEM((2, RING, T), F32),
        pltpu.VMEM((2, RING, T), F32),
        pltpu.VMEM((4, 2, STRIP, H), F32),
        pltpu.VMEM((2, STRIP, H), F32),
        pltpu.VMEM((2, RING, H), F32),
        pltpu.VMEM((2, 32, 2, 8, H), F32),
        pltpu.VMEM((2, 32, 2, 8, H), F32),
        pltpu.VMEM((32, 3, 8, H), F32),
        pltpu.VMEM((8, 3, 8, H), F32),
    ]
    landing = [
        pltpu.VMEM((2, X, H), F32),
        pltpu.VMEM((2, X, H), F32),
        pltpu.VMEM((2, STRIP, X), F32),
        pltpu.VMEM((2, STRIP, X), F32),
        pltpu.VMEM((2, 8, X), F32),
        pltpu.VMEM((3, 8, X), F32),
        pltpu.VMEM((3, 8, X), F32),
    ] + PROBE_LANDING
    landing_last = [
        pltpu.VMEM((2, X, H), F32),
        pltpu.VMEM((2, STRIP, T), F32),
        pltpu.VMEM((2, RING, T), F32),
        pltpu.VMEM((2, 8, X), F32),
        pltpu.VMEM((3, 8, X), F32),
    ] + PROBE_LANDING
    return pl.pallas_call(
        whole_kernel,
        name="reconstruct",
        out_shape=[
            jax.ShapeDtypeStruct((2, T, T), F32),
            jax.ShapeDtypeStruct((2, S, S), F32),
        ],
        in_specs=[ANY, ANY, ANY, SMEM, SMEM, ANY, SMEM, VMEM, VMEM],
        out_specs=[ANY, VMEM],
        scratch_shapes=scratch
        + landing
        + landing_last
        + [
            pltpu.SemaphoreType.DMA((5,)),
            pltpu.SemaphoreType.DMA((4,)),
            pltpu.SemaphoreType.DMA((COPIES,)),
            pltpu.SemaphoreType.DMA((COPIES,)),
        ],
        compiler_params=pltpu.CompilerParams(
            collective_id=0, has_side_effects=True, vmem_limit_bytes=VMEM_BYTES
        ),
    )(obj, probe, amps, offsets, live, classes, weights, right, left)


def hand_over_kernel(obj, probe, obj_out, probe_out, held, held_probe, in_sems, out_sems):
    pairs = [(probe, held_probe, probe_out)]
    for c in range(2):
        for first in range(0, T, H):
            rows = pl.ds(first, H)
            pairs.append((obj.at[c, rows, :], held.at[c, rows, :], obj_out.at[c, rows, :]))
    arriving = [
        pltpu.make_async_copy(src, mid, in_sems.at[k]) for k, (src, mid, _) in enumerate(pairs)
    ]
    leaving = [
        pltpu.make_async_copy(mid, dst, out_sems.at[k]) for k, (_, mid, dst) in enumerate(pairs)
    ]
    for copy in arriving:
        copy.start()
    for first, second in zip(arriving, leaving):
        first.wait()
        second.start()
    for copy in leaving:
        copy.wait()


def hand_over(obj, probe):
    return pl.pallas_call(
        hand_over_kernel,
        name="hand_over",
        out_shape=[
            jax.ShapeDtypeStruct((2, T, T), F32),
            jax.ShapeDtypeStruct((2, S, S), F32),
        ],
        in_specs=[ANY, ANY],
        out_specs=[ANY, ANY],
        scratch_shapes=[
            pltpu.VMEM((2, T, T), F32),
            pltpu.VMEM((2, S, S), F32),
            pltpu.SemaphoreType.DMA((9,)),
            pltpu.SemaphoreType.DMA((9,)),
        ],
        compiler_params=pltpu.CompilerParams(vmem_limit_bytes=VMEM_BYTES),
    )(obj, probe)


def per_device(
    object_init, probe_init, amplitudes, scan_offsets, live_count, smooth_class, class_weight
):
    right, left = (jnp.asarray(table) for table in dft_blocks())
    return tuple(
        hand_over(
            *whole(
                object_init,
                probe_init,
                amplitudes.reshape(8, S, S),
                scan_offsets.reshape(8, 2).T,
                live_count,
                smooth_class,
                class_weight,
                right,
                left,
            )
        )
    )


def solution(mesh):
    in_specs = (
        P(None, "row", "col"),
        P(),
        P("row", "col", None, None, None),
        P("row", "col", None, None),
        P("row", "col"),
        P("row", "col"),
        P(),
    )
    out_specs = (P(None, "row", "col"), P())
    return jax.shard_map(
        per_device, mesh=mesh, in_specs=in_specs, out_specs=out_specs, check_vma=False
    )
```

```python
import math

import jax
import jax.numpy as jnp
import ml_dtypes
import numpy as np
from jax import lax
from jax.experimental import pallas as pl
from jax.experimental.pallas import tpu as pltpu
from jax.sharding import PartitionSpec as P

F32 = jnp.float32
BF16 = jnp.bfloat16
T = 512
S = 256
H = 128
X = T + H
RING = 8
STRIP = H + RING
MESH = pl.DeviceIdType.MESH
ANY = pl.BlockSpec(memory_space=pl.ANY)
VMEM = pl.BlockSpec(memory_space=pltpu.VMEM)
SMEM = pl.BlockSpec(memory_space=pltpu.SMEM)
VMEM_BYTES = 64 * 1024 * 1024


def dft_blocks():
    index = np.arange(S)
    phases = 2.0 * math.pi / S * (index[:, None] * index[None, :] % S)
    re = (np.cos(phases) / math.sqrt(S)).astype(ml_dtypes.bfloat16)
    im = (-np.sin(phases) / math.sqrt(S)).astype(ml_dtypes.bfloat16)
    right = np.block([[re, im], [-im, re]])
    left = np.block([[re, -im], [im, re]])
    return right, left


class Copies:
    def __init__(self, send_sems, recv_sems):
        self.send_sems, self.recv_sems, self.count = send_sems, recv_sems, 0
        self.started = []

    def make(self, src, dst, device):
        k = self.count
        self.count += 1
        return pltpu.make_async_remote_copy(
            src_ref=src,
            dst_ref=dst,
            send_sem=self.send_sems.at[k],
            recv_sem=self.recv_sems.at[k],
            device_id=device,
            device_id_type=MESH,
        )

    def start(self, src, dst, device):
        copy = self.make(src, dst, device)
        copy.start()
        self.started.append(copy)
        return copy

    def finish(self):
        for copy in self.started:
            copy.wait_send()
        self.started = []


def around():
    row, col = lax.axis_index("row"), lax.axis_index("col")
    up = (lax.rem(row + 15, 16), col)
    down = (lax.rem(row + 1, 16), col)
    left = (row, lax.rem(col + 7, 8))
    right = (row, lax.rem(col + 1, 8))
    return up, down, left, right


def greet(devices):
    barrier = pltpu.get_barrier_semaphore()
    for device in devices:
        pl.semaphore_signal(barrier, inc=1, device_id=device, device_id_type=MESH)
    pl.semaphore_wait(barrier, len(devices))


def count_starts(offsets, live, out):
    lane = lax.broadcasted_iota(jnp.int32, (8, H), 1)
    row0 = lax.axis_index("row") * T
    col0 = lax.axis_index("col") * T
    found = jnp.zeros((8, H), F32)
    for slot in range(8):
        at = lax.div(offsets[0, slot] - row0, H) * 4 + lax.div(offsets[1, slot] - col0, H)
        found += jnp.where((lane == at) & (live[0, 0] > slot), 1.0, 0.0)
    out[...] = found


def dot(a, b):
    return jnp.dot(a, b, preferred_element_type=F32)


def side_by_side(re, im):
    return jnp.concatenate([re.astype(BF16), im.astype(BF16)], 1)


def stacked(both):
    both = both.astype(BF16)
    return jnp.concatenate([both[:, :S], both[:, S:]], 0)


def start_block(offsets, slot):
    by = lax.div(offsets[0, slot] - lax.axis_index("row") * T, H)
    bx = lax.div(offsets[1, slot] - lax.axis_index("col") * T, H)
    return jnp.clip(by, 0, 3), jnp.clip(bx, 0, 3)


def visit_slots(canvas, probe, amps, offsets, live, right, left, terms, sums):
    sums[...] = jnp.zeros_like(sums)

    def some(step, carry):
        slots = [4 * step + k for k in range(4)]
        places = []
        for slot in slots:
            by, bx = start_block(offsets, slot)
            places.append((pl.ds(by * H + RING, S), pl.ds(bx * H + H, S)))

        def leaving(rows, cols):
            probe_re, probe_im = probe[0], probe[1]
            patch_re, patch_im = canvas[0, rows, cols], canvas[1, rows, cols]
            return side_by_side(
                probe_re * patch_re - probe_im * patch_im,
                probe_re * patch_im + probe_im * patch_re,
            )

        def corrected(slot, far):
            far_re, far_im = far[:S], far[S:]
            square = far_re * far_re + far_im * far_im
            factor = amps[slot].astype(F32) * lax.rsqrt(jnp.maximum(square, 1.0)) - 1.0
            return side_by_side(far_re * factor, far_im * factor)

        waves = [leaving(rows, cols) for rows, cols in places]
        waves = [stacked(dot(wave, right[...])) for wave in waves]
        waves = [dot(left[...], wave) for wave in waves]
        waves = [corrected(slot, wave) for slot, wave in zip(slots, waves)]
        waves = [stacked(dot(wave, left[...])) for wave in waves]
        waves = [dot(right[...], wave) for wave in waves]
        inner = pl.ds(H, S)
        grads = [0.0, 0.0, 0.0]
        for slot, (rows, cols), diff in zip(slots, places, waves):
            mask = jnp.where(jnp.broadcast_to(live[0, 0], (1, S)) > slot, 1.0, 0.0)
            probe_re, probe_im = probe[0], probe[1]
            patch_re, patch_im = canvas[0, rows, cols], canvas[1, rows, cols]
            diff_re, diff_im = diff[:S] * mask, diff[S:] * mask
            terms[slot, 0, inner, inner] = probe_re * diff_re + probe_im * diff_im
            terms[slot, 1, inner, inner] = probe_re * diff_im - probe_im * diff_re
            grads[0] += patch_re * diff_re + patch_im * diff_im
            grads[1] += patch_re * diff_im - patch_im * diff_re
            grads[2] += (patch_re * patch_re + patch_im * patch_im) * mask
        for c in range(3):
            for ct in range(2):
                sums[ct, :, c] += grads[c][:, ct * H : (ct + 1) * H].reshape(32, 8, H)
        return carry

    lax.fori_loop(0, 2, some, 0)


def gather(offsets, terms, deposits, first, step, count):
    starts_at = [start_block(offsets, slot) for slot in range(8)]

    def one(block, carry):
        by, bx = first + lax.div(block, 5) * step, lax.rem(block, 5)
        total = [None, None]
        for slot in range(8):
            y = jnp.clip(by - starts_at[slot][0], -1, 2) * H + H
            x = jnp.clip(bx - starts_at[slot][1], -1, 2) * H + H
            for c in range(2):
                part = terms[slot, c, pl.ds(y, H), pl.ds(x, H)]
                total[c] = part if slot == 0 else total[c] + part
        for c in range(2):
            deposits[
                c, pl.ds(pl.multiple_of(by * H, H), H), pl.ds(pl.multiple_of(bx * H, H), H)
            ] = total[c]
        return carry

    lax.fori_loop(0, 5 * count, one, 0)


def frame_terms(terms):
    for slot in range(8):
        terms[slot, :, 0:H, :] = jnp.zeros((2, H, 2 * S), F32)
        terms[slot, :, S + H :, :] = jnp.zeros((2, H, 2 * S), F32)
        terms[slot, :, H : S + H, 0:H] = jnp.zeros((2, S, H), F32)
        terms[slot, :, H : S + H, S + H :] = jnp.zeros((2, S, H), F32)


def columns_as_rows(columns, out):
    lane = lax.broadcasted_iota(jnp.int32, (X, H), 1)
    gathered = jnp.zeros((X, H), F32)
    for k, column in enumerate(columns):
        gathered = jnp.where(lane == k, column, gathered)
    out[...] = gathered.T[:8]


class ProbeSum:
    def __init__(self, copies, sums, probe, out, pair_in, part, y_in, y_part, rows_in):
        self.row, col = lax.axis_index("row"), lax.axis_index("col")
        self.y, self.core = col // 2, lax.rem(col, 2)
        self.tile = lax.rem(self.row, 8)
        self.copies, self.sums, self.probe, self.out = copies, sums, probe, out
        self.pair_in, self.part, self.y_in, self.y_part = pair_in, part, y_in, y_part
        self.rows_in = rows_in
        self.col = col
        self.other = (self.row, self.y * 2 + 1 - self.core)
        self.y_peers = [
            (self.row, lax.rem(self.y + k, 4) * 2 + self.core) for k in range(1, 4)
        ]
        self.row_peers = [(lax.rem(self.row + k, 16), col) for k in range(1, 16)]

    def peers(self):
        return self.y_peers + self.row_peers

    def start_pair(self):
        self.pair = self.copies.start(self.sums.at[1 - self.core], self.pair_in, self.other)

    def start_y(self):
        self.pair.wait_recv()
        self.part[...] = self.sums[self.core] + self.pair_in[...]
        self.y_sent = []
        for k in range(1, 4):
            at = lax.rem(self.y + k, 4) * 8
            self.y_sent.append(
                self.copies.start(
                    self.part.at[pl.ds(at, 8)], self.y_in.at[k - 1], self.y_peers[k - 1]
                )
            )

    def start_rows(self):
        for copy in self.y_sent:
            copy.wait_recv()
        self.y_part[...] = (
            self.part[pl.ds(self.y * 8, 8)] + self.y_in[0] + self.y_in[1] + self.y_in[2]
        )
        self.rows_in[self.row] = self.y_part[self.tile]
        for k in range(1, 16):
            tile = lax.rem(self.row + k, 8)
            self.copies.start(
                self.y_part.at[tile], self.rows_in.at[self.row], self.row_peers[k - 1]
            )
        self.first = self.copies.count - 15

    def landed(self, ref, number):
        pltpu.make_async_remote_copy(
            src_ref=ref,
            dst_ref=ref,
            send_sem=self.copies.send_sems.at[number],
            recv_sem=self.copies.recv_sems.at[number],
            device_id=self.other,
            device_id_type=MESH,
        ).wait_recv()

    def start_back(self):
        for k in range(1, 16):
            self.landed(self.rows_in.at[lax.rem(self.row + 16 - k, 16)], self.first + k - 1)
        total = self.rows_in[0]
        for k in range(1, 16):
            total = total + self.rows_in[k]
        rt = self.y * 8 + self.tile
        rows, cols = pl.ds(pl.multiple_of(rt * 8, 8), 8), pl.ds(pl.multiple_of(self.core * H, H), H)
        inverse = 1.0 / (total[2] + 1.0)
        for c in range(2):
            self.out[self.core, rt, c] = self.probe[c, rows, cols] + total[c] * inverse
        mine = self.out.at[self.core, rt]
        group = self.row // 8 * 8
        self.first = self.copies.count
        for k in range(1, 8):
            self.copies.start(mine, mine, (group + lax.rem(self.tile + k, 8), self.col))

    def start_back_y(self):
        for k in range(1, 8):
            tile = lax.rem(self.tile + 8 - k, 8)
            self.landed(self.out.at[self.core, self.y * 8 + tile], self.first + k - 1)
        mine = self.out.at[self.core, pl.ds(self.y * 8, 8)]
        self.first = self.copies.count
        for k in range(1, 4):
            self.copies.start(mine, mine, self.y_peers[k - 1])

    def start_back_pair(self):
        for k in range(1, 4):
            at = lax.rem(self.y + 4 - k, 4) * 8
            self.landed(self.out.at[self.core, pl.ds(at, 8)], self.first + k - 1)
        mine = self.out.at[self.core]
        self.first = self.copies.count
        self.copies.start(mine, mine, self.other)

    def end(self):
        self.landed(self.out.at[1 - self.core], self.first)


PROBE_COPIES = 1 + 3 + 15 + 7 + 3 + 1


def start_table(starts):
    def count(by, bx):
        return starts[by // 4 + 1, bx // 4 + 1, 0, by % 4 * 4 + bx % 4]

    return count


def block_weight(count, square, by, bx, rows):
    first, size = rows
    total = 1.0
    for qy in range(2):
        for qx in range(2):
            total = total + count(by - qy, bx - qx) * square[
                pl.ds(qy * H + first, size), pl.ds(qx * H, H)
            ]
    return total


def spread_lines(rows):
    length = rows[0].shape[1]
    packed = jnp.concatenate(rows + [jnp.zeros((H - len(rows), length), F32)], 0)
    return packed.T


def shifted_sum(canvas, c, first, rows, cols):
    width = cols + 2 * H
    whole = canvas[c, pl.ds(first, rows), pl.ds(0, width)]
    left = pltpu.roll(whole, 1, 1)[:, H : H + cols]
    right = pltpu.roll(whole, width - 1, 1)[:, H : H + cols]
    above = canvas[c, pl.ds(first - 1, rows), pl.ds(H, cols)]
    below = canvas[c, pl.ds(first + 1, rows), pl.ds(H, cols)]
    return below + above + right + left, whole[:, H : H + cols]


def rates(classes, weights):
    value = jnp.full(classes.shape, weights[0], F32)
    for k in range(1, 4):
        value = jnp.where(classes == k, weights[k], value)
    return value


def blank_sides(canvas, cols_end, first, size):
    col = lax.axis_index("col")
    width = canvas.shape[2]

    @pl.when(col == 0)
    def _():
        canvas[:, pl.ds(first, size), 0:H] = jnp.zeros((2, size, H), F32)

    @pl.when(col == 7)
    def _():
        canvas[:, pl.ds(first, size), cols_end:] = jnp.zeros((2, size, width - cols_end), F32)


def blank_outside(canvas, rows_end, cols_end):
    row = lax.axis_index("row")
    _, height, width = canvas.shape

    @pl.when(row == 0)
    def _():
        canvas[:, 0:RING, :] = jnp.zeros((2, RING, width), F32)

    @pl.when(row == 15)
    def _():
        canvas[:, rows_end:, :] = jnp.zeros((2, height - rows_end, width), F32)

    blank_sides(canvas, cols_end, 0, height)


MIDDLE = pl.ds(H, T - H)
LINES = [(0, 0), (0, 1), (1, 2), (1, 3), (0, 4), (0, 5), (1, 6), (1, 7)]


def unpack_probe(tiles, out):
    for c in range(2):
        for ct in range(2):
            out[c, :, ct * H : (ct + 1) * H] = tiles[ct, :, c].reshape(S, H)


def middle_phase(
    copies, probe_sum, offsets, terms, grads, lines, rate, inverse, probe, starts,
    canvas, canvas_next, probe_next, square, corners, tiles,
    from_left, from_right, from_up, from_down, lines_lr, lines_up, lines_down,
):
    up, down, left, right = around()
    probe_sum.start_pair()
    gather(offsets, terms, grads, 0, 4, 2)
    later = []
    center = []

    probe_sum.start_y()
    center += [
        copies.start(
            grads.at[:, pl.ds(T, H), MIDDLE], from_up.at[:, pl.ds(RING, H), MIDDLE], down
        ),
        copies.start(grads.at[:, pl.ds(0, H), MIDDLE], from_down.at[:, pl.ds(0, H), MIDDLE], up),
    ]
    gather(offsets, terms, grads, 1, 1, 3)
    inside = pl.ds(RING, X)
    columns_as_rows(
        [grads[c, :, T - 1 : T] for c in range(2)]
        + [grads[c, :, H : H + 1] for c in range(2)]
        + [canvas[c, inside, H + T - 1 : H + T] for c in range(2)]
        + [canvas[c, inside, H + H : H + H + 1] for c in range(2)],
        lines,
    )
    center += [
        copies.start(
            grads.at[:, pl.ds(T - RING, RING), MIDDLE], from_up.at[:, pl.ds(0, RING), MIDDLE], down
        ),
        copies.start(
            grads.at[:, pl.ds(H, RING), MIDDLE], from_down.at[:, pl.ds(H, RING), MIDDLE], up
        ),
    ]
    later += [
        copies.start(lines, lines_up.at[2], down),
        copies.start(lines, lines_down.at[2], up),
    ]
    side = [
        copies.start(lines, lines_lr.at[0], right),
        copies.start(lines, lines_lr.at[1], left),
    ]
    for at in (pl.ds(0, STRIP), pl.ds(X - STRIP, STRIP)):
        side.append(
            copies.start(grads.at[:, at, pl.ds(T, H)], from_left.at[:, at, :], right)
        )
        side.append(
            copies.start(grads.at[:, at, pl.ds(0, H)], from_right.at[:, at, :], left)
        )
    inner = pl.ds(STRIP, X - 2 * STRIP)
    side_inner = [
        copies.start(grads.at[:, inner, pl.ds(T, H)], from_left.at[:, inner, :], right),
        copies.start(grads.at[:, inner, pl.ds(0, H)], from_right.at[:, inner, :], left),
    ]
    probe_sum.start_rows()
    count = start_table(starts)
    square[...] = probe[0] * probe[0] + probe[1] * probe[1]

    def rows_of(by):
        if by in (-1, 5):
            return (0, RING, H - RING) if by == -1 else (RING + X, RING, 0)
        return RING + by * H, H, 0

    def prepare(by, bx):
        at, size, first = rows_of(by)
        inverse[pl.ds(at, size), pl.ds(H + bx * H, H)] = 1.0 / block_weight(
            count, square, by, bx, (first, size)
        )

    def update(by, bx, ring=None):
        at, size, _ = rows_of(by)
        edge = bx in (-1, 5)
        cols = pl.ds(H + bx * H, H)
        scale = inverse[pl.ds(at, size), cols]
        for c in range(2):
            if edge:
                k = 0 if bx == -1 else 2
                grad = jnp.broadcast_to(ring[:, k + c : k + c + 1], (H, H))
                base = jnp.broadcast_to(ring[:, k + 4 + c : k + 5 + c], (H, H))
            else:
                base = canvas[c, pl.ds(at, size), cols]
                block = pl.ds(bx * H, H)
                if by == -1:
                    grad = from_up[c, 0:RING, block]
                elif by == 5:
                    grad = from_down[c, H:STRIP, block]
                else:
                    grad = grads[c, pl.ds(by * H, H), block]
                    if by == 0:
                        grad = grad + from_up[c, RING:STRIP, block]
                    if by == 4:
                        grad = grad + from_down[c, 0:H, block]
                    if bx == 0:
                        grad = grad + from_left[c, pl.ds(by * H, H), :]
                    if bx == 4:
                        grad = grad + from_right[c, pl.ds(by * H, H), :]
            canvas[c, pl.ds(at, size), cols] = base + grad * scale

    def smooth(first, size):
        for c in range(2):
            around_sum, center_now = shifted_sum(canvas, c, RING + first, size, X)
            canvas_next[c, pl.ds(RING + first, size), pl.ds(H, X)] = center_now + rate[
                pl.ds(first, size), :
            ] * (around_sum - 4.0 * center_now)

    for by in (1, 2, 3):
        for bx in (1, 2, 3):
            prepare(by, bx)
            update(by, bx)
    for by in range(-1, 6):
        for bx in range(-1, 6):
            if not (by in (1, 2, 3) and bx in (1, 2, 3) or by in (-1, 5) and bx in (-1, 5)):
                prepare(by, bx)
    probe_sum.start_back()
    for copy in side:
        copy.wait_recv()
    for k, (first, source) in enumerate(
        ((0, from_left), (0, from_right), (X - STRIP, from_left), (X - STRIP, from_right))
    ):
        column = 0 if k % 2 == 0 else T
        corners[k] = (
            grads[:, pl.ds(first, STRIP), pl.ds(column, H)]
            + source[:, pl.ds(first, STRIP), :]
        )
    later += [
        copies.start(lines_lr, lines_up.at[pl.ds(0, 2)], down),
        copies.start(lines_lr, lines_down.at[pl.ds(0, 2)], up),
        copies.start(corners.at[0], from_down.at[:, :, pl.ds(0, H)], up),
        copies.start(corners.at[2], from_up.at[:, :, pl.ds(0, H)], down),
        copies.start(corners.at[1], from_down.at[:, :, pl.ds(T, H)], up),
        copies.start(corners.at[3], from_up.at[:, :, pl.ds(T, H)], down),
    ]
    for copy in side_inner:
        copy.wait_recv()
    for by in (1, 2, 3):
        update(by, 0)
        update(by, 4)
    probe_sum.start_back_y()
    for copy in center:
        copy.wait_recv()
    for by in (-1, 0, 4, 5):
        for bx in (1, 2, 3):
            update(by, bx)
    rows = [lines_lr[side_at, k : k + 1] for side_at, k in LINES]
    ring = spread_lines(rows)
    for by in (1, 2, 3):
        for bx in (-1, 5):
            update(by, bx, ring[by * H : (by + 1) * H])
    blank_sides(canvas, H + T, RING + H, 3 * H)
    for first, size in ((STRIP, H - RING), (2 * H, H), (3 * H, H - RING)):
        smooth(first, size)
    probe_sum.start_back_pair()
    for copy in later:
        copy.wait_recv()
    far = []
    for n, (side_at, k) in enumerate(LINES):
        above = lines_up[side_at, k : k + 1, T:]
        below_it = lines_down[side_at, k : k + 1, :H]
        if n < 4:
            pieces = [rows[n][:, :H] + above, rows[n][:, T:] + below_it]
        else:
            pieces = [rows[n][:, :H], below_it]
        far.append(jnp.concatenate(pieces, 1))
    ring = spread_lines(far)
    for by in (0, 4):
        for bx in (0, 4):
            update(by, bx)
        for bx in (-1, 5):
            update(by, bx, ring[:H] if by == 0 else ring[H:])
    for by in (-1, 5):
        for bx in (0, 4):
            update(by, bx)
    blank_outside(canvas, RING + T, H + T)
    for first in (0, X - STRIP):
        smooth(first, STRIP)
    probe_sum.end()
    unpack_probe(tiles, probe_next)
    copies.finish()


def last_phase(
    copies, probe_sum, offsets, terms, grads, lines, rate, inverse, probe, starts,
    canvas, ring_out, ring_up, obj_now, obj_out, out_sems, probe_out, square, corner_down, corner_up, tiles,
    from_left, from_up, from_down, lines_lr, lines_up,
):
    up, down, left, right = around()
    probe_sum.start_pair()
    ring_out[...] = canvas[:, pl.ds(T, RING), pl.ds(H, T)]
    gather(offsets, terms, grads, 0, 4, 2)
    later = []
    center = [
        copies.start(ring_out, ring_up, down),
        copies.start(grads.at[:, pl.ds(0, RING), MIDDLE], from_down.at[:, :, MIDDLE], up),
    ]

    probe_sum.start_y()
    center.append(
        copies.start(grads.at[:, pl.ds(T, H), MIDDLE], from_up.at[:, pl.ds(RING, H), MIDDLE], down)
    )
    gather(offsets, terms, grads, 1, 1, 3)
    inside = pl.ds(RING, X)
    columns_as_rows(
        [grads[c, :, T - 1 : T] for c in range(2)]
        + [grads[c, :, 0:1] for c in range(2)]
        + [grads[c, :, T : T + 1] for c in range(2)]
        + [canvas[c, inside, H + T - 1 : H + T] for c in range(2)],
        lines,
    )
    center.append(
        copies.start(
            grads.at[:, pl.ds(T - RING, RING), MIDDLE], from_up.at[:, pl.ds(0, RING), MIDDLE], down
        )
    )
    later.append(copies.start(lines, lines_up.at[2], down))
    line_copies = [
        copies.start(lines, lines_lr.at[0], right),
        copies.start(lines, lines_lr.at[1], left),
    ]
    side = [
        copies.start(grads.at[:, at, pl.ds(T, H)], from_left.at[:, at, :], right)
        for at in (pl.ds(0, RING), pl.ds(X - STRIP, STRIP), pl.ds(RING, X - STRIP - RING))
    ]
    probe_sum.start_rows()
    count = start_table(starts)
    square[...] = probe[0] * probe[0] + probe[1] * probe[1]

    def rows_of(by):
        if by in (-1, 4):
            return (0, RING, H - RING) if by == -1 else (RING + T, RING, 0)
        return RING + by * H, H, 0

    def prepare(by, bx):
        at, size, first = rows_of(by)
        inverse[pl.ds(at, size), pl.ds(H + bx * H, H)] = 1.0 / block_weight(
            count, square, by, bx, (first, size)
        )

    def update(by, bx, ring=None):
        at, size, _ = rows_of(by)
        cols = pl.ds(H + bx * H, H)
        scale = inverse[pl.ds(at, size), cols]
        block = pl.ds(max(bx, 0) * H, H)
        for c in range(2):
            base = canvas[c, pl.ds(at, size), cols]
            if bx == -1:
                grad = jnp.broadcast_to(ring[:, c : c + 1], (H, H))
                base = jnp.broadcast_to(ring[:, 4 + c : 5 + c], (H, H))
            elif bx == 4:
                grad = jnp.broadcast_to(ring[:, 2 + c : 3 + c], (H, H))
                grad = grad + grads[c, pl.ds(by * H, H), block]
            elif by == -1:
                base = ring_up[c, :, block]
                grad = from_up[c, 0:RING, block]
            else:
                grad = grads[c, pl.ds(by * H, size), block]
                if by == 0:
                    grad = grad + from_up[c, RING:STRIP, block]
                if by == 4:
                    grad = grad + from_down[c, :, block]
                if bx == 0:
                    grad = grad + from_left[c, pl.ds(by * H, size), :]
            canvas[c, pl.ds(at, size), cols] = base + grad * scale

    leaving = []

    def smooth(first, size):
        rows = pl.ds(first, size)
        for c in range(2):
            around_sum, center_now = shifted_sum(canvas, c, RING + first, size, T)
            obj_now[c, rows, :] = center_now + rate[rows, 0:T] * (around_sum - 4.0 * center_now)
        copy = pltpu.make_async_copy(
            obj_now.at[:, rows, :], obj_out.at[:, rows, :], out_sems.at[len(leaving)]
        )
        copy.start()
        leaving.append(copy)

    for by in (1, 2, 3):
        for bx in (1, 2, 3):
            prepare(by, bx)
            update(by, bx)
    for by in range(-1, 5):
        for bx in range(-1, 5):
            if not (by in (1, 2, 3) and bx in (1, 2, 3) or by in (-1, 4) and bx in (-1, 4)):
                prepare(by, bx)
    probe_sum.start_back()
    for copy in side[:2]:
        copy.wait_recv()
    for copy in line_copies:
        copy.wait_recv()
    corner_down[...] = (
        grads[:, pl.ds(X - STRIP, STRIP), pl.ds(0, H)] + from_left[:, pl.ds(X - STRIP, STRIP), :]
    )
    corner_up[...] = grads[:, pl.ds(0, RING), pl.ds(0, H)] + from_left[:, pl.ds(0, RING), :]
    later += [
        copies.start(lines_lr, lines_up.at[pl.ds(0, 2)], down),
        copies.start(corner_down, from_up.at[:, :, pl.ds(0, H)], down),
        copies.start(corner_up, from_down.at[:, :, pl.ds(0, H)], up),
    ]
    side[2].wait_recv()
    for by in (1, 2, 3):
        update(by, 0)
    probe_sum.start_back_y()
    for copy in center:
        copy.wait_recv()
    for by in (-1, 0, 4):
        for bx in (1, 2, 3):
            update(by, bx)
    rows = [lines_lr[0, c : c + 1] for c in range(2)]
    rows += [lines_lr[1, 2 + c : 3 + c] for c in range(2)]
    rows += [lines_lr[0, 6 + c : 7 + c] for c in range(2)]
    ring = spread_lines(rows)
    for by in (1, 2, 3):
        for bx in (-1, 4):
            update(by, bx, ring[by * H : (by + 1) * H])
    blank_sides(canvas, H + T, RING + H, 3 * H)
    for first, size in ((STRIP, H - RING), (2 * H, H), (3 * H, H - RING)):
        smooth(first, size)
    probe_sum.start_back_pair()
    for copy in later:
        copy.wait_recv()
    far = [rows[c][:, :H] + lines_up[0, c : c + 1, T:] for c in range(2)]
    far += [
        rows[2 + c][:, :H] + lines_up[1, 2 + c : 3 + c, T:] + lines_up[2, 4 + c : 5 + c, T:]
        for c in range(2)
    ]
    far += [rows[4 + c][:, :H] for c in range(2)]
    ring = spread_lines(far)
    update(0, 0)
    for bx in (-1, 4):
        update(0, bx, ring)
    for by in (-1, 4):
        update(by, 0)
    blank_outside(canvas, RING + T, H + T)
    smooth(0, STRIP)
    smooth(T - RING, RING)
    probe_sum.end()
    unpack_probe(tiles, probe_out)
    for copy in leaving:
        copy.wait()
    copies.finish()


def whole_kernel(
    obj, probe_in, amps_in, offsets, live, classes_in, weights, right_table, left_table,
    obj_out, probe_out,
    canvas, canvas_next, terms, grads, sums, probe, probe_next, amps, classes, class_down,
    class_right, rate, inverse, obj_now, square, counted, starts_in, starts, lines, ring_out, ring_up, corners, corner_down,
    corner_up, tiles, tiles_last, part, y_part, *refs
):
    landing, landing_last, (sems, out_sems, send_sems, recv_sems) = refs[:10], refs[10:18], refs[18:]
    up, down, left, right = around()
    row, col = lax.axis_index("row"), lax.axis_index("col")
    copies = Copies(send_sems, recv_sems)
    probe_sum = ProbeSum(
        copies, sums, probe, tiles, landing[7], part, landing[8], y_part, landing[9]
    )
    probe_sum_last = ProbeSum(
        copies, sums, probe_next, tiles_last, landing_last[5], part, landing_last[6], y_part,
        landing_last[7],
    )
    near = {
        (dr, dc): (lax.rem(row + dr + 16, 16), lax.rem(col + dc + 8, 8))
        for dr in (-1, 0, 1)
        for dc in (-1, 0, 1)
        if (dr, dc) != (0, 0)
    }
    pairs = [
        (obj, canvas.at[:, pl.ds(RING, T), pl.ds(H, T)]),
        (probe_in, probe),
        (amps_in, amps),
        (classes_in, classes),
    ]
    own = [pltpu.make_async_copy(src, dst, sems.at[k]) for k, (src, dst) in enumerate(pairs)]
    for copy in own:
        copy.start()
    count_starts(offsets, live, counted)
    greet([device for (dr, dc), device in near.items() if dc != 0] + probe_sum.peers())
    rows = copies.start(
        obj.at[:, pl.ds(0, STRIP), :], canvas.at[:, pl.ds(RING + T, STRIP), pl.ds(H, T)], up
    )
    beside = copies.start(
        obj.at[:, :, pl.ds(0, H)], canvas.at[:, pl.ds(RING, T), pl.ds(H + T, H)], left
    )
    class_beside = copies.start(classes_in.at[:, pl.ds(0, H)], class_right, left)
    strips = [
        rows,
        copies.start(
            obj.at[:, pl.ds(T - RING, RING), :], canvas.at[:, pl.ds(0, RING), pl.ds(H, T)], down
        ),
    ]
    small = [
        copies.start(counted, starts_in.at[1 - dr, 1 - dc], device)
        for (dr, dc), device in near.items()
    ]
    starts_in[1, 1] = counted[...]
    frame_terms(terms)
    own[3].wait()
    rate[0:T, 0:T] = rates(classes[...], weights)
    beside.wait_recv()
    corner = [
        copies.start(
            canvas.at[:, pl.ds(RING, STRIP), pl.ds(H + T, H)],
            canvas.at[:, pl.ds(RING + T, STRIP), pl.ds(H + T, H)],
            up,
        ),
        copies.start(
            canvas.at[:, pl.ds(T, RING), pl.ds(H + T, H)],
            canvas.at[:, pl.ds(0, RING), pl.ds(H + T, H)],
            down,
        ),
    ]
    class_beside.wait_recv()
    class_later = [
        copies.start(classes_in.at[pl.ds(0, H), :], class_down.at[:, pl.ds(0, T)], up),
        copies.start(class_right.at[pl.ds(0, H), :], class_down.at[:, pl.ds(T, H)], up),
    ]
    for copy in own[:3]:
        copy.wait()
    for copy in small:
        copy.wait_recv()
    to_scalars = pltpu.make_async_copy(starts_in, starts, sems.at[4])
    to_scalars.start()
    for copy in strips + corner:
        copy.wait_recv()
    to_scalars.wait()
    visit_slots(canvas, probe, amps, offsets, live, right_table, left_table, terms, sums)
    for copy in class_later:
        copy.wait_recv()
    rate[0:T, T:X] = rates(class_right[...], weights)
    rate[T:X, :] = rates(class_down[...], weights)
    copies.finish()
    middle_phase(
        copies, probe_sum, offsets, terms, grads, lines, rate, inverse, probe, starts, canvas, canvas_next, probe_next, square, corners, tiles, *landing[:7],
    )
    visit_slots(
        canvas_next, probe_next, amps, offsets, live, right_table, left_table, terms, sums
    )
    last_phase(
        copies, probe_sum_last, offsets, terms, grads, lines, rate, inverse, probe_next, starts,
        canvas_next, ring_out, ring_up, obj_now, obj_out, out_sems, probe_out, square, corner_down, corner_up, tiles_last,
        *landing_last[:5],
    )
    assert copies.count == send_sems.shape[0]


PROBE_LANDING = [
    pltpu.VMEM((32, 3, 8, H), F32),
    pltpu.VMEM((3, 8, 3, 8, H), F32),
    pltpu.VMEM((16, 3, 8, H), F32),
]
COPIES = 16 + 2 * PROBE_COPIES + 20 + 13


def whole(obj, probe, amps, offsets, live, classes, weights, right, left):
    wide = (2, X + 2 * RING, X + 2 * H)
    scratch = [
        pltpu.VMEM(wide, F32),
        pltpu.VMEM(wide, F32),
        pltpu.VMEM((8, 2, 2 * S, 2 * S), F32),
        pltpu.VMEM((2, X, X), F32),
        pltpu.VMEM((2, 32, 3, 8, H), F32),
        pltpu.VMEM((2, S, S), F32),
        pltpu.VMEM((2, S, S), F32),
        pltpu.VMEM((8, S, S), BF16),
        pltpu.VMEM((T, T), jnp.int32),
        pltpu.VMEM((H, X), jnp.int32),
        pltpu.VMEM((T, H), jnp.int32),
        pltpu.VMEM((X, X), F32),
        pltpu.VMEM(wide[1:], F32),
        pltpu.VMEM((2, T, T), F32),
        pltpu.VMEM((S, S), F32),
        pltpu.VMEM((8, H), F32),
        pltpu.VMEM((3, 3, 8, H), F32),
        pltpu.SMEM((3, 3, 8, H), F32),
        pltpu.VMEM((8, X), F32),
        pltpu.VMEM((2, RING, T), F32),
        pltpu.VMEM((2, RING, T), F32),
        pltpu.VMEM((4, 2, STRIP, H), F32),
        pltpu.VMEM((2, STRIP, H), F32),
        pltpu.VMEM((2, RING, H), F32),
        pltpu.VMEM((2, 32, 2, 8, H), F32),
        pltpu.VMEM((2, 32, 2, 8, H), F32),
        pltpu.VMEM((32, 3, 8, H), F32),
        pltpu.VMEM((8, 3, 8, H), F32),
    ]
    landing = [
        pltpu.VMEM((2, X, H), F32),
        pltpu.VMEM((2, X, H), F32),
        pltpu.VMEM((2, STRIP, X), F32),
        pltpu.VMEM((2, STRIP, X), F32),
        pltpu.VMEM((2, 8, X), F32),
        pltpu.VMEM((3, 8, X), F32),
        pltpu.VMEM((3, 8, X), F32),
    ] + PROBE_LANDING
    landing_last = [
        pltpu.VMEM((2, X, H), F32),
        pltpu.VMEM((2, STRIP, T), F32),
        pltpu.VMEM((2, RING, T), F32),
        pltpu.VMEM((2, 8, X), F32),
        pltpu.VMEM((3, 8, X), F32),
    ] + PROBE_LANDING
    return pl.pallas_call(
        whole_kernel,
        name="reconstruct",
        out_shape=[
            jax.ShapeDtypeStruct((2, T, T), F32),
            jax.ShapeDtypeStruct((2, S, S), F32),
        ],
        in_specs=[ANY, ANY, ANY, SMEM, SMEM, ANY, SMEM, VMEM, VMEM],
        out_specs=[ANY, VMEM],
        scratch_shapes=scratch
        + landing
        + landing_last
        + [
            pltpu.SemaphoreType.DMA((5,)),
            pltpu.SemaphoreType.DMA((5,)),
            pltpu.SemaphoreType.DMA((COPIES,)),
            pltpu.SemaphoreType.DMA((COPIES,)),
        ],
        compiler_params=pltpu.CompilerParams(
            collective_id=0, has_side_effects=True, vmem_limit_bytes=VMEM_BYTES
        ),
    )(obj, probe, amps, offsets, live, classes, weights, right, left)


def hand_over_kernel(obj, probe, obj_out, probe_out, held, held_probe, in_sems, out_sems):
    pairs = [(probe, held_probe, probe_out)]
    for c in range(2):
        for first in range(0, T, H):
            rows = pl.ds(first, H)
            pairs.append((obj.at[c, rows, :], held.at[c, rows, :], obj_out.at[c, rows, :]))
    arriving = [
        pltpu.make_async_copy(src, mid, in_sems.at[k]) for k, (src, mid, _) in enumerate(pairs)
    ]
    leaving = [
        pltpu.make_async_copy(mid, dst, out_sems.at[k]) for k, (_, mid, dst) in enumerate(pairs)
    ]
    for copy in arriving:
        copy.start()
    for first, second in zip(arriving, leaving):
        first.wait()
        second.start()
    for copy in leaving:
        copy.wait()


def hand_over(obj, probe):
    return pl.pallas_call(
        hand_over_kernel,
        name="hand_over",
        out_shape=[
            jax.ShapeDtypeStruct((2, T, T), F32),
            jax.ShapeDtypeStruct((2, S, S), F32),
        ],
        in_specs=[ANY, ANY],
        out_specs=[ANY, ANY],
        scratch_shapes=[
            pltpu.VMEM((2, T, T), F32),
            pltpu.VMEM((2, S, S), F32),
            pltpu.SemaphoreType.DMA((9,)),
            pltpu.SemaphoreType.DMA((9,)),
        ],
        compiler_params=pltpu.CompilerParams(vmem_limit_bytes=VMEM_BYTES),
    )(obj, probe)


def per_device(
    object_init, probe_init, amplitudes, scan_offsets, live_count, smooth_class, class_weight
):
    right, left = (jnp.asarray(table) for table in dft_blocks())
    return tuple(
        hand_over(
            *whole(
                object_init,
                probe_init,
                amplitudes.reshape(8, S, S),
                scan_offsets.reshape(8, 2).T,
                live_count,
                smooth_class,
                class_weight,
                right,
                left,
            )
        )
    )


def solution(mesh):
    in_specs = (
        P(None, "row", "col"),
        P(),
        P("row", "col", None, None, None),
        P("row", "col", None, None),
        P("row", "col"),
        P("row", "col"),
        P(),
    )
    out_specs = (P(None, "row", "col"), P())
    return jax.shard_map(
        per_device, mesh=mesh, in_specs=in_specs, out_specs=out_specs, check_vma=False
    )
```

```python
import math

import jax
import jax.numpy as jnp
import ml_dtypes
import numpy as np
from jax import lax
from jax.experimental import pallas as pl
from jax.experimental.pallas import tpu as pltpu
from jax.sharding import PartitionSpec as P

F32 = jnp.float32
BF16 = jnp.bfloat16
T = 512
S = 256
H = 128
X = T + H
RING = 8
STRIP = H + RING
MESH = pl.DeviceIdType.MESH
ANY = pl.BlockSpec(memory_space=pl.ANY)
VMEM = pl.BlockSpec(memory_space=pltpu.VMEM)
SMEM = pl.BlockSpec(memory_space=pltpu.SMEM)
VMEM_BYTES = 64 * 1024 * 1024


def dft_blocks():
    index = np.arange(S)
    phases = 2.0 * math.pi / S * (index[:, None] * index[None, :] % S)
    re = (np.cos(phases) / math.sqrt(S)).astype(ml_dtypes.bfloat16)
    im = (-np.sin(phases) / math.sqrt(S)).astype(ml_dtypes.bfloat16)
    right = np.block([[re, im], [-im, re]])
    left = np.block([[re, -im], [im, re]])
    return right, left


class Copies:
    def __init__(self, send_sems, recv_sems):
        self.send_sems, self.recv_sems, self.count = send_sems, recv_sems, 0
        self.started = []

    def make(self, src, dst, device):
        k = self.count
        self.count += 1
        return pltpu.make_async_remote_copy(
            src_ref=src,
            dst_ref=dst,
            send_sem=self.send_sems.at[k],
            recv_sem=self.recv_sems.at[k],
            device_id=device,
            device_id_type=MESH,
        )

    def start(self, src, dst, device):
        copy = self.make(src, dst, device)
        copy.start()
        self.started.append(copy)
        return copy

    def finish(self):
        for copy in self.started:
            copy.wait_send()
        self.started = []


def around():
    row, col = lax.axis_index("row"), lax.axis_index("col")
    up = (lax.rem(row + 15, 16), col)
    down = (lax.rem(row + 1, 16), col)
    left = (row, lax.rem(col + 7, 8))
    right = (row, lax.rem(col + 1, 8))
    return up, down, left, right


def greet(devices):
    barrier = pltpu.get_barrier_semaphore()
    for device in devices:
        pl.semaphore_signal(barrier, inc=1, device_id=device, device_id_type=MESH)
    pl.semaphore_wait(barrier, len(devices))


def count_starts(offsets, live, out):
    lane = lax.broadcasted_iota(jnp.int32, (8, H), 1)
    row0 = lax.axis_index("row") * T
    col0 = lax.axis_index("col") * T
    found = jnp.zeros((8, H), F32)
    for slot in range(8):
        at = lax.div(offsets[0, slot] - row0, H) * 4 + lax.div(offsets[1, slot] - col0, H)
        found += jnp.where((lane == at) & (live[0, 0] > slot), 1.0, 0.0)
    out[...] = found


def dot(a, b):
    return jnp.dot(a, b, preferred_element_type=F32)


def side_by_side(re, im):
    return jnp.concatenate([re.astype(BF16), im.astype(BF16)], 1)


def stacked(both):
    both = both.astype(BF16)
    return jnp.concatenate([both[:, :S], both[:, S:]], 0)


def start_block(offsets, slot):
    by = lax.div(offsets[0, slot] - lax.axis_index("row") * T, H)
    bx = lax.div(offsets[1, slot] - lax.axis_index("col") * T, H)
    return jnp.clip(by, 0, 3), jnp.clip(bx, 0, 3)


def visit_slots(canvas, probe, amps, offsets, live, right, left, terms, sums, halfway):
    sums[...] = jnp.zeros_like(sums)

    def some(step, carry):
        @pl.when(step == 1)
        def _():
            halfway()

        slots = [4 * step + k for k in range(4)]
        places = []
        for slot in slots:
            by, bx = start_block(offsets, slot)
            places.append((pl.ds(by * H + RING, S), pl.ds(bx * H + H, S)))

        def leaving(rows, cols):
            probe_re, probe_im = probe[0], probe[1]
            patch_re, patch_im = canvas[0, rows, cols], canvas[1, rows, cols]
            return side_by_side(
                probe_re * patch_re - probe_im * patch_im,
                probe_re * patch_im + probe_im * patch_re,
            )

        def corrected(slot, far):
            far_re, far_im = far[:S], far[S:]
            square = far_re * far_re + far_im * far_im
            factor = amps[slot].astype(F32) * lax.rsqrt(jnp.maximum(square, 1.0)) - 1.0
            return side_by_side(far_re * factor, far_im * factor)

        waves = [leaving(rows, cols) for rows, cols in places]
        waves = [stacked(dot(wave, right[...])) for wave in waves]
        waves = [dot(left[...], wave) for wave in waves]
        waves = [corrected(slot, wave) for slot, wave in zip(slots, waves)]
        waves = [stacked(dot(wave, left[...])) for wave in waves]
        waves = [dot(right[...], wave) for wave in waves]
        inner = pl.ds(H, S)
        grads = [0.0, 0.0]
        for slot, (rows, cols), diff in zip(slots, places, waves):
            mask = jnp.where(jnp.broadcast_to(live[0, 0], (1, S)) > slot, 1.0, 0.0)
            probe_re, probe_im = probe[0], probe[1]
            patch_re, patch_im = canvas[0, rows, cols], canvas[1, rows, cols]
            diff_re, diff_im = diff[:S] * mask, diff[S:] * mask
            terms[slot, 0, inner, inner] = probe_re * diff_re + probe_im * diff_im
            terms[slot, 1, inner, inner] = probe_re * diff_im - probe_im * diff_re
            grads[0] += patch_re * diff_re + patch_im * diff_im
            grads[1] += patch_re * diff_im - patch_im * diff_re
        for c in range(2):
            for ct in range(2):
                sums[ct, :, c] += grads[c][:, ct * H : (ct + 1) * H].reshape(32, 8, H)
        return carry

    lax.fori_loop(0, 2, some, 0)


def weigh(canvas, offsets, live, mass):
    quarter = S // 4
    places = [start_block(offsets, slot) for slot in range(8)]
    for k in range(4):
        total = 0.0
        for slot, (by, bx) in enumerate(places):
            rows, cols = pl.ds(by * H + RING + k * quarter, quarter), pl.ds(bx * H + H, S)
            patch_re, patch_im = canvas[0, rows, cols], canvas[1, rows, cols]
            mask = jnp.where(jnp.broadcast_to(live[0, 0], (1, S)) > slot, 1.0, 0.0)
            total = total + (patch_re * patch_re + patch_im * patch_im) * mask
        for ct in range(2):
            mass[ct, 8 * k : 8 * k + 8] = total[:, ct * H : (ct + 1) * H].reshape(8, 8, H)


def gather(offsets, terms, deposits, first, step, count):
    starts_at = [start_block(offsets, slot) for slot in range(8)]

    def one(block, carry):
        by, bx = first + lax.div(block, 5) * step, lax.rem(block, 5)
        total = [None, None]
        for slot in range(8):
            y = jnp.clip(by - starts_at[slot][0], -1, 2) * H + H
            x = jnp.clip(bx - starts_at[slot][1], -1, 2) * H + H
            for c in range(2):
                part = terms[slot, c, pl.ds(y, H), pl.ds(x, H)]
                total[c] = part if slot == 0 else total[c] + part
        for c in range(2):
            deposits[
                c, pl.ds(pl.multiple_of(by * H, H), H), pl.ds(pl.multiple_of(bx * H, H), H)
            ] = total[c]
        return carry

    lax.fori_loop(0, 5 * count, one, 0)


def frame_terms(terms):
    for slot in range(8):
        terms[slot, :, 0:H, :] = jnp.zeros((2, H, 2 * S), F32)
        terms[slot, :, S + H :, :] = jnp.zeros((2, H, 2 * S), F32)
        terms[slot, :, H : S + H, 0:H] = jnp.zeros((2, S, H), F32)
        terms[slot, :, H : S + H, S + H :] = jnp.zeros((2, S, H), F32)


def columns_as_rows(columns, out):
    lane = lax.broadcasted_iota(jnp.int32, (X, H), 1)
    gathered = jnp.zeros((X, H), F32)
    for k, column in enumerate(columns):
        gathered = jnp.where(lane == k, column, gathered)
    out[...] = gathered.T[:8]


class ProbeSum:
    def __init__(
        self, copies, sums, mass, probe, out, pair_in, part, y_in, y_part, rows_in, mass_in,
        mass_part, mass_y,
    ):
        self.row, col = lax.axis_index("row"), lax.axis_index("col")
        self.y, self.core = col // 2, lax.rem(col, 2)
        self.tile = lax.rem(self.row, 8)
        self.copies, self.sums, self.probe, self.out = copies, sums, probe, out
        self.pair_in, self.part, self.y_in, self.y_part = pair_in, part, y_in, y_part
        self.rows_in = rows_in
        self.mass, self.mass_in, self.mass_part, self.mass_y = mass, mass_in, mass_part, mass_y
        self.col = col
        self.other = (self.row, self.y * 2 + 1 - self.core)
        self.y_peers = [
            (self.row, lax.rem(self.y + k, 4) * 2 + self.core) for k in range(1, 4)
        ]
        self.row_peers = [(lax.rem(self.row + k, 16), col) for k in range(1, 16)]

    def peers(self):
        return self.y_peers + self.row_peers

    def start_mass(self):
        self.mass_pair = self.copies.start(self.mass.at[1 - self.core], self.mass_in, self.other)
        self.mass_sent = []
        for k in range(1, 4):
            at = lax.rem(self.y + k, 4) * 8
            self.mass_sent.append(
                self.copies.make(
                    self.mass_part.at[pl.ds(at, 8)], self.mass_y.at[k - 1], self.y_peers[k - 1]
                )
            )

    def start_mass_y(self):
        self.mass_pair.wait_recv()
        self.mass_part[...] = self.mass[self.core] + self.mass_in[...]
        for copy in self.mass_sent:
            copy.start()

    def start_pair(self):
        self.pair = self.copies.start(self.sums.at[1 - self.core], self.pair_in, self.other)

    def start_y(self):
        self.pair.wait_recv()
        self.part[...] = self.sums[self.core] + self.pair_in[...]
        self.y_sent = []
        for k in range(1, 4):
            at = lax.rem(self.y + k, 4) * 8
            self.y_sent.append(
                self.copies.start(
                    self.part.at[pl.ds(at, 8)], self.y_in.at[k - 1], self.y_peers[k - 1]
                )
            )

    def start_rows(self):
        self.copies.started += self.mass_sent
        for copy in self.y_sent + self.mass_sent:
            copy.wait_recv()
        mine = pl.ds(self.y * 8, 8)
        self.y_part[:, 0:2] = self.part[mine] + self.y_in[0] + self.y_in[1] + self.y_in[2]
        self.y_part[:, 2] = (
            self.mass_part[mine] + self.mass_y[0] + self.mass_y[1] + self.mass_y[2]
        )
        self.rows_in[self.row] = self.y_part[self.tile]
        for k in range(1, 16):
            tile = lax.rem(self.row + k, 8)
            self.copies.start(
                self.y_part.at[tile], self.rows_in.at[self.row], self.row_peers[k - 1]
            )
        self.first = self.copies.count - 15

    def landed(self, ref, number):
        pltpu.make_async_remote_copy(
            src_ref=ref,
            dst_ref=ref,
            send_sem=self.copies.send_sems.at[number],
            recv_sem=self.copies.recv_sems.at[number],
            device_id=self.other,
            device_id_type=MESH,
        ).wait_recv()

    def start_back(self):
        for k in range(1, 16):
            self.landed(self.rows_in.at[lax.rem(self.row + 16 - k, 16)], self.first + k - 1)
        total = self.rows_in[0]
        for k in range(1, 16):
            total = total + self.rows_in[k]
        rt = self.y * 8 + self.tile
        rows, cols = pl.ds(pl.multiple_of(rt * 8, 8), 8), pl.ds(pl.multiple_of(self.core * H, H), H)
        inverse = 1.0 / (total[2] + 1.0)
        for c in range(2):
            self.out[self.core, rt, c] = self.probe[c, rows, cols] + total[c] * inverse
        mine = self.out.at[self.core, rt]
        group = self.row // 8 * 8
        self.first = self.copies.count
        for k in range(1, 8):
            self.copies.start(mine, mine, (group + lax.rem(self.tile + k, 8), self.col))

    def start_back_y(self):
        for k in range(1, 8):
            tile = lax.rem(self.tile + 8 - k, 8)
            self.landed(self.out.at[self.core, self.y * 8 + tile], self.first + k - 1)
        mine = self.out.at[self.core, pl.ds(self.y * 8, 8)]
        self.first = self.copies.count
        for k in range(1, 4):
            self.copies.start(mine, mine, self.y_peers[k - 1])
        self.pair_first = self.copies.count
        self.copies.start(mine, mine, self.other)

    def start_back_pair(self):
        for k in range(1, 4):
            at = lax.rem(self.y + 4 - k, 4) * 8
            theirs = self.out.at[self.core, pl.ds(at, 8)]
            self.landed(theirs, self.first + k - 1)
            self.copies.start(theirs, theirs, self.other)

    def end(self):
        for k in range(4):
            at = lax.rem(self.y + 4 - k, 4) * 8
            self.landed(self.out.at[1 - self.core, pl.ds(at, 8)], self.pair_first + k)


PROBE_COPIES = 4 + 1 + 3 + 15 + 7 + 3 + 4


def start_table(starts):
    def count(by, bx):
        return starts[by // 4 + 1, bx // 4 + 1, 0, by % 4 * 4 + bx % 4]

    return count


def block_weight(count, square, by, bx, rows):
    first, size = rows
    total = 1.0
    for qy in range(2):
        for qx in range(2):
            total = total + count(by - qy, bx - qx) * square[
                pl.ds(qy * H + first, size), pl.ds(qx * H, H)
            ]
    return total


def spread_lines(rows):
    length = rows[0].shape[1]
    packed = jnp.concatenate(rows + [jnp.zeros((H - len(rows), length), F32)], 0)
    return packed.T


def shifted_sum(canvas, c, first, rows, cols):
    width = cols + 2 * H
    whole = canvas[c, pl.ds(first, rows), pl.ds(0, width)]
    left = pltpu.roll(whole, 1, 1)[:, H : H + cols]
    right = pltpu.roll(whole, width - 1, 1)[:, H : H + cols]
    above = canvas[c, pl.ds(first - 1, rows), pl.ds(H, cols)]
    below = canvas[c, pl.ds(first + 1, rows), pl.ds(H, cols)]
    return below + above + right + left, whole[:, H : H + cols]


def rates(classes, weights):
    value = jnp.full(classes.shape, weights[0], F32)
    for k in range(1, 4):
        value = jnp.where(classes == k, weights[k], value)
    return value


def blank_sides(canvas, cols_end, first, size):
    col = lax.axis_index("col")
    width = canvas.shape[2]

    @pl.when(col == 0)
    def _():
        canvas[:, pl.ds(first, size), 0:H] = jnp.zeros((2, size, H), F32)

    @pl.when(col == 7)
    def _():
        canvas[:, pl.ds(first, size), cols_end:] = jnp.zeros((2, size, width - cols_end), F32)


def blank_outside(canvas, rows_end, cols_end):
    row = lax.axis_index("row")
    _, height, width = canvas.shape

    @pl.when(row == 0)
    def _():
        canvas[:, 0:RING, :] = jnp.zeros((2, RING, width), F32)

    @pl.when(row == 15)
    def _():
        canvas[:, rows_end:, :] = jnp.zeros((2, height - rows_end, width), F32)

    blank_sides(canvas, cols_end, 0, height)


MIDDLE = pl.ds(H, T - H)
LINES = [(0, 0), (0, 1), (1, 2), (1, 3), (0, 4), (0, 5), (1, 6), (1, 7)]


def unpack_probe(tiles, out):
    for c in range(2):
        for ct in range(2):
            out[c, :, ct * H : (ct + 1) * H] = tiles[ct, :, c].reshape(S, H)


def middle_phase(
    copies, probe_sum, offsets, terms, grads, lines, rate, inverse, probe, starts,
    canvas, canvas_next, probe_next, square, corners, tiles,
    from_left, from_right, from_up, from_down, lines_lr, lines_up, lines_down, ahead,
):
    up, down, left, right = around()
    probe_sum.start_pair()
    gather(offsets, terms, grads, 0, 4, 2)
    later = []
    center = []

    probe_sum.start_y()
    center += [
        copies.start(
            grads.at[:, pl.ds(T, H), MIDDLE], from_up.at[:, pl.ds(RING, H), MIDDLE], down
        ),
        copies.start(grads.at[:, pl.ds(0, H), MIDDLE], from_down.at[:, pl.ds(0, H), MIDDLE], up),
    ]
    gather(offsets, terms, grads, 1, 1, 3)
    inside = pl.ds(RING, X)
    columns_as_rows(
        [grads[c, :, T - 1 : T] for c in range(2)]
        + [grads[c, :, H : H + 1] for c in range(2)]
        + [canvas[c, inside, H + T - 1 : H + T] for c in range(2)]
        + [canvas[c, inside, H + H : H + H + 1] for c in range(2)],
        lines,
    )
    center += [
        copies.start(
            grads.at[:, pl.ds(T - RING, RING), MIDDLE], from_up.at[:, pl.ds(0, RING), MIDDLE], down
        ),
        copies.start(
            grads.at[:, pl.ds(H, RING), MIDDLE], from_down.at[:, pl.ds(H, RING), MIDDLE], up
        ),
    ]
    later += [
        copies.start(lines, lines_up.at[2], down),
        copies.start(lines, lines_down.at[2], up),
    ]
    side = [
        copies.start(lines, lines_lr.at[0], right),
        copies.start(lines, lines_lr.at[1], left),
    ]
    for at in (pl.ds(0, STRIP), pl.ds(X - STRIP, STRIP)):
        side.append(
            copies.start(grads.at[:, at, pl.ds(T, H)], from_left.at[:, at, :], right)
        )
        side.append(
            copies.start(grads.at[:, at, pl.ds(0, H)], from_right.at[:, at, :], left)
        )
    inner = pl.ds(STRIP, X - 2 * STRIP)
    side_inner = [
        copies.start(grads.at[:, inner, pl.ds(T, H)], from_left.at[:, inner, :], right),
        copies.start(grads.at[:, inner, pl.ds(0, H)], from_right.at[:, inner, :], left),
    ]
    probe_sum.start_rows()
    count = start_table(starts)
    square[...] = probe[0] * probe[0] + probe[1] * probe[1]

    def rows_of(by):
        if by in (-1, 5):
            return (0, RING, H - RING) if by == -1 else (RING + X, RING, 0)
        return RING + by * H, H, 0

    def prepare(by, bx):
        at, size, first = rows_of(by)
        inverse[pl.ds(at, size), pl.ds(H + bx * H, H)] = 1.0 / block_weight(
            count, square, by, bx, (first, size)
        )

    def update(by, bx, ring=None):
        at, size, _ = rows_of(by)
        edge = bx in (-1, 5)
        cols = pl.ds(H + bx * H, H)
        scale = inverse[pl.ds(at, size), cols]
        for c in range(2):
            if edge:
                k = 0 if bx == -1 else 2
                grad = jnp.broadcast_to(ring[:, k + c : k + c + 1], (H, H))
                base = jnp.broadcast_to(ring[:, k + 4 + c : k + 5 + c], (H, H))
            else:
                base = canvas[c, pl.ds(at, size), cols]
                block = pl.ds(bx * H, H)
                if by == -1:
                    grad = from_up[c, 0:RING, block]
                elif by == 5:
                    grad = from_down[c, H:STRIP, block]
                else:
                    grad = grads[c, pl.ds(by * H, H), block]
                    if by == 0:
                        grad = grad + from_up[c, RING:STRIP, block]
                    if by == 4:
                        grad = grad + from_down[c, 0:H, block]
                    if bx == 0:
                        grad = grad + from_left[c, pl.ds(by * H, H), :]
                    if bx == 4:
                        grad = grad + from_right[c, pl.ds(by * H, H), :]
            canvas[c, pl.ds(at, size), cols] = base + grad * scale

    def smooth(first, size):
        for c in range(2):
            around_sum, center_now = shifted_sum(canvas, c, RING + first, size, X)
            canvas_next[c, pl.ds(RING + first, size), pl.ds(H, X)] = center_now + rate[
                pl.ds(first, size), :
            ] * (around_sum - 4.0 * center_now)

    for by in (1, 2, 3):
        for bx in (1, 2, 3):
            prepare(by, bx)
            update(by, bx)
    for by in range(-1, 6):
        for bx in range(-1, 6):
            if not (by in (1, 2, 3) and bx in (1, 2, 3) or by in (-1, 5) and bx in (-1, 5)):
                prepare(by, bx)
    probe_sum.start_back()
    for copy in side:
        copy.wait_recv()
    for k, (first, source) in enumerate(
        ((0, from_left), (0, from_right), (X - STRIP, from_left), (X - STRIP, from_right))
    ):
        column = 0 if k % 2 == 0 else T
        corners[k] = (
            grads[:, pl.ds(first, STRIP), pl.ds(column, H)]
            + source[:, pl.ds(first, STRIP), :]
        )
    later += [
        copies.start(lines_lr, lines_up.at[pl.ds(0, 2)], down),
        copies.start(lines_lr, lines_down.at[pl.ds(0, 2)], up),
        copies.start(corners.at[0], from_down.at[:, :, pl.ds(0, H)], up),
        copies.start(corners.at[2], from_up.at[:, :, pl.ds(0, H)], down),
        copies.start(corners.at[1], from_down.at[:, :, pl.ds(T, H)], up),
        copies.start(corners.at[3], from_up.at[:, :, pl.ds(T, H)], down),
    ]
    for copy in side_inner:
        copy.wait_recv()
    for by in (1, 2, 3):
        update(by, 0)
        update(by, 4)
    probe_sum.start_back_y()
    for copy in center:
        copy.wait_recv()
    for by in (-1, 0, 4, 5):
        for bx in (1, 2, 3):
            update(by, bx)
    rows = [lines_lr[side_at, k : k + 1] for side_at, k in LINES]
    ring = spread_lines(rows)
    for by in (1, 2, 3):
        for bx in (-1, 5):
            update(by, bx, ring[by * H : (by + 1) * H])
    blank_sides(canvas, H + T, RING + H, 3 * H)
    for first, size in ((STRIP, H - RING), (2 * H, H), (3 * H, H - RING)):
        smooth(first, size)
    probe_sum.start_back_pair()
    for copy in later:
        copy.wait_recv()
    far = []
    for n, (side_at, k) in enumerate(LINES):
        above = lines_up[side_at, k : k + 1, T:]
        below_it = lines_down[side_at, k : k + 1, :H]
        if n < 4:
            pieces = [rows[n][:, :H] + above, rows[n][:, T:] + below_it]
        else:
            pieces = [rows[n][:, :H], below_it]
        far.append(jnp.concatenate(pieces, 1))
    ring = spread_lines(far)
    for by in (0, 4):
        for bx in (0, 4):
            update(by, bx)
        for bx in (-1, 5):
            update(by, bx, ring[:H] if by == 0 else ring[H:])
    for by in (-1, 5):
        for bx in (0, 4):
            update(by, bx)
    blank_outside(canvas, RING + T, H + T)
    for first in (0, X - STRIP):
        smooth(first, STRIP)
    ahead()
    probe_sum.end()
    unpack_probe(tiles, probe_next)
    copies.finish()


def last_phase(
    copies, probe_sum, offsets, terms, grads, lines, rate, inverse, probe, starts,
    canvas, ring_out, ring_up, obj_now, obj_out, out_sems, probe_out, square, corner_down, corner_up, tiles,
    from_left, from_up, from_down, lines_lr, lines_up,
):
    up, down, left, right = around()
    probe_sum.start_pair()
    ring_out[...] = canvas[:, pl.ds(T, RING), pl.ds(H, T)]
    gather(offsets, terms, grads, 0, 4, 2)
    later = []
    center = [
        copies.start(ring_out, ring_up, down),
        copies.start(grads.at[:, pl.ds(0, RING), MIDDLE], from_down.at[:, :, MIDDLE], up),
    ]

    probe_sum.start_y()
    center.append(
        copies.start(grads.at[:, pl.ds(T, H), MIDDLE], from_up.at[:, pl.ds(RING, H), MIDDLE], down)
    )
    gather(offsets, terms, grads, 1, 1, 3)
    inside = pl.ds(RING, X)
    columns_as_rows(
        [grads[c, :, T - 1 : T] for c in range(2)]
        + [grads[c, :, 0:1] for c in range(2)]
        + [grads[c, :, T : T + 1] for c in range(2)]
        + [canvas[c, inside, H + T - 1 : H + T] for c in range(2)],
        lines,
    )
    center.append(
        copies.start(
            grads.at[:, pl.ds(T - RING, RING), MIDDLE], from_up.at[:, pl.ds(0, RING), MIDDLE], down
        )
    )
    later.append(copies.start(lines, lines_up.at[2], down))
    line_copies = [
        copies.start(lines, lines_lr.at[0], right),
        copies.start(lines, lines_lr.at[1], left),
    ]
    side = [
        copies.start(grads.at[:, at, pl.ds(T, H)], from_left.at[:, at, :], right)
        for at in (pl.ds(0, RING), pl.ds(X - STRIP, STRIP), pl.ds(RING, X - STRIP - RING))
    ]
    probe_sum.start_rows()
    count = start_table(starts)
    square[...] = probe[0] * probe[0] + probe[1] * probe[1]

    def rows_of(by):
        if by in (-1, 4):
            return (0, RING, H - RING) if by == -1 else (RING + T, RING, 0)
        return RING + by * H, H, 0

    def prepare(by, bx):
        at, size, first = rows_of(by)
        inverse[pl.ds(at, size), pl.ds(H + bx * H, H)] = 1.0 / block_weight(
            count, square, by, bx, (first, size)
        )

    def update(by, bx, ring=None):
        at, size, _ = rows_of(by)
        cols = pl.ds(H + bx * H, H)
        scale = inverse[pl.ds(at, size), cols]
        block = pl.ds(max(bx, 0) * H, H)
        for c in range(2):
            base = canvas[c, pl.ds(at, size), cols]
            if bx == -1:
                grad = jnp.broadcast_to(ring[:, c : c + 1], (H, H))
                base = jnp.broadcast_to(ring[:, 4 + c : 5 + c], (H, H))
            elif bx == 4:
                grad = jnp.broadcast_to(ring[:, 2 + c : 3 + c], (H, H))
                grad = grad + grads[c, pl.ds(by * H, H), block]
            elif by == -1:
                base = ring_up[c, :, block]
                grad = from_up[c, 0:RING, block]
            else:
                grad = grads[c, pl.ds(by * H, size), block]
                if by == 0:
                    grad = grad + from_up[c, RING:STRIP, block]
                if by == 4:
                    grad = grad + from_down[c, :, block]
                if bx == 0:
                    grad = grad + from_left[c, pl.ds(by * H, size), :]
            canvas[c, pl.ds(at, size), cols] = base + grad * scale

    leaving = []

    def smooth(first, size):
        rows = pl.ds(first, size)
        for c in range(2):
            around_sum, center_now = shifted_sum(canvas, c, RING + first, size, T)
            obj_now[c, rows, :] = center_now + rate[rows, 0:T] * (around_sum - 4.0 * center_now)
        copy = pltpu.make_async_copy(
            obj_now.at[:, rows, :], obj_out.at[:, rows, :], out_sems.at[len(leaving)]
        )
        copy.start()
        leaving.append(copy)

    for by in (1, 2, 3):
        for bx in (1, 2, 3):
            prepare(by, bx)
            update(by, bx)
    for by in range(-1, 5):
        for bx in range(-1, 5):
            if not (by in (1, 2, 3) and bx in (1, 2, 3) or by in (-1, 4) and bx in (-1, 4)):
                prepare(by, bx)
    probe_sum.start_back()
    for copy in side[:2]:
        copy.wait_recv()
    for copy in line_copies:
        copy.wait_recv()
    corner_down[...] = (
        grads[:, pl.ds(X - STRIP, STRIP), pl.ds(0, H)] + from_left[:, pl.ds(X - STRIP, STRIP), :]
    )
    corner_up[...] = grads[:, pl.ds(0, RING), pl.ds(0, H)] + from_left[:, pl.ds(0, RING), :]
    later += [
        copies.start(lines_lr, lines_up.at[pl.ds(0, 2)], down),
        copies.start(corner_down, from_up.at[:, :, pl.ds(0, H)], down),
        copies.start(corner_up, from_down.at[:, :, pl.ds(0, H)], up),
    ]
    side[2].wait_recv()
    for by in (1, 2, 3):
        update(by, 0)
    probe_sum.start_back_y()
    for copy in center:
        copy.wait_recv()
    for by in (-1, 0, 4):
        for bx in (1, 2, 3):
            update(by, bx)
    rows = [lines_lr[0, c : c + 1] for c in range(2)]
    rows += [lines_lr[1, 2 + c : 3 + c] for c in range(2)]
    rows += [lines_lr[0, 6 + c : 7 + c] for c in range(2)]
    ring = spread_lines(rows)
    for by in (1, 2, 3):
        for bx in (-1, 4):
            update(by, bx, ring[by * H : (by + 1) * H])
    blank_sides(canvas, H + T, RING + H, 3 * H)
    for first, size in ((STRIP, H - RING), (2 * H, H), (3 * H, H - RING)):
        smooth(first, size)
    probe_sum.start_back_pair()
    for copy in later:
        copy.wait_recv()
    far = [rows[c][:, :H] + lines_up[0, c : c + 1, T:] for c in range(2)]
    far += [
        rows[2 + c][:, :H] + lines_up[1, 2 + c : 3 + c, T:] + lines_up[2, 4 + c : 5 + c, T:]
        for c in range(2)
    ]
    far += [rows[4 + c][:, :H] for c in range(2)]
    ring = spread_lines(far)
    update(0, 0)
    for bx in (-1, 4):
        update(0, bx, ring)
    for by in (-1, 4):
        update(by, 0)
    blank_outside(canvas, RING + T, H + T)
    smooth(0, STRIP)
    smooth(T - RING, RING)
    probe_sum.end()
    unpack_probe(tiles, probe_out)
    for copy in leaving:
        copy.wait()
    copies.finish()


def whole_kernel(
    obj, probe_in, amps_in, offsets, live, classes_in, weights, right_table, left_table,
    obj_out, probe_out,
    canvas, canvas_next, terms, grads, sums, probe, probe_next, amps, classes, class_down,
    class_right, rate, inverse, obj_now, square, counted, starts_in, starts, lines, ring_out, ring_up, corners, corner_down,
    corner_up, tiles, tiles_last, part, y_part, mass, mass_part, *refs
):
    landing, landing_last, (sems, out_sems, send_sems, recv_sems) = refs[:12], refs[12:22], refs[22:]
    up, down, left, right = around()
    row, col = lax.axis_index("row"), lax.axis_index("col")
    copies = Copies(send_sems, recv_sems)
    probe_sum = ProbeSum(
        copies, sums, mass, probe, tiles, landing[7], part, landing[8], y_part, landing[9],
        landing[10], mass_part, landing[11],
    )
    probe_sum_last = ProbeSum(
        copies, sums, mass, probe_next, tiles_last, landing_last[5], part, landing_last[6],
        y_part, landing_last[7], landing_last[8], mass_part, landing_last[9],
    )
    near = {
        (dr, dc): (lax.rem(row + dr + 16, 16), lax.rem(col + dc + 8, 8))
        for dr in (-1, 0, 1)
        for dc in (-1, 0, 1)
        if (dr, dc) != (0, 0)
    }
    pairs = [
        (obj, canvas.at[:, pl.ds(RING, T), pl.ds(H, T)]),
        (probe_in, probe),
        (amps_in, amps),
        (classes_in, classes),
    ]
    own = [pltpu.make_async_copy(src, dst, sems.at[k]) for k, (src, dst) in enumerate(pairs)]
    greet([device for (dr, dc), device in near.items() if dc != 0] + probe_sum.peers())
    rows = copies.start(
        obj.at[:, pl.ds(0, STRIP), :], canvas.at[:, pl.ds(RING + T, STRIP), pl.ds(H, T)], up
    )
    beside = copies.start(
        obj.at[:, :, pl.ds(0, H)], canvas.at[:, pl.ds(RING, T), pl.ds(H + T, H)], left
    )
    class_beside = copies.start(classes_in.at[:, pl.ds(0, H)], class_right, left)
    strips = [
        rows,
        copies.start(
            obj.at[:, pl.ds(T - RING, RING), :], canvas.at[:, pl.ds(0, RING), pl.ds(H, T)], down
        ),
    ]
    for copy in own:
        copy.start()
    count_starts(offsets, live, counted)
    small = [
        copies.start(counted, starts_in.at[1 - dr, 1 - dc], device)
        for (dr, dc), device in near.items()
    ]
    starts_in[1, 1] = counted[...]
    frame_terms(terms)
    own[3].wait()
    rate[0:T, 0:T] = rates(classes[...], weights)
    beside.wait_recv()
    corner = [
        copies.start(
            canvas.at[:, pl.ds(RING, STRIP), pl.ds(H + T, H)],
            canvas.at[:, pl.ds(RING + T, STRIP), pl.ds(H + T, H)],
            up,
        ),
        copies.start(
            canvas.at[:, pl.ds(T, RING), pl.ds(H + T, H)],
            canvas.at[:, pl.ds(0, RING), pl.ds(H + T, H)],
            down,
        ),
    ]
    class_beside.wait_recv()
    class_later = [
        copies.start(classes_in.at[pl.ds(0, H), :], class_down.at[:, pl.ds(0, T)], up),
        copies.start(class_right.at[pl.ds(0, H), :], class_down.at[:, pl.ds(T, H)], up),
    ]
    for copy in own[:3]:
        copy.wait()
    for copy in small:
        copy.wait_recv()
    to_scalars = pltpu.make_async_copy(starts_in, starts, sems.at[4])
    to_scalars.start()
    for copy in strips + corner:
        copy.wait_recv()
    to_scalars.wait()
    weigh(canvas, offsets, live, mass)
    probe_sum.start_mass()
    visit_slots(
        canvas, probe, amps, offsets, live, right_table, left_table, terms, sums,
        probe_sum.start_mass_y,
    )
    for copy in class_later:
        copy.wait_recv()
    rate[0:T, T:X] = rates(class_right[...], weights)
    rate[T:X, :] = rates(class_down[...], weights)
    copies.finish()

    def ahead():
        weigh(canvas_next, offsets, live, mass)
        probe_sum_last.start_mass()

    middle_phase(
        copies, probe_sum, offsets, terms, grads, lines, rate, inverse, probe, starts, canvas, canvas_next, probe_next, square, corners, tiles, *landing[:7], ahead,
    )
    visit_slots(
        canvas_next, probe_next, amps, offsets, live, right_table, left_table, terms, sums,
        probe_sum_last.start_mass_y,
    )
    last_phase(
        copies, probe_sum_last, offsets, terms, grads, lines, rate, inverse, probe_next, starts,
        canvas_next, ring_out, ring_up, obj_now, obj_out, out_sems, probe_out, square, corner_down, corner_up, tiles_last,
        *landing_last[:5],
    )
    assert copies.count == send_sems.shape[0]


PROBE_LANDING = [
    pltpu.VMEM((32, 2, 8, H), F32),
    pltpu.VMEM((3, 8, 2, 8, H), F32),
    pltpu.VMEM((16, 3, 8, H), F32),
    pltpu.VMEM((32, 8, H), F32),
    pltpu.VMEM((3, 8, 8, H), F32),
]
COPIES = 16 + 2 * PROBE_COPIES + 20 + 13


def whole(obj, probe, amps, offsets, live, classes, weights, right, left):
    wide = (2, X + 2 * RING, X + 2 * H)
    scratch = [
        pltpu.VMEM(wide, F32),
        pltpu.VMEM(wide, F32),
        pltpu.VMEM((8, 2, 2 * S, 2 * S), F32),
        pltpu.VMEM((2, X, X), F32),
        pltpu.VMEM((2, 32, 2, 8, H), F32),
        pltpu.VMEM((2, S, S), F32),
        pltpu.VMEM((2, S, S), F32),
        pltpu.VMEM((8, S, S), BF16),
        pltpu.VMEM((T, T), jnp.int32),
        pltpu.VMEM((H, X), jnp.int32),
        pltpu.VMEM((T, H), jnp.int32),
        pltpu.VMEM((X, X), F32),
        pltpu.VMEM(wide[1:], F32),
        pltpu.VMEM((2, T, T), F32),
        pltpu.VMEM((S, S), F32),
        pltpu.VMEM((8, H), F32),
        pltpu.VMEM((3, 3, 8, H), F32),
        pltpu.SMEM((3, 3, 8, H), F32),
        pltpu.VMEM((8, X), F32),
        pltpu.VMEM((2, RING, T), F32),
        pltpu.VMEM((2, RING, T), F32),
        pltpu.VMEM((4, 2, STRIP, H), F32),
        pltpu.VMEM((2, STRIP, H), F32),
        pltpu.VMEM((2, RING, H), F32),
        pltpu.VMEM((2, 32, 2, 8, H), F32),
        pltpu.VMEM((2, 32, 2, 8, H), F32),
        pltpu.VMEM((32, 2, 8, H), F32),
        pltpu.VMEM((8, 3, 8, H), F32),
        pltpu.VMEM((2, 32, 8, H), F32),
        pltpu.VMEM((32, 8, H), F32),
    ]
    landing = [
        pltpu.VMEM((2, X, H), F32),
        pltpu.VMEM((2, X, H), F32),
        pltpu.VMEM((2, STRIP, X), F32),
        pltpu.VMEM((2, STRIP, X), F32),
        pltpu.VMEM((2, 8, X), F32),
        pltpu.VMEM((3, 8, X), F32),
        pltpu.VMEM((3, 8, X), F32),
    ] + PROBE_LANDING
    landing_last = [
        pltpu.VMEM((2, X, H), F32),
        pltpu.VMEM((2, STRIP, T), F32),
        pltpu.VMEM((2, RING, T), F32),
        pltpu.VMEM((2, 8, X), F32),
        pltpu.VMEM((3, 8, X), F32),
    ] + PROBE_LANDING
    return pl.pallas_call(
        whole_kernel,
        name="reconstruct",
        out_shape=[
            jax.ShapeDtypeStruct((2, T, T), F32),
            jax.ShapeDtypeStruct((2, S, S), F32),
        ],
        in_specs=[ANY, ANY, ANY, SMEM, SMEM, ANY, SMEM, VMEM, VMEM],
        out_specs=[ANY, VMEM],
        scratch_shapes=scratch
        + landing
        + landing_last
        + [
            pltpu.SemaphoreType.DMA((5,)),
            pltpu.SemaphoreType.DMA((5,)),
            pltpu.SemaphoreType.DMA((COPIES,)),
            pltpu.SemaphoreType.DMA((COPIES,)),
        ],
        compiler_params=pltpu.CompilerParams(
            collective_id=0, has_side_effects=True, vmem_limit_bytes=VMEM_BYTES
        ),
    )(obj, probe, amps, offsets, live, classes, weights, right, left)


def hand_over_kernel(obj, probe, obj_out, probe_out, held, held_probe, in_sems, out_sems):
    pairs = [(probe, held_probe, probe_out)]
    for c in range(2):
        for first in range(0, T, H):
            rows = pl.ds(first, H)
            pairs.append((obj.at[c, rows, :], held.at[c, rows, :], obj_out.at[c, rows, :]))
    arriving = [
        pltpu.make_async_copy(src, mid, in_sems.at[k]) for k, (src, mid, _) in enumerate(pairs)
    ]
    leaving = [
        pltpu.make_async_copy(mid, dst, out_sems.at[k]) for k, (_, mid, dst) in enumerate(pairs)
    ]
    for copy in arriving:
        copy.start()
    for first, second in zip(arriving, leaving):
        first.wait()
        second.start()
    for copy in leaving:
        copy.wait()


def hand_over(obj, probe):
    return pl.pallas_call(
        hand_over_kernel,
        name="hand_over",
        out_shape=[
            jax.ShapeDtypeStruct((2, T, T), F32),
            jax.ShapeDtypeStruct((2, S, S), F32),
        ],
        in_specs=[ANY, ANY],
        out_specs=[ANY, ANY],
        scratch_shapes=[
            pltpu.VMEM((2, T, T), F32),
            pltpu.VMEM((2, S, S), F32),
            pltpu.SemaphoreType.DMA((9,)),
            pltpu.SemaphoreType.DMA((9,)),
        ],
        compiler_params=pltpu.CompilerParams(vmem_limit_bytes=VMEM_BYTES),
    )(obj, probe)


def per_device(
    object_init, probe_init, amplitudes, scan_offsets, live_count, smooth_class, class_weight
):
    right, left = (jnp.asarray(table) for table in dft_blocks())
    return tuple(
        hand_over(
            *whole(
                object_init,
                probe_init,
                amplitudes.reshape(8, S, S),
                scan_offsets.reshape(8, 2).T,
                live_count,
                smooth_class,
                class_weight,
                right,
                left,
            )
        )
    )


def solution(mesh):
    in_specs = (
        P(None, "row", "col"),
        P(),
        P("row", "col", None, None, None),
        P("row", "col", None, None),
        P("row", "col"),
        P("row", "col"),
        P(),
    )
    out_specs = (P(None, "row", "col"), P())
    return jax.shard_map(
        per_device, mesh=mesh, in_specs=in_specs, out_specs=out_specs, check_vma=False
    )
```
